32 devices in a mesh: rep: 2 (over x), shard: 16 (over z, y, core).
Axes of the slice: x: 2, y: 2, z: 4, core: 2. Of those that a mesh axis runs over, the one named last changes fastest.
Arguments:
- hidden_in: bfloat16 [8192, 768], P(('rep', 'shard')), may hold values from -6 to 6
- gate_in: float32 [8192, 8], P(('rep', 'shard')), may hold values from -4 to 4
- routes: int32 [2, 8192, 2], P(None, ('rep', 'shard')), may hold values from 0 to 7, all different within a row
- priority: int32 [2, 32, 512], P(None, ('rep', 'shard')), may hold values from 0 to 511, each once within a row
- segments: int32 [32, 256], P(('rep', 'shard')), may hold values from 0 to 3, never falling along the last dimension, each value on 1 to 128 neighbouring positions
- norm_attn: bfloat16 [2, 768], P(None, 'shard'), may hold values from 0.25 to 1.75
- w_qkv: bfloat16 [2, 768, 2304], P(None, 'shard'), may hold values from -0.21875 to 0.21875
- w_out: bfloat16 [2, 768, 768], P(None, 'shard'), may hold values from -0.875 to 0.875
- norm_moe: bfloat16 [2, 768], P(None, 'shard'), may hold values from 0.25 to 1.75
- w_router: bfloat16 [2, 768, 8], P(None, 'shard'), may hold values from -0.109375 to 0.109375
- w_const: bfloat16 [2, 768, 4], P(None, 'shard'), may hold values from -0.21875 to 0.21875
- const_vec: bfloat16 [2, 2, 768], P(None, None, 'shard'), may hold values from -5 to 5
- w_gate_up: bfloat16 [2, 4, 768, 4096], P(None, None, 'shard'), may hold values from -0.21875 to 0.21875
- w_down: bfloat16 [2, 4, 2048, 768], P(None, None, 'shard'), may hold values from -0.25 to 0.25
- grad_out: float32 [8192, 768], P(('rep', 'shard')), may hold values from -6 to 6
Outputs:
- hidden_out: bfloat16 [8192, 768], P(('rep', 'shard'))
- grad_hidden: float32 [8192, 768], P(('rep', 'shard'))
- grad_gate: float32 [8192, 8], P(('rep', 'shard'))
- grad_norm_attn: float32 [2, 768], P(None, 'shard')
- grad_qkv: float32 [2, 768, 2304], P(None, 'shard')
- grad_out_proj: float32 [2, 768, 768], P(None, 'shard')
- grad_norm_moe: float32 [2, 768], P(None, 'shard')
- grad_router: float32 [2, 768, 8], P(None, 'shard')
- grad_const_mix: float32 [2, 768, 4], P(None, 'shard')
- grad_const_vec: float32 [2, 2, 768], P(None, None, 'shard')
- grad_gate_up: float32 [2, 4, 768, 4096], P(None, None, 'shard')
- grad_down: float32 [2, 4, 2048, 768], P(None, None, 'shard')
The draws below stay inside these ranges and needn't reach their ends.
Inputs may be any that keep to these rules, and one draw needn't show every extreme that they name: Each token's 2 routes name different experts; experts below 4 have feed-forward weights, 4 is the zero expert, 5 the copy expert, the rest constant experts. `priority`: for each layer and device the 512 ranks are a permutation; rank of pair t * 2 + k belongs to the device's token t and its k-th route. `segments`: document numbers never fall along a device's row; each document has 1 to 128 tokens and one has exactly that many.
All inputs are finite; a program needn't handle non-finite values.
Results may differ from the reference program's by a relative error of at most 0.02.
Values may be sent and summed in bfloat16 or wider, within the bound.
No kernel may reach another device: no remote copies, remote signals or barrier semaphores. Data moves between devices by JAX's collectives and lax.ppermute only.
A program may use at most 448 MiB of HBM per device.

```python
import math
import jax
import jax.numpy as jnp
import numpy as np
from jax import lax

D = 768
HEAD_DIM = 64
FF = 2048
EF = 4
NCONST = 2
TOP = 2
LAYERS = 2
DOCS = 4
TOK_DEV = 256
EXPERTS = 8
CAP = 80
TOKENS = 8192
DEVICES = 32


def levels(rng, shape, cuts, least, top_value):
    loudness, own = 1.0, jax.random.fold_in(rng, 6)
    for dim, blocks in cuts:
        draws = jnp.exp(jax.random.uniform(jax.random.fold_in(own, dim), (blocks,), jnp.float32, least / len(cuts), top_value / len(cuts)))
        loudness = loudness * jnp.repeat(draws, shape[dim] // blocks).reshape([-1 if axis == dim else 1 for axis in range(len(shape))])
    return loudness


def choose_distinct(stream_key, rows, amount, top, lift):
    order = jax.random.permutation(jax.random.fold_in(stream_key, 1), amount)
    boost = order
    for power in range(3):
        boost = boost * boost // amount
    boost = boost * lift // amount
    chance = jax.random.randint(jax.random.fold_in(stream_key, 2), (rows, amount), 0, 4096) + boost
    holders = jax.random.permutation(jax.random.fold_in(stream_key, 3), rows)[jnp.arange(amount) % rows]
    chance = jnp.where(jnp.arange(rows)[:, None] == holders[None, :], 1 << 14, chance)
    score = chance * amount + jnp.arange(amount)
    return lax.top_k(score.astype(jnp.int32), top)[1].astype(jnp.int32)


def length_profile(count, total, bound, lean):
    portions = [(1 << 20) // math.isqrt(grade ** lean) + 1 for grade in range(2, count + 1)]
    rest, counts = total - bound - (count - 1), [1] * (count - 1)
    while rest > 0:
        free = [i for i in range(count - 1) if counts[i] < bound]
        mass, budget = sum([portions[i] for i in free]), rest
        for i in free:
            more = min(bound - counts[i], max(1, budget * portions[i] // mass), rest)
            counts[i] = counts[i] + more
            rest = rest - more
    return np.array([bound] + counts)


def ragged(key, amount, total, limit, skew):
    if amount == 2:
        one = jax.random.randint(key, (), max(1, total - limit), min(limit, total - 1) + 1)
        return jnp.stack([one, total - one])
    tallies = jnp.asarray(length_profile(amount, total, limit, skew), jnp.int32)
    couples = (amount - 1) // 2
    donor, taker = tallies[1:1 + 2 * couples:2], tallies[2:2 + 2 * couples:2]
    slack = jnp.minimum(donor - 1, limit - taker)
    moved = jax.random.randint(jax.random.fold_in(key, 1), (couples,), 0, 1 << 20) % (slack + 1)
    tallies = tallies.at[1:1 + 2 * couples:2].set(donor - moved).at[2:2 + 2 * couples:2].set(taker + moved)
    return tallies[jax.random.permutation(jax.random.fold_in(key, 2), amount)]


def gaussian(own_key, shape, spread, limit, split=(), kind=jnp.bfloat16):
    gain = levels(own_key, shape, split, -0.22, 0.18) if split else 1.0
    values = jax.random.normal(own_key, shape, jnp.float32) * spread * gain
    return jnp.minimum(jnp.maximum(values, -limit), limit).astype(kind)


def setup_inputs(seed: int = 0) -> dict:
    streams_of = jax.random.split(jax.random.key(seed), 16)
    return {
        "hidden_in": gaussian(streams_of[0], (TOKENS, D), 1.0, 6.0, ((0, 32),)),
        "gate_in": gaussian(streams_of[1], (TOKENS, EXPERTS), 0.5, 4.0, ((0, 32),), jnp.float32),
        "routes": choose_distinct(streams_of[2], LAYERS * TOKENS, EXPERTS, TOP, 2048).reshape((LAYERS, TOKENS, TOP)),
        "priority": jax.vmap(lambda own: jax.random.permutation(own, TOP * TOK_DEV))(jax.random.split(streams_of[3], LAYERS * DEVICES)).reshape((LAYERS, DEVICES, TOP * TOK_DEV)).astype(jnp.int32),
        "segments": jax.vmap(lambda own: jnp.searchsorted(jnp.cumsum(ragged(own, DOCS, TOK_DEV, TOK_DEV // 2, 0)), jnp.arange(TOK_DEV), side="right"))(jax.random.split(streams_of[4], DEVICES)).reshape((DEVICES, TOK_DEV)).astype(jnp.int32),
        "norm_attn": jnp.clip(1.0 + 0.15 * jax.random.normal(streams_of[5], (LAYERS, D), jnp.float32), 0.25, 1.75).astype(jnp.bfloat16),
        "w_qkv": gaussian(streams_of[6], (LAYERS, D, 3 * D), D ** -0.5, 0.21875, ((1, 16),)),
        "w_out": gaussian(streams_of[7], (LAYERS, D, D), (D // 16) ** -0.5, 0.875, ((1, 16),)),
        "norm_moe": jnp.clip(1.0 + 0.15 * jax.random.normal(streams_of[8], (LAYERS, D), jnp.float32), 0.25, 1.75).astype(jnp.bfloat16),
        "w_router": gaussian(streams_of[9], (LAYERS, D, EXPERTS), (4 * D) ** -0.5, 0.109375, ((1, 16),)),
        "w_const": gaussian(streams_of[10], (LAYERS, D, 2 * NCONST), D ** -0.5, 0.21875, ((1, 16),)),
        "const_vec": gaussian(streams_of[11], (LAYERS, NCONST, D), 1.0, 5.0, ((2, 16),)),
        "w_gate_up": gaussian(streams_of[12], (LAYERS, EF, D, 2 * FF), D ** -0.5, 0.21875, ((2, 16),)),
        "w_down": gaussian(streams_of[13], (LAYERS, EF, FF, D), (FF // 4) ** -0.5, 0.25, ((2, 16),)),
        "grad_out": gaussian(streams_of[14], (TOKENS, D), 1.0, 6.0, ((0, 32),), jnp.float32),
    }


@jax.custom_vjp
def low(v):
    return lax.optimization_barrier(v.astype(jnp.bfloat16)).astype(jnp.float32)

@jax.custom_vjp
def low_back(v):
    return v

def low_keep(v):
    return (low(v), None)

def low_pass(kept, grad):
    return (grad,)

def back_keep(v):
    return (v, None)

def back_low(kept, grad):
    return (low(grad),)
low.defvjp(low_keep, low_pass)
low_back.defvjp(back_keep, back_low)
EPSILON = 1e-06
SCALE = 0.125
MASKED = -1000000000.0
HIGHEST_PRECISION = lax.Precision.HIGHEST

def rope_tables(tokens, head_size):
    half = head_size // 2
    places = jnp.arange(tokens, dtype=jnp.int32).astype(jnp.float32)[:, None]
    powers = jnp.arange(half, dtype=jnp.int32).astype(jnp.float32) / half
    angles = places * jnp.exp(-math.log(10000.0) * powers)[None, :]
    return (jnp.cos(angles)[:, None, :], jnp.sin(angles)[:, None, :])

def rotate(source, cosine, sine):
    half = source.shape[-1] // 2
    first, second = (source[..., :half], source[..., half:])
    return jnp.concatenate([first * cosine - second * sine, second * cosine + first * sine], axis=-1)

def softmax_rows(scores):
    shifted = jnp.exp(scores - lax.optimization_barrier(jnp.max(scores, axis=-1, keepdims=True)))
    return shifted / lax.optimization_barrier(jnp.sum(shifted, axis=-1, keepdims=True))

def silu_gate(source):
    return source * jax.nn.sigmoid(source)

def place_pairs(routes_now, order_now, ffn_count, capacity):
    flat_routes = routes_now.reshape(-1)
    pair_count = flat_routes.shape[0]
    numbers = jnp.arange(pair_count, dtype=jnp.int32)
    pair_at_rank = jnp.zeros((pair_count,), jnp.int32).at[order_now].set(numbers)
    route_by_rank = flat_routes[pair_at_rank]
    expert_ids = jnp.arange(EXPERTS, dtype=jnp.int32)
    hot_rank = (route_by_rank[:, None] == expert_ids[None, :]).astype(jnp.int32)
    before = jnp.cumsum(hot_rank, axis=0) - hot_rank
    place_by_rank = lax.optimization_barrier(jnp.sum(before * hot_rank, axis=1))
    position = place_by_rank[order_now]
    accepted = (flat_routes < ffn_count) & (position < capacity)
    sink = ffn_count * capacity
    slot_of_pair = jnp.where(accepted, flat_routes * capacity + position, sink).astype(jnp.int32)
    token_of_slot = jnp.full((sink + 1,), routes_now.shape[0], jnp.int32).at[slot_of_pair].set(numbers // routes_now.shape[1])[:sink]
    pair_of_slot = jnp.full((sink + 1,), pair_count, jnp.int32).at[slot_of_pair].set(numbers)[:sink]
    return (slot_of_pair, token_of_slot, pair_of_slot)

def layer_pass(weights, hidden, previous, routes_now, order_now, segment, cosine, sine):
    gain_attn, w_qkv, w_out, gain_moe, w_router, w_const, const_vec, w_gate_up, w_down = weights
    tokens, features = hidden.shape
    head_count = features // HEAD_DIM
    ffn_count, hidden_units = (w_down.shape[0], w_down.shape[1])
    inv_attn = lax.rsqrt(lax.optimization_barrier(jnp.mean(hidden * hidden, axis=-1, keepdims=True)) + EPSILON)
    normed = low(hidden * inv_attn * gain_attn)
    projected = low_back(jnp.dot(normed, w_qkv, precision=HIGHEST_PRECISION)).reshape(tokens, 3, head_count, HEAD_DIM)
    query = low(rotate(projected[:, 0], cosine, sine))
    keys = low(rotate(projected[:, 1], cosine, sine))
    values = low(projected[:, 2])
    scores = low_back(jnp.einsum('qhd,khd->hqk', query, keys, precision=HIGHEST_PRECISION) * SCALE)
    places = jnp.arange(tokens, dtype=jnp.int32)
    allowed = (segment[:, None] == segment[None, :]) & (places[None, :] <= places[:, None])
    probs = low(softmax_rows(jnp.where(allowed[None], scores, MASKED)))
    attended = low(low_back(jnp.einsum('hqk,khd->qhd', probs, values, precision=HIGHEST_PRECISION))).reshape(tokens, features)
    middle = hidden + low_back(jnp.dot(attended, w_out, precision=HIGHEST_PRECISION))
    inv_moe = lax.rsqrt(lax.optimization_barrier(jnp.mean(middle * middle, axis=-1, keepdims=True)) + EPSILON)
    mixed_in = middle * inv_moe * gain_moe
    mixed_low = low(mixed_in)
    logits = jnp.dot(mixed_low, w_router, precision=HIGHEST_PRECISION) + previous
    route_hot = (routes_now[:, :, None] == jnp.arange(EXPERTS, dtype=jnp.int32)[None, None, :]).astype(jnp.float32)
    gate_probs = softmax_rows(lax.optimization_barrier(jnp.sum(route_hot * logits[:, None, :], axis=-1)))
    shares = softmax_rows(jnp.dot(mixed_low, w_const, precision=HIGHEST_PRECISION).reshape(tokens, NCONST, 2))
    constant = shares[..., 0:1] * mixed_in[:, None, :] + shares[..., 1:2] * const_vec[None]
    slot_of_pair, token_of_slot, pair_of_slot = place_pairs(routes_now, order_now, ffn_count, CAP)
    padded = jnp.concatenate([mixed_low, jnp.zeros((1, features), jnp.float32)], axis=0)
    inputs = padded[token_of_slot].reshape(ffn_count, CAP, features)
    gate_up = low_back(jnp.einsum('ecd,edf->ecf', inputs, w_gate_up, precision=HIGHEST_PRECISION))
    activated = low(silu_gate(gate_up[..., :hidden_units]) * gate_up[..., hidden_units:])
    expert_out = low_back(jnp.einsum('ecf,efd->ecd', activated, w_down, precision=HIGHEST_PRECISION)).reshape(ffn_count * CAP, features)
    out_padded = jnp.concatenate([expert_out, jnp.zeros((1, features), jnp.float32)], axis=0)
    pair_out = out_padded[slot_of_pair].reshape(tokens, TOP, features)
    copy_flag = (routes_now == ffn_count + 1).astype(jnp.float32)
    const_flag = (routes_now[:, :, None] == ffn_count + 2 + jnp.arange(NCONST, dtype=jnp.int32)[None, None, :]).astype(jnp.float32)
    pair_value = pair_out + copy_flag[..., None] * mixed_in[:, None, :] + lax.optimization_barrier(jnp.sum(const_flag[..., None] * constant[:, None, :, :], axis=2))
    return (middle + lax.optimization_barrier(jnp.sum(gate_probs[..., None] * pair_value, axis=1)), logits)

def reference(hidden_in, gate_in, routes, priority, segments, norm_attn, w_qkv, w_out, norm_moe, w_router, w_const, const_vec, w_gate_up, w_down, grad_out):
    weights = tuple((member.astype(jnp.float32) for member in (norm_attn, w_qkv, w_out, norm_moe, w_router, w_const, const_vec, w_gate_up, w_down)))
    hidden = hidden_in.astype(jnp.float32).reshape(DEVICES, TOK_DEV, D)
    gates_start = gate_in.reshape(DEVICES, TOK_DEV, EXPERTS)
    route_blocks = jnp.transpose(routes.reshape(LAYERS, DEVICES, TOK_DEV, TOP), (1, 0, 2, 3))
    order_blocks = jnp.transpose(priority, (1, 0, 2))
    cosine, sine = rope_tables(TOK_DEV, HEAD_DIM)

    def whole(weights, hidden, gates_start):

        def one_block(block_items):
            state, logits, route_now, order_now, segment = block_items
            for layer_index in range(LAYERS):
                layer_weights = tuple((member[layer_index] for member in weights))
                state, logits = layer_pass(layer_weights, state, logits, route_now[layer_index], order_now[layer_index], segment, cosine, sine)
            return state
        return lax.map(jax.checkpoint(one_block), (hidden, gates_start, route_blocks, order_blocks, segments))
    result, pullback = jax.vjp(whole, weights, hidden, gates_start)
    d_weights, d_hidden, d_gates = pullback(grad_out.reshape(DEVICES, TOK_DEV, D))
    return (result.reshape(TOKENS, D).astype(jnp.bfloat16), d_hidden.reshape(TOKENS, D), d_gates.reshape(TOKENS, EXPERTS), d_weights[0], d_weights[1], d_weights[2], d_weights[3], d_weights[4], d_weights[5], d_weights[6], d_weights[7], d_weights[8])
```

```python
import functools
import math

import jax
import jax.numpy as jnp
from jax import lax
from jax.sharding import PartitionSpec as P

HEAD_DIM = 64
EF = 4
NCONST = 2
TOP = 2
EXPERTS = 8
CAP = 80
SMALL = 2 + EXPERTS + 2 * NCONST + NCONST
LANES = 128

EPSILON = 1e-06
SCALE = 0.125
MASKED = -1000000000.0
EXACT = lax.Precision.HIGHEST
AXES = ("rep", "shard")
BF16 = jnp.bfloat16
F32 = jnp.float32


def dot(a, b, dims=((1,), (0,))):
    return lax.dot_general(a, b, (dims, ((), ())), preferred_element_type=F32)


def rope_tables(tokens, head_size):
    half = head_size // 2
    places = jnp.arange(tokens, dtype=jnp.int32).astype(F32)[:, None]
    powers = jnp.arange(half, dtype=jnp.int32).astype(F32) / half
    angles = places * jnp.exp(-math.log(10000.0) * powers)[None, :]
    return (jnp.cos(angles)[:, None, :], jnp.sin(angles)[:, None, :])


def rotate(source, cosine, sine):
    half = source.shape[-1] // 2
    first, second = (source[..., :half], source[..., half:])
    return jnp.concatenate(
        [first * cosine - second * sine, second * cosine + first * sine], axis=-1
    )


def rotate_back(grad_rows, cosine, sine):
    return rotate(grad_rows, cosine, -sine)


def softmax_rows(scores):
    shifted = jnp.exp(scores - jnp.max(scores, axis=-1, keepdims=True))
    return shifted / jnp.sum(shifted, axis=-1, keepdims=True)


def norm_back(grad_rows, source, inverse, gain):
    scaled = grad_rows * gain
    gain_grad = jnp.sum(grad_rows * source * inverse, axis=0)
    source_grad = inverse * scaled - source * inverse**3 * jnp.mean(
        scaled * source, axis=-1, keepdims=True
    )
    return (source_grad, gain_grad)


class Layout:
    def __init__(self, mesh):
        self.reps, self.shards = mesh.shape["rep"], mesh.shape["shard"]
        self.lines = self.shards // EF
        assert self.shards % EF == 0 and EF % self.reps == 0

    def pairs(self, move):
        found = []
        for rep in range(self.reps):
            for shard in range(self.shards):
                r, z, j = move(rep, shard // EF, shard % EF)
                found.append((rep * self.shards + shard, r * self.shards + z * EF + j))
        return found

    def send(self, x, move):
        return lax.ppermute(x, AXES, self.pairs(move))

    def expert_move(self, mask, shift):
        def move(r, z, j):
            number = r * EF + j
            e, f = (number // self.reps) ^ mask, (number % self.reps + shift) % self.reps
            number = e * self.reps + f
            return number // EF, z, number % EF

        return move

    def place(self):
        rep, shard = lax.axis_index("rep"), lax.axis_index("shard")
        j = shard % EF
        return rep, j, (rep * EF + j) // self.reps

    def quad_exchange(self, blocks, j):
        got = lax.dynamic_update_slice_in_dim(
            jnp.zeros_like(blocks), lax.dynamic_slice_in_dim(blocks, j, 1, 0), j, 0
        )
        for mask in range(1, EF):
            other = j ^ mask
            block = lax.dynamic_slice_in_dim(blocks, other, 1, 0)
            block = self.send(block, lambda r, z, q: (r, z, q ^ mask))
            got = lax.dynamic_update_slice_in_dim(got, block, other, 0)
        return got

    def part_exchange(self, blocks, j):
        count = EF // self.reps
        mine = j // self.reps
        got = lax.dynamic_update_slice_in_dim(
            jnp.zeros_like(blocks), lax.dynamic_slice_in_dim(blocks, mine, 1, 0), mine, 0
        )
        for mask in range(1, count):
            other = mine ^ mask
            block = lax.dynamic_slice_in_dim(blocks, other, 1, 0)
            block = self.send(block, lambda r, z, q: (r, z, q ^ (mask * self.reps)))
            got = lax.dynamic_update_slice_in_dim(got, block, other, 0)
        return got

    def rep_gather(self, x, rep):
        got = lax.dynamic_update_slice_in_dim(
            jnp.zeros((self.reps,) + x.shape, x.dtype), x[None], rep, 0
        )
        for shift in range(1, self.reps):
            block = self.send(x, lambda r, z, q: ((r + shift) % self.reps, z, q))
            got = lax.dynamic_update_slice_in_dim(
                got, block[None], (rep + self.reps - shift) % self.reps, 0
            )
        return got

    def line_groups(self):
        return [[z * EF + j for z in range(self.lines)] for j in range(EF)]

    def line_gather(self, x):
        return lax.all_gather(
            x, "shard", axis=0, tiled=True, axis_index_groups=self.line_groups()
        )

    def line_sum(self, x):
        return lax.psum_scatter(
            x, "shard", scatter_dimension=0, tiled=True, axis_index_groups=self.line_groups()
        )

    def dispatch(self, rows):
        blocks = rows.reshape(EF, CAP, -1)
        own = jnp.stack(
            [blocks[0]] + [self.send(blocks[m], self.expert_move(m, 0)) for m in range(1, EF)]
        )
        parts = [own] + [self.send(own, self.expert_move(0, g)) for g in range(1, self.reps)]
        return jnp.concatenate(parts).reshape(self.reps * EF * CAP, -1)

    def collect(self, rows):
        blocks = rows.reshape(self.reps, EF * CAP, -1)
        total = blocks[0]
        for g in range(1, self.reps):
            total = total + self.send(
                blocks[g].astype(BF16), self.expert_move(0, self.reps - g)
            ).astype(F32)
        total = total.astype(BF16).reshape(EF, CAP, -1)
        return jnp.concatenate(
            [total[0]] + [self.send(total[m], self.expert_move(m, 0)) for m in range(1, EF)]
        )


def split_columns(array, layout):
    width = array.shape[-1] // (2 * layout.shards)
    return array.reshape(array.shape[:-1] + (2, layout.shards // layout.reps, layout.reps, width))


def expert_weights(layout, w_gate_up, w_down, rep, j):
    features = w_gate_up.shape[1]
    blocks = split_columns(w_gate_up, layout)
    blocks = jnp.transpose(blocks, (0, 4, 1, 2, 3, 5)).reshape(EF * layout.reps, features, -1)
    mine = lax.dynamic_slice_in_dim(blocks, rep * EF, EF, 0)
    mine = layout.quad_exchange(mine, j).reshape(EF * features, -1)
    gate_up = layout.line_gather(mine)
    count = EF // layout.reps
    down = lax.dynamic_slice_in_dim(w_down, rep * count, count, 0)
    down = layout.part_exchange(down, j).reshape(count * w_down.shape[1], -1)
    return gate_up, layout.line_gather(down)


def expert_grads(layout, grad_gate_up, grad_down, rep, j):
    down = layout.line_sum(grad_down)
    count = EF // layout.reps
    down = layout.part_exchange(down.reshape(count, -1, down.shape[-1]), j)
    down = layout.rep_gather(down, rep).reshape((EF,) + down.shape[1:]).astype(F32)
    mine = layout.line_sum(grad_gate_up)
    mine = layout.quad_exchange(mine.reshape(EF, -1, mine.shape[-1]), j)
    full = layout.rep_gather(mine, rep)
    features = mine.shape[1]
    full = full.reshape(EF, layout.reps, features, 2, layout.shards // layout.reps, -1)
    full = jnp.transpose(full, (0, 2, 3, 4, 1, 5)).reshape(EF, features, -1)
    return full.astype(F32), down


def place_pairs(routes, priority, expert):
    flat = routes.reshape(-1)
    ahead = (flat[:, None] == flat[None, :]) & (priority[:, None] < priority[None, :])
    position = jnp.sum(ahead.astype(jnp.int32), axis=0)
    kept = (flat < EF) & (position < CAP)
    slot = jnp.where(kept, (flat ^ expert) * CAP + position, EF * CAP).reshape(-1, TOP)
    places = jnp.arange(EF * CAP, dtype=jnp.int32)[:, None]
    return [(places == slot[:, k][None, :]).astype(BF16) for k in range(TOP)]


def attention_forward(weights, hidden, allowed, cosine, sine):
    gain, w_qkv, w_out = weights
    tokens, features = hidden.shape
    heads = features // HEAD_DIM
    inverse = lax.rsqrt(jnp.mean(hidden * hidden, axis=-1, keepdims=True) + EPSILON)
    normed = (hidden * inverse * gain).astype(BF16)
    projected = dot(normed, w_qkv).reshape(tokens, 3, heads, HEAD_DIM)
    query = rotate(projected[:, 0], cosine, sine).astype(BF16)
    keys = rotate(projected[:, 1], cosine, sine).astype(BF16)
    values = projected[:, 2].astype(BF16)
    scores = jnp.einsum("qhd,khd->hqk", query, keys, preferred_element_type=F32) * SCALE
    scores = jnp.where(allowed[None], scores, MASKED)
    row_max = jnp.max(scores, axis=-1, keepdims=True)
    weight = jnp.exp(scores - row_max)
    total = jnp.sum(weight, axis=-1, keepdims=True)
    probs = (weight / total).astype(BF16)
    outputs = jnp.einsum("hqk,khd->qhd", probs, values, preferred_element_type=F32)
    attended = outputs.reshape(tokens, features).astype(BF16)
    middle = hidden + dot(attended, w_out)
    log_total = row_max + jnp.log(total)
    return middle, (hidden, inverse, normed, query, keys, values, log_total, attended)


def attention_backward(weights, kept, d_middle, allowed, cosine, sine):
    gain, w_qkv, w_out = weights
    hidden, inverse, normed, query, keys, values, log_total, attended = kept
    tokens, features = hidden.shape
    heads = features // HEAD_DIM
    d_branch = d_middle.astype(BF16)
    grad_out = dot(attended, d_branch, ((0,), (0,)))
    d_attended = dot(d_branch, w_out, ((1,), (1,))).astype(BF16)
    d_attended = d_attended.reshape(tokens, heads, HEAD_DIM)
    scores = jnp.einsum("qhd,khd->hqk", query, keys, preferred_element_type=F32) * SCALE
    scores = jnp.where(allowed[None], scores, MASKED)
    probs = jnp.exp(scores - log_total)
    d_values = jnp.einsum(
        "hqk,qhd->khd", probs.astype(BF16), d_attended, preferred_element_type=F32
    )
    d_probs = jnp.einsum("qhd,khd->hqk", d_attended, values, preferred_element_type=F32)
    d_scores = (probs * (d_probs - jnp.sum(d_probs * probs, axis=-1, keepdims=True))).astype(BF16)
    d_query = jnp.einsum("hqk,khd->qhd", d_scores, keys, preferred_element_type=F32) * SCALE
    d_keys = jnp.einsum("hqk,qhd->khd", d_scores, query, preferred_element_type=F32) * SCALE
    d_projected = (
        jnp.stack(
            [rotate_back(d_query, cosine, sine), rotate_back(d_keys, cosine, sine), d_values],
            axis=1,
        )
        .reshape(tokens, 3 * features)
        .astype(BF16)
    )
    grad_qkv = dot(normed, d_projected, ((0,), (0,)))
    d_normed = dot(d_projected, w_qkv, ((1,), (1,)))
    d_hidden, grad_gain = norm_back(d_normed, hidden, inverse, gain)
    return d_hidden + d_middle, grad_gain, grad_qkv, grad_out


def moe_forward(layout, small, w_gate_up, w_down, middle, previous, routes, onehots):
    gain, w_router, w_const, const_vec = small
    tokens, features = middle.shape
    inverse = lax.rsqrt(jnp.mean(middle * middle, axis=-1, keepdims=True) + EPSILON)
    mixed = middle * inverse * gain
    mixed_low = mixed.astype(BF16)
    rows = dot(onehots[0] + onehots[1], mixed_low).astype(BF16)
    inputs = layout.dispatch(rows)
    logits = dot(mixed_low, w_router) + previous
    ids = jnp.arange(EXPERTS, dtype=jnp.int32)
    hot = (routes[:, :, None] == ids[None, None, :]).astype(F32)
    gates = softmax_rows(jnp.sum(hot * logits[:, None, :], axis=-1))
    shares = softmax_rows(dot(mixed_low, w_const).reshape(tokens, NCONST, 2))
    const_flag = hot[:, :, EF + 2 :]
    copy_flag = hot[:, :, EF + 1]
    mixed_part = copy_flag + jnp.sum(const_flag * shares[:, None, :, 0], axis=-1)
    vector_part = const_flag * shares[:, None, :, 1]
    gate_up = dot(inputs, w_gate_up)
    hidden_units = gate_up.shape[-1] // 2
    gate_part = gate_up[:, :hidden_units]
    activated = (gate_part * jax.nn.sigmoid(gate_part) * gate_up[:, hidden_units:]).astype(BF16)
    outputs = layout.collect(dot(activated, w_down))
    values = [
        dot(onehots[k], outputs, ((0,), (0,)))
        + mixed_part[:, k : k + 1] * mixed
        + sum(vector_part[:, k, c : c + 1] * const_vec[c][None] for c in range(NCONST))
        for k in range(TOP)
    ]
    result = middle + sum(gates[:, k : k + 1] * values[k] for k in range(TOP))
    kept = (middle, inverse, mixed, mixed_low, hot, gates, shares, values, inputs, gate_up, activated)
    return result, logits, kept


def moe_backward(layout, small, w_gate_up, w_down, kept, onehots, d_result, d_next):
    gain, w_router, w_const, const_vec = small
    middle, inverse, mixed, mixed_low, hot, gates, shares, values, inputs, gate_up, activated = kept
    tokens, features = middle.shape
    rows = sum(
        dot(onehots[k], (gates[:, k : k + 1] * d_result).astype(BF16)) for k in range(TOP)
    ).astype(BF16)
    d_expert = layout.dispatch(rows)
    d_gates = jnp.stack([jnp.sum(v * d_result, axis=-1) for v in values], axis=-1)
    d_chosen = gates * (d_gates - jnp.sum(gates * d_gates, axis=-1, keepdims=True))
    d_logits = jnp.sum(hot * d_chosen[..., None], axis=1) + d_next
    const_weight = jnp.sum(hot[:, :, EF + 2 :] * gates[..., None], axis=1)
    d_shares = jnp.stack(
        [
            const_weight * jnp.sum(d_result * mixed, axis=-1, keepdims=True),
            const_weight
            * jnp.stack(
                [jnp.sum(d_result * const_vec[c][None], axis=-1) for c in range(NCONST)], axis=-1
            ),
        ],
        axis=-1,
    )
    d_mix = (shares * (d_shares - jnp.sum(shares * d_shares, axis=-1, keepdims=True))).reshape(
        tokens, 2 * NCONST
    )
    terms = jnp.concatenate([d_logits, d_mix], axis=-1)
    grad_terms = lax.dot_general(
        mixed_low.astype(F32), terms, (((0,), (0,)), ((), ())), precision=EXACT
    )
    grad_vec = lax.dot_general(
        d_result, shares[..., 1] * const_weight, (((0,), (0,)), ((), ())), precision=EXACT
    )
    direct = jnp.sum(hot[:, :, EF + 1] * gates, axis=-1, keepdims=True) + jnp.sum(
        shares[..., 0] * const_weight, axis=-1, keepdims=True
    )
    both = jnp.concatenate([w_router, w_const], axis=-1).astype(F32)
    d_mixed = direct * d_result + lax.dot_general(
        terms, both, (((1,), (1,)), ((), ())), precision=EXACT
    )
    hidden_units = gate_up.shape[-1] // 2
    gate_part, up_part = gate_up[:, :hidden_units], gate_up[:, hidden_units:]
    d_activated = dot(d_expert, w_down, ((1,), (1,)))
    grad_down = dot(activated, d_expert, ((0,), (0,))).astype(BF16)
    sigmoid = jax.nn.sigmoid(gate_part)
    d_gate_up = jnp.concatenate(
        [
            d_activated * up_part * sigmoid * (1.0 + gate_part * (1.0 - sigmoid)),
            d_activated * gate_part * sigmoid,
        ],
        axis=-1,
    ).astype(BF16)
    d_rows = layout.collect(dot(d_gate_up, w_gate_up, ((1,), (1,))))
    grad_gate_up = dot(inputs, d_gate_up, ((0,), (0,))).astype(BF16)
    d_mixed = d_mixed + dot(onehots[0] + onehots[1], d_rows, ((0,), (0,)))
    d_middle, grad_gain = norm_back(d_mixed, middle, inverse, gain)
    small_grads = (grad_gain, grad_terms, grad_vec)
    return d_middle + d_result, d_logits, small_grads, grad_gate_up, grad_down


def local(
    layout,
    hidden_in,
    gate_in,
    routes,
    priority,
    segments,
    norm_attn,
    w_qkv,
    w_out,
    norm_moe,
    w_router,
    w_const,
    const_vec,
    w_gate_up,
    w_down,
    grad_out,
):
    layers = w_qkv.shape[0]
    tokens, features = hidden_in.shape
    rep, j, expert = layout.place()
    slim = w_qkv.shape[1]
    small = jnp.concatenate(
        [
            piece
            for l in range(layers)
            for piece in (
                norm_attn[l][:, None],
                norm_moe[l][:, None],
                w_router[l],
                w_const[l],
                const_vec[l].T,
            )
        ]
        + [jnp.zeros((slim, LANES - layers * SMALL), BF16)],
        axis=-1,
    )
    dense = []
    moe = []
    for l in range(layers):
        packed = [w_qkv[l], w_out[l]] + ([small] if l == 0 else [])
        dense.append(lax.all_gather(jnp.concatenate(packed, axis=-1), "shard", axis=0, tiled=True))
        moe.append(expert_weights(layout, w_gate_up[l], w_down[l], rep, j))
    wide = 3 * features
    small_full = dense[0][:, wide + features :].astype(F32)
    attn_weights, small_weights = [], []
    for l in range(layers):
        part = small_full[:, l * SMALL : (l + 1) * SMALL]
        router = part[:, 2 : 2 + EXPERTS].astype(BF16)
        const = part[:, 2 + EXPERTS : 2 + EXPERTS + 2 * NCONST].astype(BF16)
        attn_weights.append((part[:, 0][None], dense[l][:, :wide], dense[l][:, wide : wide + features]))
        small_weights.append((part[:, 1][None], router, const, part[:, SMALL - NCONST :].T))

    segment = segments[0]
    places = jnp.arange(tokens, dtype=jnp.int32)
    allowed = (segment[:, None] == segment[None, :]) & (places[None, :] <= places[:, None])
    cosine, sine = rope_tables(tokens, HEAD_DIM)
    onehots = [place_pairs(routes[l], priority[l, 0], expert) for l in range(layers)]

    hidden = hidden_in.astype(F32)
    previous = gate_in
    attn_kept, moe_kept = [], []
    for l in range(layers):
        middle, kept = attention_forward(attn_weights[l], hidden, allowed, cosine, sine)
        attn_kept.append(kept)
        hidden, previous, kept = moe_forward(
            layout, small_weights[l], *moe[l], middle, previous, routes[l], onehots[l]
        )
        moe_kept.append(kept)

    grad_hidden = grad_out
    grad_gate = jnp.zeros_like(gate_in)
    dense_grads, moe_grads = [None] * layers, [None] * layers
    for l in reversed(range(layers)):
        d_middle, grad_gate, small_grads, grad_gate_up, grad_down = moe_backward(
            layout, small_weights[l], *moe[l], moe_kept[l], onehots[l], grad_hidden, grad_gate
        )
        moe_grads[l] = expert_grads(layout, grad_gate_up, grad_down, rep, j)
        grad_hidden, grad_gain, grad_qkv, grad_proj = attention_backward(
            attn_weights[l], attn_kept[l], d_middle, allowed, cosine, sine
        )
        packed = jnp.concatenate(
            [
                grad_qkv,
                grad_proj,
                grad_gain[:, None],
                small_grads[0][:, None],
                small_grads[1],
                small_grads[2],
                jnp.zeros((features, LANES - SMALL), F32),
            ],
            axis=-1,
        ).astype(BF16)
        piece = lax.psum_scatter(packed, "shard", scatter_dimension=0, tiled=True)
        dense_grads[l] = jnp.sum(layout.rep_gather(piece, rep).astype(F32), axis=0)

    dense_all = jnp.stack(dense_grads)
    base = wide + features
    return (
        hidden.astype(BF16),
        grad_hidden,
        grad_gate,
        dense_all[:, :, base],
        dense_all[:, :, :wide],
        dense_all[:, :, wide:base],
        dense_all[:, :, base + 1],
        dense_all[:, :, base + 2 : base + 2 + EXPERTS],
        dense_all[:, :, base + 2 + EXPERTS : base + SMALL - NCONST],
        jnp.transpose(dense_all[:, :, base + SMALL - NCONST : base + SMALL], (0, 2, 1)),
        jnp.stack([g[0] for g in moe_grads]),
        jnp.stack([g[1] for g in moe_grads]),
    )


def solution(mesh):
    return jax.shard_map(
        functools.partial(local, Layout(mesh)),
        mesh=mesh,
        in_specs=(
            P(("rep", "shard"), None),
            P(("rep", "shard"), None),
            P(None, ("rep", "shard"), None),
            P(None, ("rep", "shard"), None),
            P(("rep", "shard"), None),
            P(None, "shard"),
            P(None, "shard", None),
            P(None, "shard", None),
            P(None, "shard"),
            P(None, "shard", None),
            P(None, "shard", None),
            P(None, None, "shard"),
            P(None, None, "shard", None),
            P(None, None, "shard", None),
            P(("rep", "shard"), None),
        ),
        out_specs=(
            P(("rep", "shard"), None),
            P(("rep", "shard"), None),
            P(("rep", "shard"), None),
            P(None, "shard"),
            P(None, "shard", None),
            P(None, "shard", None),
            P(None, "shard"),
            P(None, "shard", None),
            P(None, "shard", None),
            P(None, None, "shard"),
            P(None, None, "shard", None),
            P(None, None, "shard", None),
        ),
        check_vma=False,
    )
```

```python
import functools
import math

import jax
import jax.numpy as jnp
from jax import lax
from jax.experimental import pallas as pl
from jax.experimental.pallas import tpu as pltpu
from jax.sharding import PartitionSpec as P

HEAD_DIM = 64
EF = 4
NCONST = 2
TOP = 2
EXPERTS = 8
CAP = 80
SMALL = 2 + EXPERTS + 2 * NCONST + NCONST
ROWS = 16
LANES = 128

EPSILON = 1e-06
SCALE = 0.125
MASKED = -1000000000.0
AXES = ("rep", "shard")
BF16 = jnp.bfloat16
F32 = jnp.float32


def dot(a, b, dims=((1,), (0,))):
    return lax.dot_general(a, b, (dims, ((), ())), preferred_element_type=F32)


def rope_tables(tokens):
    half = HEAD_DIM // 2
    places = jnp.arange(tokens, dtype=jnp.int32).astype(F32)[:, None]
    powers = jnp.arange(half, dtype=jnp.int32).astype(F32) / half
    angles = places * jnp.exp(-math.log(10000.0) * powers)[None, :]
    cosine, sine = jnp.cos(angles), jnp.sin(angles)
    heads = LANES // HEAD_DIM
    return jnp.tile(cosine, (1, 2 * heads)), jnp.tile(
        jnp.concatenate([-sine, sine], axis=-1), (1, heads)
    )


def turn(block, cosine, sine):
    half = HEAD_DIM // 2
    lane = lax.broadcasted_iota(jnp.int32, block.shape, 1)
    width = block.shape[1]
    partner = jnp.where(
        lane % HEAD_DIM < half,
        pltpu.roll(block, width - half, 1),
        pltpu.roll(block, half, 1),
    )
    return block * cosine + partner * sine


def lane_pick(array, lane, index):
    return jnp.sum(jnp.where(lane == index, array, 0.0), axis=-1, keepdims=True)


def inverse_rms(x):
    return lax.rsqrt(jnp.mean(x * x, axis=-1, keepdims=True) + EPSILON)


def attention_bias(seg_col, seg_row):
    shape = (seg_col.shape[0], seg_row.shape[1])
    rows = lax.broadcasted_iota(jnp.int32, shape, 0)
    columns = lax.broadcasted_iota(jnp.int32, shape, 1)
    allowed = (seg_col[...] == seg_row[...]) & (columns <= rows)
    return jnp.where(allowed, 0.0, MASKED)


def head_masks(shape):
    lane = lax.broadcasted_iota(jnp.int32, shape, 1)
    return [(lane // HEAD_DIM) == half for half in range(LANES // HEAD_DIM)]


def columns_of(step, width):
    return pl.ds(pl.multiple_of(step * width, width), width)


def attention_forward_kernel(
    hidden, gains, weights, cosine, sine, seg_col, seg_row, mixing, previous, routes, gather,
    normed, query, keys, values, log_total, attended, middle, mixed_low, logits, coefs, rows,
    bias,
):
    tokens, features = hidden.shape
    h = hidden[...].astype(F32)
    normed[...] = (h * inverse_rms(h) * gains[0:1]).astype(BF16)
    bias[...] = attention_bias(seg_col, seg_row)
    wide = 2 * LANES
    for block, out in ((0, query), (1, keys)):

        @pl.loop(0, features // wide)
        def _(step):
            part = dot(normed[...], weights[block, :, columns_of(step, wide)])
            for k in range(2):
                turned = turn(part[:, k * LANES : (k + 1) * LANES], cosine[...], sine[...])
                out[:, columns_of(2 * step + k, LANES)] = turned.astype(BF16)

    @pl.loop(0, features // wide)
    def _(step):
        at = columns_of(step, wide)
        values[:, at] = dot(normed[...], weights[2, :, at]).astype(BF16)

    log_total[...] = jnp.zeros_like(log_total)

    @pl.loop(0, features // LANES)
    def _(step):
        at = columns_of(step, LANES)
        q, k, v = query[:, at], keys[:, at], values[:, at]
        lane = lax.broadcasted_iota(jnp.int32, log_total.shape, 1)
        total_out = jnp.zeros((tokens, LANES), F32)
        for half, mask in enumerate(head_masks(q.shape)):
            scores = dot(jnp.where(mask, q, 0), k, ((1,), (1,))) * SCALE + bias[...]
            top = jnp.max(scores, axis=-1, keepdims=True)
            weight = jnp.exp(scores - top)
            total = jnp.sum(weight, axis=-1, keepdims=True)
            probs = (weight * (1.0 / total)).astype(BF16)
            total_out += dot(probs, jnp.where(mask, v, 0))
            log_total[...] = jnp.where(
                lane == step * (LANES // HEAD_DIM) + half, top + jnp.log(total), log_total[...]
            )
        attended[:, at] = total_out.astype(BF16)

    @pl.loop(0, features // wide)
    def _(step):
        at = columns_of(step, wide)
        middle[:, at] = hidden[:, at].astype(F32) + dot(attended[...], weights[3, :, at])

    m = middle[...]
    low = (m * inverse_rms(m) * gains[1:2]).astype(BF16)
    mixed_low[...] = low
    rows[...] = dot(gather[...], low).astype(BF16)
    raw = dot(low, mixing[...])
    lane = lax.broadcasted_iota(jnp.int32, raw.shape, 1)
    now = jnp.where(lane < EXPERTS, raw + previous[...], 0.0)
    logits[...] = now
    route = [routes[:, k : k + 1] for k in range(TOP)]
    chosen = [lane_pick(now, lane, route[k]) for k in range(TOP)]
    best = jnp.maximum(chosen[0], chosen[1])
    chosen = [jnp.exp(c - best) for c in chosen]
    gates = [c / (chosen[0] + chosen[1]) for c in chosen]
    shares = []
    for c in range(NCONST):
        pair = [lane_pick(raw, lane, EXPERTS + 2 * c + i) for i in range(2)]
        best = jnp.maximum(pair[0], pair[1])
        pair = [jnp.exp(p - best) for p in pair]
        shares.append([p / (pair[0] + pair[1]) for p in pair])
    copies = [(route[k] == EF + 1).astype(F32) for k in range(TOP)]
    consts = [[(route[k] == EF + 2 + c).astype(F32) for c in range(NCONST)] for k in range(TOP)]
    weight = [sum(consts[k][c] * gates[k] for k in range(TOP)) for c in range(NCONST)]
    columns = list(gates)
    columns += [
        copies[k] + sum(consts[k][c] * shares[c][0] for c in range(NCONST)) for k in range(TOP)
    ]
    columns += [consts[k][c] * shares[c][1] for k in range(TOP) for c in range(NCONST)]
    columns += [shares[c][i] for c in range(NCONST) for i in range(2)]
    columns += weight
    columns += [
        sum(copies[k] * gates[k] for k in range(TOP))
        + sum(shares[c][0] * weight[c] for c in range(NCONST))
    ]
    columns += [shares[c][1] * weight[c] for c in range(NCONST)]
    packed = jnp.zeros_like(raw)
    for index, column in enumerate(columns):
        packed = jnp.where(lane == index, column, packed)
    coefs[...] = packed


GATE, MIXED, VECTOR, SHARE, WEIGHT, DIRECT, CONST = 0, 2, 4, 8, 12, 14, 15


def combine_kernel(coefs, middle, gains, scatter, outputs, vectors, result):
    coef = coefs[...]
    m = middle[...]
    total = m + coef[:, DIRECT : DIRECT + 1] * (m * inverse_rms(m) * gains[1:2])
    for k in range(TOP):
        total += coef[:, GATE + k : GATE + k + 1] * dot(scatter[k], outputs[...])
    for c in range(NCONST):
        total += coef[:, CONST + c : CONST + c + 1] * vectors[c : c + 1]
    result[...] = total


def value_rows_kernel(coefs, gather, d_result, rows):
    coef = coefs[...]
    rows[...] = sum(
        dot(gather[k], (coef[:, GATE + k : GATE + k + 1] * d_result[...]).astype(BF16))
        for k in range(TOP)
    ).astype(BF16)


def two_parts(x):
    high = x.astype(BF16)
    return high, (x - high.astype(F32)).astype(BF16)


def gate_backward_kernel(
    coefs, middle, gains, scatter, outputs, vectors, routes, mixed_low, mixing_t, d_result, d_next,
    d_logits, d_mixed, grads,
):
    coef = coefs[...]
    m = middle[...]
    dh = d_result[...]
    lane = lax.broadcasted_iota(jnp.int32, coef.shape, 1)

    def column(index):
        return coef[:, index : index + 1]

    along = jnp.sum(m * inverse_rms(m) * gains[1:2] * dh, axis=-1, keepdims=True)
    with_vector = [
        jnp.sum(dh * vectors[c : c + 1], axis=-1, keepdims=True) for c in range(NCONST)
    ]
    d_gates = []
    for k in range(TOP):
        value = jnp.sum(dot(scatter[k], outputs[...]) * dh, axis=-1, keepdims=True)
        value += column(MIXED + k) * along
        value += sum(column(VECTOR + k * NCONST + c) * with_vector[c] for c in range(NCONST))
        d_gates.append(value)
    mean = sum(column(GATE + k) * d_gates[k] for k in range(TOP))
    terms = d_next[...]
    for k in range(TOP):
        chosen = column(GATE + k) * (d_gates[k] - mean)
        terms += jnp.where(lane == routes[:, k : k + 1], chosen, 0.0)
    d_logits[...] = terms
    vector_terms = jnp.zeros_like(terms)
    for c in range(NCONST):
        share = [column(SHARE + 2 * c + i) for i in range(2)]
        d_share = [column(WEIGHT + c) * along, column(WEIGHT + c) * with_vector[c]]
        mean = share[0] * d_share[0] + share[1] * d_share[1]
        for i in range(2):
            terms = jnp.where(
                lane == EXPERTS + 2 * c + i, share[i] * (d_share[i] - mean), terms
            )
        vector_terms = jnp.where(
            lane == EXPERTS + 2 * NCONST + c, column(CONST + c), vector_terms
        )
    high, lowest = two_parts(terms)
    d_mixed[...] = column(DIRECT) * dh + dot(high, mixing_t[...]) + dot(lowest, mixing_t[...])
    both = ((0,), (0,))
    total = dot(high, mixed_low[...], both) + dot(lowest, mixed_low[...], both)
    high, lowest = two_parts(vector_terms)
    dh_high, dh_low = two_parts(dh)
    total += dot(high, dh_high, both) + dot(lowest, dh_high, both) + dot(high, dh_low, both)
    grads[...] = total[: grads.shape[0]]


def expert_forward_kernel(inputs, w_gate_up, w_down, gate_up, activated, own, others):
    units = w_down.shape[0]
    wide = min(2 * LANES, units)
    kept = own.shape[0]

    @pl.loop(0, units // wide)
    def _(step):
        at = columns_of(step, wide)
        gate = dot(inputs[...], w_gate_up[:, at])
        up_at = pl.ds(pl.multiple_of(units + step * wide, wide), wide)
        up = dot(inputs[...], w_gate_up[:, up_at])
        gate_up[:, at] = gate
        gate_up[:, up_at] = up
        activated[:, at] = (gate / (1.0 + jnp.exp(-gate)) * up).astype(BF16)

    @pl.loop(0, w_down.shape[1] // (2 * LANES))
    def _(step):
        at = columns_of(step, 2 * LANES)
        out = dot(activated[...], w_down[:, at])
        own[:, at] = out[:kept]
        others[:, at] = out[kept:].astype(BF16)


def expert_backward_kernel(d_expert, w_gate_up, w_down, gate_up, d_gate_up, own, others):
    units = w_down.shape[0]
    wide = min(2 * LANES, units)
    kept = own.shape[0]

    @pl.loop(0, units // wide)
    def _(step):
        at = columns_of(step, wide)
        up_at = pl.ds(pl.multiple_of(units + step * wide, wide), wide)
        d_active = dot(d_expert[...], w_down[at, :], ((1,), (1,)))
        gate, up = gate_up[:, at], gate_up[:, up_at]
        sigmoid = 1.0 / (1.0 + jnp.exp(-gate))
        d_gate_up[:, at] = (
            d_active * up * sigmoid * (1.0 + gate * (1.0 - sigmoid))
        ).astype(BF16)
        d_gate_up[:, up_at] = (d_active * gate * sigmoid).astype(BF16)

    @pl.loop(0, w_gate_up.shape[0] // (2 * LANES))
    def _(step):
        at = columns_of(step, 2 * LANES)
        out = dot(d_gate_up[...], w_gate_up[at, :], ((1,), (1,)))
        own[:, at] = out[:kept]
        others[:, at] = out[kept:].astype(BF16)


def norm_backward(grad, source, gain):
    inverse = inverse_rms(source)
    scaled = grad * gain
    gain_grad = jnp.sum(grad * source * inverse, axis=0, keepdims=True)
    mean = jnp.mean(scaled * source, axis=-1, keepdims=True)
    return inverse * scaled - source * (inverse * inverse * inverse * mean), gain_grad


def attention_backward_kernel(
    d_result, d_mixed, d_rows, scatter, middle, hidden, gains, weights, cosine, sine, seg_col,
    seg_row, query, keys, values, log_total,
    d_hidden, d_branch, d_projected, gain_grads,
    bias, d_attended, d_normed,
):
    tokens, features = hidden.shape
    wide = 2 * LANES
    total = d_mixed[...] + dot(scatter[...], d_rows[...])
    d_middle, gain_grad = norm_backward(total, middle[...], gains[1:2])
    d_middle = d_middle + d_result[...]
    gain_grads[1:2] = gain_grad
    d_hidden[...] = d_middle
    d_branch[...] = d_middle.astype(BF16)
    bias[...] = attention_bias(seg_col, seg_row)

    @pl.loop(0, features // wide)
    def _(step):
        at = columns_of(step, wide)
        d_attended[:, at] = dot(d_branch[...], weights[3, at, :], ((1,), (1,))).astype(BF16)

    @pl.loop(0, features // LANES)
    def _(step):
        at = columns_of(step, LANES)
        q, k, v, da = query[:, at], keys[:, at], values[:, at], d_attended[:, at]
        lane = lax.broadcasted_iota(jnp.int32, log_total.shape, 1)
        zero = jnp.zeros((tokens, LANES), F32)
        dq, dk, dv = zero, zero, zero
        for half, mask in enumerate(head_masks(q.shape)):
            q_half, da_half = jnp.where(mask, q, 0), jnp.where(mask, da, 0)
            scores = dot(q_half, k, ((1,), (1,))) * SCALE + bias[...]
            shift = lane_pick(log_total[...], lane, step * (LANES // HEAD_DIM) + half)
            probs = jnp.exp(scores - shift)
            dv += dot(probs.astype(BF16), da_half, ((0,), (0,)))
            d_probs = dot(da_half, v, ((1,), (1,)))
            mean = jnp.sum(d_probs * probs, axis=-1, keepdims=True)
            d_scores = (probs * (d_probs - mean)).astype(BF16)
            dq += dot(d_scores, jnp.where(mask, k, 0))
            dk += dot(d_scores, q_half, ((0,), (0,)))
        d_projected[0, :, at] = turn(dq * SCALE, cosine[...], -sine[...]).astype(BF16)
        d_projected[1, :, at] = turn(dk * SCALE, cosine[...], -sine[...]).astype(BF16)
        d_projected[2, :, at] = dv.astype(BF16)

    @pl.loop(0, features // wide)
    def _(step):
        at = columns_of(step, wide)
        d_normed[:, at] = sum(
            dot(d_projected[b], weights[b, at, :], ((1,), (1,))) for b in range(3)
        )

    d_input, gain_grad = norm_backward(d_normed[...], hidden[...].astype(F32), gains[0:1])
    gain_grads[0:1] = gain_grad
    d_hidden[...] += d_input


def call(kernel, outs, args, scratch=(), megabytes=32):
    return pl.pallas_call(
        kernel,
        out_shape=[jax.ShapeDtypeStruct(shape, dtype) for shape, dtype in outs],
        scratch_shapes=[pltpu.VMEM(shape, dtype) for shape, dtype in scratch],
        compiler_params=pltpu.CompilerParams(vmem_limit_bytes=megabytes * 1024 * 1024),
    )(*args)


class Layout:
    def __init__(self, mesh):
        self.reps, self.shards = mesh.shape["rep"], mesh.shape["shard"]
        self.lines = self.shards // EF
        assert self.shards % EF == 0 and EF % self.reps == 0

    def pairs(self, move):
        found = []
        for rep in range(self.reps):
            for shard in range(self.shards):
                r, z, j = move(rep, shard // EF, shard % EF)
                found.append((rep * self.shards + shard, r * self.shards + z * EF + j))
        return found

    def send(self, x, move):
        return lax.ppermute(x, AXES, self.pairs(move))

    def expert_move(self, mask, shift):
        def move(r, z, j):
            number = r * EF + j
            e, f = (number // self.reps) ^ mask, (number % self.reps + shift) % self.reps
            number = e * self.reps + f
            return number // EF, z, number % EF

        return move

    def place(self):
        rep, shard = lax.axis_index("rep"), lax.axis_index("shard")
        j = shard % EF
        return rep, j, (rep * EF + j) // self.reps

    def quad_exchange(self, blocks, j):
        got = lax.dynamic_update_slice_in_dim(
            jnp.zeros_like(blocks), lax.dynamic_slice_in_dim(blocks, j, 1, 0), j, 0
        )
        for mask in range(1, EF):
            other = j ^ mask
            block = lax.dynamic_slice_in_dim(blocks, other, 1, 0)
            block = self.send(block, lambda r, z, q: (r, z, q ^ mask))
            got = lax.dynamic_update_slice_in_dim(got, block, other, 0)
        return got

    def part_exchange(self, blocks, j):
        count = EF // self.reps
        mine = j // self.reps
        got = lax.dynamic_update_slice_in_dim(
            jnp.zeros_like(blocks), lax.dynamic_slice_in_dim(blocks, mine, 1, 0), mine, 0
        )
        for mask in range(1, count):
            other = mine ^ mask
            block = lax.dynamic_slice_in_dim(blocks, other, 1, 0)
            block = self.send(block, lambda r, z, q: (r, z, q ^ (mask * self.reps)))
            got = lax.dynamic_update_slice_in_dim(got, block, other, 0)
        return got

    def rep_gather(self, x, rep):
        got = lax.dynamic_update_slice_in_dim(
            jnp.zeros((self.reps,) + x.shape, x.dtype), x[None], rep, 0
        )
        for shift in range(1, self.reps):
            block = self.send(x, lambda r, z, q: ((r + shift) % self.reps, z, q))
            got = lax.dynamic_update_slice_in_dim(
                got, block[None], (rep + self.reps - shift) % self.reps, 0
            )
        return got

    def line_groups(self):
        return [[z * EF + j for z in range(self.lines)] for j in range(EF)]

    def line_gather(self, x):
        return lax.all_gather(
            x, "shard", axis=0, tiled=True, axis_index_groups=self.line_groups()
        )

    def line_sum(self, x):
        return lax.psum_scatter(
            x, "shard", scatter_dimension=0, tiled=True, axis_index_groups=self.line_groups()
        )

    def dense_gather(self, x, rep, j):
        z = lax.axis_index("shard") // EF
        reps, lines = self.reps, self.lines
        line = lax.dynamic_update_slice_in_dim(
            jnp.zeros((lines,) + x.shape, x.dtype), x[None], z, 0
        )
        for shift in range(1, lines):
            block = self.send(x, lambda r, q, k: (r, (q + shift) % lines, k))
            line = lax.dynamic_update_slice_in_dim(
                line, block[None], (z + lines - shift) % lines, 0
            )
        cut = lines // 2
        high, core = j // 2, j % 2
        full = jnp.zeros((reps, lines, 2, 2) + x.shape, x.dtype)

        def put(full, block, r, at, hi, lo):
            return lax.dynamic_update_slice(full, block[None, :, None, None], (r, at, hi, lo, 0, 0))

        def over_rep(block, shift):
            return self.send(block, lambda r, q, k: ((r + shift) % reps, q, k))

        def over_high(block):
            return self.send(block, lambda r, q, k: (r, q, k ^ 2))

        sides = [(shift, over_rep(line, shift)) for shift in range(1, reps)]
        flip = over_high(line)
        full = put(full, line, rep, 0, high, core)
        full = put(full, flip, rep, 0, 1 - high, core)
        for shift, block in sides:
            source = (rep + reps - shift) % reps
            full = put(full, block, source, 0, high, core)
            full = put(full, over_high(block[:cut]), source, 0, 1 - high, core)
            full = put(full, over_rep(flip[cut:], shift), source, cut, 1 - high, core)
        half = lax.dynamic_slice_in_dim(full, core, 1, 3)
        half = self.send(half, lambda r, q, k: (r, q, k ^ 1))
        return lax.dynamic_update_slice_in_dim(full, half, 1 - core, 3)

    def dense_sum(self, parts, rep, j):
        z = lax.axis_index("shard") // EF
        reps, lines = self.reps, self.lines
        high, core = j // 2, j % 2

        def over_rep(block, shift):
            return self.send(block, lambda r, q, k: ((r + shift) % reps, q, k))

        def over_high(block):
            return self.send(block, lambda r, q, k: (r, q, k ^ 2))

        def rep_step(x):
            total = lax.dynamic_slice_in_dim(x, rep, 1, 0)[0].astype(F32)
            for shift in range(1, reps):
                block = lax.dynamic_slice_in_dim(x, (rep + shift) % reps, 1, 0)[0]
                total = total + over_rep(block, shift).astype(F32)
            return total.astype(BF16)

        def high_step(x, axis):
            mine = lax.dynamic_slice_in_dim(x, high, 1, axis)
            other = over_high(lax.dynamic_slice_in_dim(x, 1 - high, 1, axis))
            return jnp.squeeze(mine.astype(F32) + other.astype(F32), axis).astype(BF16)

        other = self.send(parts(1 - core), lambda r, q, k: (r, q, k ^ 1))
        both = (parts(core).astype(F32) + other.astype(F32)).astype(BF16)
        cut = lines // 2
        first = rep_step(high_step(both[:, :cut], 2))
        second = high_step(rep_step(both[:, cut:]), 1)
        line = jnp.concatenate([first, second])
        total = lax.dynamic_slice_in_dim(line, z, 1, 0)[0].astype(F32)
        for shift in range(1, lines):
            block = lax.dynamic_slice_in_dim(line, (z + shift) % lines, 1, 0)[0]
            block = self.send(block, lambda r, q, k: (r, (q + shift) % lines, k))
            total = total + block.astype(F32)
        return self.rep_gather(total.astype(BF16), rep)

    def dispatch(self, rows):
        blocks = rows.reshape(EF, CAP, -1)
        own = jnp.stack(
            [blocks[0]] + [self.send(blocks[m], self.expert_move(m, 0)) for m in range(1, EF)]
        )
        parts = [own] + [self.send(own, self.expert_move(0, g)) for g in range(1, self.reps)]
        return jnp.concatenate(parts).reshape(self.reps * EF * CAP, -1)

    def collect(self, own, others):
        total = own
        for g in range(1, self.reps):
            block = others[(g - 1) * EF * CAP : g * EF * CAP]
            total = total + self.send(block, self.expert_move(0, self.reps - g)).astype(F32)
        total = total.astype(BF16).reshape(EF, CAP, -1)
        return jnp.concatenate(
            [total[0]] + [self.send(total[m], self.expert_move(m, 0)) for m in range(1, EF)]
        )


def split_columns(array, layout):
    width = array.shape[-1] // (2 * layout.shards)
    return array.reshape(array.shape[:-1] + (2, layout.shards // layout.reps, layout.reps, width))


def expert_weights(layout, w_gate_up, w_down, rep, j):
    features = w_gate_up.shape[1]
    blocks = split_columns(w_gate_up, layout)
    blocks = jnp.transpose(blocks, (0, 4, 1, 2, 3, 5)).reshape(EF * layout.reps, features, -1)
    mine = lax.dynamic_slice_in_dim(blocks, rep * EF, EF, 0)
    mine = layout.quad_exchange(mine, j).reshape(EF * features, -1)
    gate_up = layout.line_gather(mine)
    count = EF // layout.reps
    down = lax.dynamic_slice_in_dim(w_down, rep * count, count, 0)
    down = layout.part_exchange(down, j).reshape(count * w_down.shape[1], -1)
    return gate_up, layout.line_gather(down)


def expert_grads(layout, grad_gate_up, grad_down, rep, j):
    down = layout.line_sum(grad_down)
    count = EF // layout.reps
    down = layout.part_exchange(down.reshape(count, -1, down.shape[-1]), j)
    down = layout.rep_gather(down, rep).reshape((EF,) + down.shape[1:]).astype(F32)
    mine = layout.line_sum(grad_gate_up)
    mine = layout.quad_exchange(mine.reshape(EF, -1, mine.shape[-1]), j)
    full = layout.rep_gather(mine, rep)
    features = mine.shape[1]
    full = full.reshape(EF, layout.reps, features, 2, layout.shards // layout.reps, -1)
    full = jnp.transpose(full, (0, 2, 3, 4, 1, 5)).reshape(EF, features, -1)
    return full.astype(F32), down


def place_pairs(routes, priority, expert):
    flat = routes.reshape(-1)
    ahead = (flat[:, None] == flat[None, :]) & (priority[:, None] < priority[None, :])
    position = jnp.sum(ahead.astype(jnp.int32), axis=0)
    kept = (flat < EF) & (position < CAP)
    slot = jnp.where(kept, (flat ^ expert) * CAP + position, EF * CAP).reshape(-1, TOP).T
    places = jnp.arange(EF * CAP, dtype=jnp.int32)
    gather = (places[None, :, None] == slot[:, None, :]).astype(BF16)
    scatter = (places[None, None, :] == slot[:, :, None]).astype(BF16)
    return gather, scatter


def attention_forward(shared, dense, hidden, previous, routes, gather):
    gains, weights, mixing = dense
    tokens, features = hidden.shape
    cosine, sine, seg_col, seg_row = shared
    low = ((tokens, features), BF16)
    lanes = ((tokens, LANES), F32)
    return call(
        attention_forward_kernel,
        [low, low, low, low, lanes, low, ((tokens, features), F32), low, lanes, lanes]
        + [((EF * CAP, features), BF16)],
        (hidden, gains, weights, cosine, sine, seg_col, seg_row, mixing, previous, routes)
        + (gather[0] + gather[1],),
        [((tokens, tokens), F32)],
    )


def expert_forward(layout, inputs, w_gate_up, w_down):
    count, features = inputs.shape
    units = w_down.shape[0]
    return call(
        expert_forward_kernel,
        [((count, 2 * units), F32), ((count, units), BF16)]
        + [((EF * CAP, features), F32), ((count - EF * CAP, features), BF16)],
        (inputs, w_gate_up, w_down),
    )


def expert_backward(layout, d_expert, w_gate_up, w_down, gate_up):
    count, features = d_expert.shape
    units = w_down.shape[0]
    return call(
        expert_backward_kernel,
        [((count, 2 * units), BF16)]
        + [((EF * CAP, features), F32), ((count - EF * CAP, features), BF16)],
        (d_expert, w_gate_up, w_down, gate_up),
    )


def local(
    layout,
    hidden_in,
    gate_in,
    routes,
    priority,
    segments,
    norm_attn,
    w_qkv,
    w_out,
    norm_moe,
    w_router,
    w_const,
    const_vec,
    w_gate_up,
    w_down,
    grad_out,
):
    layers = w_qkv.shape[0]
    tokens, features = hidden_in.shape
    rep, j, expert = layout.place()
    slim = w_qkv.shape[1]
    small = [
        jnp.concatenate(
            [norm_attn[l][:, None], norm_moe[l][:, None], w_router[l], w_const[l], const_vec[l].T],
            axis=-1,
        ).reshape(1, -1)
        for l in range(layers)
    ]
    small = jnp.concatenate(small, axis=-1)
    extra = ROWS * features
    small = jnp.pad(small, ((0, 0), (0, extra - small.shape[1]))).reshape(ROWS, features)
    count = EF // layout.reps
    dense, moe = [], []
    small_full = None
    for l in range(layers):
        blocks = jnp.concatenate(
            [jnp.transpose(w_qkv[l].reshape(slim, 3, features), (1, 0, 2)), w_out[l][None]]
        )
        mine = lax.dynamic_slice_in_dim(blocks, rep * count, count, 0).reshape(count * slim, features)
        if l == 0:
            mine = jnp.concatenate([mine, small])
        full = layout.dense_gather(mine, rep, j)
        if l == 0:
            small_full = full[0, :, :, :, count * slim :].reshape(layout.shards, -1)
        full = full[:, :, :, :, : count * slim].reshape(
            layout.reps, layout.shards, count, slim, features
        )
        dense.append(jnp.transpose(full, (0, 2, 1, 3, 4)).reshape(4, features, features))
        moe.append(expert_weights(layout, w_gate_up[l], w_down[l], rep, j))
    packs, vectors, mixing_t = [], [], []
    for l in range(layers):
        part = small_full[:, l * slim * SMALL : (l + 1) * slim * SMALL]
        part = part.reshape(features, SMALL)
        mixing = part[:, 2 : SMALL - NCONST]
        mixing = jnp.pad(mixing, ((0, 0), (0, LANES - mixing.shape[1])))
        packs.append((part[:, :2].T.astype(F32), dense[l], mixing))
        mixing_t.append(mixing.T)
        vectors.append(part[:, SMALL - NCONST :].T.astype(F32))

    shared = (*rope_tables(tokens), segments.reshape(-1, 1), segments)
    pairs = [place_pairs(routes[l], priority[l, 0], expert) for l in range(layers)]

    hidden = hidden_in
    previous = jnp.pad(gate_in, ((0, 0), (0, LANES - EXPERTS)))
    kept = []
    for l in range(layers):
        gather, scatter = pairs[l]
        state = attention_forward(shared, packs[l], hidden, previous, routes[l], gather)
        normed, query, keys, values, log_total, attended, middle, low, logits, coefs, rows = state
        inputs = layout.dispatch(rows)
        gate_up, activated, own, others = expert_forward(layout, inputs, *moe[l])
        outputs = layout.collect(own, others)
        (result,) = call(
            combine_kernel,
            [((tokens, features), F32)],
            (coefs, middle, packs[l][0], scatter, outputs, vectors[l]),
        )
        kept.append((hidden, state, inputs, gate_up, activated, outputs))
        hidden, previous = result, logits

    grad_hidden = grad_out
    grad_gate = jnp.zeros_like(previous)
    dense_grads, moe_grads = [None] * layers, [None] * layers
    for l in reversed(range(layers)):
        gather, scatter = pairs[l]
        source, state, inputs, gate_up, activated, outputs = kept[l]
        normed, query, keys, values, log_total, attended, middle, low, logits, coefs, _ = state
        (rows,) = call(
            value_rows_kernel,
            [((EF * CAP, features), BF16)],
            (coefs, gather, grad_hidden),
        )
        d_expert = layout.dispatch(rows)
        grad_gate, d_mixed, mix_grads = call(
            gate_backward_kernel,
            [((tokens, LANES), F32), ((tokens, features), F32), ((SMALL - 2, features), F32)],
            (coefs, middle, packs[l][0], scatter, outputs, vectors[l], routes[l], low)
            + (mixing_t[l], grad_hidden, grad_gate),
        )
        grad_down = dot(activated, d_expert, ((0,), (0,))).astype(BF16)
        d_gate_up, own, others = expert_backward(layout, d_expert, *moe[l], gate_up)
        d_rows = layout.collect(own, others)
        grad_gate_up = dot(inputs, d_gate_up, ((0,), (0,))).astype(BF16)
        moe_grads[l] = expert_grads(layout, grad_gate_up, grad_down, rep, j)
        grad_hidden, d_branch, d_projected, gain_grads = call(
            attention_backward_kernel,
            [((tokens, features), F32), ((tokens, features), BF16)]
            + [((3, tokens, features), BF16), ((2, features), F32)],
            (grad_hidden, d_mixed, d_rows, scatter[0] + scatter[1], middle, source)
            + (packs[l][0], packs[l][1], *shared, query, keys, values, log_total),
            [((tokens, tokens), F32), ((tokens, features), BF16), ((tokens, features), F32)],
        )
        grad_dense = jnp.stack(
            [dot(normed, d_projected[b], ((0,), (0,))).astype(BF16) for b in range(3)]
            + [dot(attended, d_branch, ((0,), (0,))).astype(BF16)]
        )
        small_grads = jnp.concatenate([gain_grads, mix_grads]).T.astype(BF16)
        lines = layout.lines
        blocks = grad_dense.reshape(layout.reps, count, lines, 2, 2, slim, features)
        small_grads = small_grads.reshape(lines, 2, 2, slim * SMALL)
        small_grads = jnp.pad(
            small_grads, ((0, 0),) * 3 + ((0, ROWS * features - slim * SMALL),)
        ).reshape(lines, 2, 2, ROWS, features)

        def parts(c):
            chosen = lax.dynamic_slice_in_dim(blocks, c, 1, 4)[:, :, :, :, 0]
            chosen = jnp.transpose(chosen, (0, 2, 3, 1, 4, 5)).reshape(
                layout.reps, lines, 2, count * slim, features
            )
            extra = lax.dynamic_slice_in_dim(small_grads, c, 1, 2)[:, :, 0]
            extra = jnp.broadcast_to(extra[None], (layout.reps,) + extra.shape)
            return jnp.concatenate([chosen, extra], axis=3)

        dense_grads[l] = layout.dense_sum(parts, rep, j)

    dense_all = jnp.stack(dense_grads).astype(F32)
    small_all = dense_all[:, 0, count * slim :].reshape(layers, -1)[:, : slim * SMALL]
    small_all = small_all.reshape(layers, slim, SMALL)
    dense_all = dense_all[:, :, : count * slim].reshape(layers, 4, slim, features)
    qkv_all = jnp.transpose(dense_all[:, :3], (0, 2, 1, 3)).reshape(layers, slim, 3 * features)
    return (
        hidden.astype(BF16),
        grad_hidden,
        grad_gate[:, :EXPERTS],
        small_all[:, :, 0],
        qkv_all,
        dense_all[:, 3],
        small_all[:, :, 1],
        small_all[:, :, 2 : 2 + EXPERTS],
        small_all[:, :, 2 + EXPERTS : SMALL - NCONST],
        jnp.transpose(small_all[:, :, SMALL - NCONST :], (0, 2, 1)),
        jnp.stack([g[0] for g in moe_grads]),
        jnp.stack([g[1] for g in moe_grads]),
    )


def solution(mesh):
    return jax.shard_map(
        functools.partial(local, Layout(mesh)),
        mesh=mesh,
        in_specs=(
            P(("rep", "shard"), None),
            P(("rep", "shard"), None),
            P(None, ("rep", "shard"), None),
            P(None, ("rep", "shard"), None),
            P(("rep", "shard"), None),
            P(None, "shard"),
            P(None, "shard", None),
            P(None, "shard", None),
            P(None, "shard"),
            P(None, "shard", None),
            P(None, "shard", None),
            P(None, None, "shard"),
            P(None, None, "shard", None),
            P(None, None, "shard", None),
            P(("rep", "shard"), None),
        ),
        out_specs=(
            P(("rep", "shard"), None),
            P(("rep", "shard"), None),
            P(("rep", "shard"), None),
            P(None, "shard"),
            P(None, "shard", None),
            P(None, "shard", None),
            P(None, "shard"),
            P(None, "shard", None),
            P(None, "shard", None),
            P(None, None, "shard"),
            P(None, None, "shard", None),
            P(None, None, "shard", None),
        ),
        check_vma=False,
    )
```

```python
import functools
import math

import jax
import jax.numpy as jnp
from jax import lax
from jax.experimental import pallas as pl
from jax.experimental.pallas import tpu as pltpu
from jax.sharding import PartitionSpec as P

HEAD_DIM = 64
EF = 4
NCONST = 2
TOP = 2
EXPERTS = 8
CAP = 80
SMALL = 2 + EXPERTS + 2 * NCONST + NCONST
ROWS = 16
LANES = 128

EPSILON = 1e-06
SCALE = 0.125
MASKED = -1000000000.0
AXES = ("rep", "shard")
BF16 = jnp.bfloat16
F32 = jnp.float32


def dot(a, b, dims=((1,), (0,))):
    return lax.dot_general(a, b, (dims, ((), ())), preferred_element_type=F32)


def rope_tables(tokens):
    half = HEAD_DIM // 2
    places = jnp.arange(tokens, dtype=jnp.int32).astype(F32)[:, None]
    powers = jnp.arange(half, dtype=jnp.int32).astype(F32) / half
    angles = places * jnp.exp(-math.log(10000.0) * powers)[None, :]
    cosine, sine = jnp.cos(angles), jnp.sin(angles)
    heads = LANES // HEAD_DIM
    return jnp.tile(cosine, (1, 2 * heads)), jnp.tile(
        jnp.concatenate([-sine, sine], axis=-1), (1, heads)
    )


def turn(block, cosine, sine):
    half = HEAD_DIM // 2
    lane = lax.broadcasted_iota(jnp.int32, block.shape, 1)
    width = block.shape[1]
    partner = jnp.where(
        lane % HEAD_DIM < half,
        pltpu.roll(block, width - half, 1),
        pltpu.roll(block, half, 1),
    )
    return block * cosine + partner * sine


def lane_pick(array, lane, index):
    return jnp.sum(jnp.where(lane == index, array, 0.0), axis=-1, keepdims=True)


def inverse_rms(x):
    return lax.rsqrt(jnp.mean(x * x, axis=-1, keepdims=True) + EPSILON)


def attention_bias(seg_col, seg_row):
    shape = (seg_col.shape[0], seg_row.shape[1])
    rows = lax.broadcasted_iota(jnp.int32, shape, 0)
    columns = lax.broadcasted_iota(jnp.int32, shape, 1)
    allowed = (seg_col[...] == seg_row[...]) & (columns <= rows)
    return jnp.where(allowed, 0.0, MASKED)


def head_masks(shape):
    lane = lax.broadcasted_iota(jnp.int32, shape, 1)
    return [(lane // HEAD_DIM) == half for half in range(LANES // HEAD_DIM)]


def columns_of(step, width):
    return pl.ds(pl.multiple_of(step * width, width), width)


def attention_forward_kernel(
    hidden, gains, weights, cosine, sine, seg_col, seg_row, mixing, previous, routes, gather,
    normed, query, keys, values, log_total, attended, middle, mixed_low, logits, coefs, rows,
    bias,
):
    tokens, features = hidden.shape
    h = hidden[...].astype(F32)
    normed[...] = (h * inverse_rms(h) * gains[0:1]).astype(BF16)
    bias[...] = attention_bias(seg_col, seg_row)
    wide = 2 * LANES
    for block, out in ((0, query), (1, keys)):

        @pl.loop(0, features // wide)
        def _(step):
            part = dot(normed[...], weights[block, :, columns_of(step, wide)])
            for k in range(2):
                turned = turn(part[:, k * LANES : (k + 1) * LANES], cosine[...], sine[...])
                out[:, columns_of(2 * step + k, LANES)] = turned.astype(BF16)

    @pl.loop(0, features // wide)
    def _(step):
        at = columns_of(step, wide)
        values[:, at] = dot(normed[...], weights[2, :, at]).astype(BF16)

    log_total[...] = jnp.zeros_like(log_total)

    @pl.loop(0, features // LANES)
    def _(step):
        at = columns_of(step, LANES)
        q, k, v = query[:, at], keys[:, at], values[:, at]
        lane = lax.broadcasted_iota(jnp.int32, log_total.shape, 1)
        total_out = jnp.zeros((tokens, LANES), F32)
        for half, mask in enumerate(head_masks(q.shape)):
            scores = dot(jnp.where(mask, q, 0), k, ((1,), (1,))) * SCALE + bias[...]
            top = jnp.max(scores, axis=-1, keepdims=True)
            weight = jnp.exp(scores - top)
            total = jnp.sum(weight, axis=-1, keepdims=True)
            probs = (weight * (1.0 / total)).astype(BF16)
            total_out += dot(probs, jnp.where(mask, v, 0))
            log_total[...] = jnp.where(
                lane == step * (LANES // HEAD_DIM) + half, top + jnp.log(total), log_total[...]
            )
        attended[:, at] = total_out.astype(BF16)

    @pl.loop(0, features // wide)
    def _(step):
        at = columns_of(step, wide)
        middle[:, at] = hidden[:, at].astype(F32) + dot(attended[...], weights[3, :, at])

    m = middle[...]
    low = (m * inverse_rms(m) * gains[1:2]).astype(BF16)
    mixed_low[...] = low
    rows[...] = dot(gather[...], low).astype(BF16)
    raw = dot(low, mixing[...])
    lane = lax.broadcasted_iota(jnp.int32, raw.shape, 1)
    now = jnp.where(lane < EXPERTS, raw + previous[...], 0.0)
    logits[...] = now
    route = [routes[:, k : k + 1] for k in range(TOP)]
    chosen = [lane_pick(now, lane, route[k]) for k in range(TOP)]
    best = jnp.maximum(chosen[0], chosen[1])
    chosen = [jnp.exp(c - best) for c in chosen]
    gates = [c / (chosen[0] + chosen[1]) for c in chosen]
    shares = []
    for c in range(NCONST):
        pair = [lane_pick(raw, lane, EXPERTS + 2 * c + i) for i in range(2)]
        best = jnp.maximum(pair[0], pair[1])
        pair = [jnp.exp(p - best) for p in pair]
        shares.append([p / (pair[0] + pair[1]) for p in pair])
    copies = [(route[k] == EF + 1).astype(F32) for k in range(TOP)]
    consts = [[(route[k] == EF + 2 + c).astype(F32) for c in range(NCONST)] for k in range(TOP)]
    weight = [sum(consts[k][c] * gates[k] for k in range(TOP)) for c in range(NCONST)]
    columns = list(gates)
    columns += [
        copies[k] + sum(consts[k][c] * shares[c][0] for c in range(NCONST)) for k in range(TOP)
    ]
    columns += [consts[k][c] * shares[c][1] for k in range(TOP) for c in range(NCONST)]
    columns += [shares[c][i] for c in range(NCONST) for i in range(2)]
    columns += weight
    columns += [
        sum(copies[k] * gates[k] for k in range(TOP))
        + sum(shares[c][0] * weight[c] for c in range(NCONST))
    ]
    columns += [shares[c][1] * weight[c] for c in range(NCONST)]
    packed = jnp.zeros_like(raw)
    for index, column in enumerate(columns):
        packed = jnp.where(lane == index, column, packed)
    coefs[...] = packed


GATE, MIXED, VECTOR, SHARE, WEIGHT, DIRECT, CONST = 0, 2, 4, 8, 12, 14, 15


def combine_kernel(coefs, middle, gains, scatter, outputs, vectors, result):
    coef = coefs[...]
    m = middle[...]
    total = m + coef[:, DIRECT : DIRECT + 1] * (m * inverse_rms(m) * gains[1:2])
    for k in range(TOP):
        total += coef[:, GATE + k : GATE + k + 1] * dot(scatter[k], outputs[...])
    for c in range(NCONST):
        total += coef[:, CONST + c : CONST + c + 1] * vectors[c : c + 1]
    result[...] = total


def value_rows_kernel(coefs, gather, d_result, rows):
    coef = coefs[...]
    rows[...] = sum(
        dot(gather[k], (coef[:, GATE + k : GATE + k + 1] * d_result[...]).astype(BF16))
        for k in range(TOP)
    ).astype(BF16)


def two_parts(x):
    high = x.astype(BF16)
    return high, (x - high.astype(F32)).astype(BF16)


def gate_backward_kernel(
    coefs, middle, gains, scatter, outputs, vectors, routes, mixed_low, mixing_t, d_result, d_next,
    d_logits, d_mixed, grads,
):
    coef = coefs[...]
    m = middle[...]
    dh = d_result[...]
    lane = lax.broadcasted_iota(jnp.int32, coef.shape, 1)

    def column(index):
        return coef[:, index : index + 1]

    along = jnp.sum(m * inverse_rms(m) * gains[1:2] * dh, axis=-1, keepdims=True)
    with_vector = [
        jnp.sum(dh * vectors[c : c + 1], axis=-1, keepdims=True) for c in range(NCONST)
    ]
    d_gates = []
    for k in range(TOP):
        value = jnp.sum(dot(scatter[k], outputs[...]) * dh, axis=-1, keepdims=True)
        value += column(MIXED + k) * along
        value += sum(column(VECTOR + k * NCONST + c) * with_vector[c] for c in range(NCONST))
        d_gates.append(value)
    mean = sum(column(GATE + k) * d_gates[k] for k in range(TOP))
    terms = d_next[...]
    for k in range(TOP):
        chosen = column(GATE + k) * (d_gates[k] - mean)
        terms += jnp.where(lane == routes[:, k : k + 1], chosen, 0.0)
    d_logits[...] = terms
    vector_terms = jnp.zeros_like(terms)
    for c in range(NCONST):
        share = [column(SHARE + 2 * c + i) for i in range(2)]
        d_share = [column(WEIGHT + c) * along, column(WEIGHT + c) * with_vector[c]]
        mean = share[0] * d_share[0] + share[1] * d_share[1]
        for i in range(2):
            terms = jnp.where(
                lane == EXPERTS + 2 * c + i, share[i] * (d_share[i] - mean), terms
            )
        vector_terms = jnp.where(
            lane == EXPERTS + 2 * NCONST + c, column(CONST + c), vector_terms
        )
    high, lowest = two_parts(terms)
    d_mixed[...] = column(DIRECT) * dh + dot(high, mixing_t[...]) + dot(lowest, mixing_t[...])
    both = ((0,), (0,))
    total = dot(high, mixed_low[...], both) + dot(lowest, mixed_low[...], both)
    high, lowest = two_parts(vector_terms)
    dh_high, dh_low = two_parts(dh)
    total += dot(high, dh_high, both) + dot(lowest, dh_high, both) + dot(high, dh_low, both)
    grads[...] = total[: grads.shape[0]]


def expert_forward_kernel(inputs, w_gate_up, w_down, gate_up, activated, own, others):
    units = w_down.shape[0]
    wide = min(2 * LANES, units)
    kept = own.shape[0]

    @pl.loop(0, units // wide)
    def _(step):
        at = columns_of(step, wide)
        gate = dot(inputs[...], w_gate_up[:, at])
        up_at = pl.ds(pl.multiple_of(units + step * wide, wide), wide)
        up = dot(inputs[...], w_gate_up[:, up_at])
        gate_up[:, at] = gate
        gate_up[:, up_at] = up
        activated[:, at] = (gate / (1.0 + jnp.exp(-gate)) * up).astype(BF16)

    @pl.loop(0, w_down.shape[1] // (2 * LANES))
    def _(step):
        at = columns_of(step, 2 * LANES)
        out = dot(activated[...], w_down[:, at])
        own[:, at] = out[:kept]
        others[:, at] = out[kept:].astype(BF16)


def expert_backward_kernel(d_expert, w_gate_up, w_down, gate_up, d_gate_up, own, others):
    units = w_down.shape[0]
    wide = min(2 * LANES, units)
    kept = own.shape[0]

    @pl.loop(0, units // wide)
    def _(step):
        at = columns_of(step, wide)
        up_at = pl.ds(pl.multiple_of(units + step * wide, wide), wide)
        d_active = dot(d_expert[...], w_down[at, :], ((1,), (1,)))
        gate, up = gate_up[:, at], gate_up[:, up_at]
        sigmoid = 1.0 / (1.0 + jnp.exp(-gate))
        d_gate_up[:, at] = (
            d_active * up * sigmoid * (1.0 + gate * (1.0 - sigmoid))
        ).astype(BF16)
        d_gate_up[:, up_at] = (d_active * gate * sigmoid).astype(BF16)

    @pl.loop(0, w_gate_up.shape[0] // (2 * LANES))
    def _(step):
        at = columns_of(step, 2 * LANES)
        out = dot(d_gate_up[...], w_gate_up[at, :], ((1,), (1,)))
        own[:, at] = out[:kept]
        others[:, at] = out[kept:].astype(BF16)


def norm_backward(grad, source, gain):
    inverse = inverse_rms(source)
    scaled = grad * gain
    gain_grad = jnp.sum(grad * source * inverse, axis=0, keepdims=True)
    mean = jnp.mean(scaled * source, axis=-1, keepdims=True)
    return inverse * scaled - source * (inverse * inverse * inverse * mean), gain_grad


def attention_backward_kernel(
    d_result, d_mixed, d_rows, scatter, middle, hidden, gains, weights, cosine, sine, seg_col,
    seg_row, query, keys, values, log_total,
    d_hidden, d_branch, d_projected, gain_grads,
    bias, d_attended, d_normed,
):
    tokens, features = hidden.shape
    wide = 2 * LANES
    total = d_mixed[...] + dot(scatter[...], d_rows[...])
    d_middle, gain_grad = norm_backward(total, middle[...], gains[1:2])
    d_middle = d_middle + d_result[...]
    gain_grads[1:2] = gain_grad
    d_hidden[...] = d_middle
    d_branch[...] = d_middle.astype(BF16)
    bias[...] = attention_bias(seg_col, seg_row)

    @pl.loop(0, features // wide)
    def _(step):
        at = columns_of(step, wide)
        d_attended[:, at] = dot(d_branch[...], weights[3, at, :], ((1,), (1,))).astype(BF16)

    @pl.loop(0, features // LANES)
    def _(step):
        at = columns_of(step, LANES)
        q, k, v, da = query[:, at], keys[:, at], values[:, at], d_attended[:, at]
        lane = lax.broadcasted_iota(jnp.int32, log_total.shape, 1)
        zero = jnp.zeros((tokens, LANES), F32)
        dq, dk, dv = zero, zero, zero
        for half, mask in enumerate(head_masks(q.shape)):
            q_half, da_half = jnp.where(mask, q, 0), jnp.where(mask, da, 0)
            scores = dot(q_half, k, ((1,), (1,))) * SCALE + bias[...]
            shift = lane_pick(log_total[...], lane, step * (LANES // HEAD_DIM) + half)
            probs = jnp.exp(scores - shift)
            dv += dot(probs.astype(BF16), da_half, ((0,), (0,)))
            d_probs = dot(da_half, v, ((1,), (1,)))
            mean = jnp.sum(d_probs * probs, axis=-1, keepdims=True)
            d_scores = (probs * (d_probs - mean)).astype(BF16)
            dq += dot(d_scores, jnp.where(mask, k, 0))
            dk += dot(d_scores, q_half, ((0,), (0,)))
        d_projected[0, :, at] = turn(dq * SCALE, cosine[...], -sine[...]).astype(BF16)
        d_projected[1, :, at] = turn(dk * SCALE, cosine[...], -sine[...]).astype(BF16)
        d_projected[2, :, at] = dv.astype(BF16)

    @pl.loop(0, features // wide)
    def _(step):
        at = columns_of(step, wide)
        d_normed[:, at] = sum(
            dot(d_projected[b], weights[b, at, :], ((1,), (1,))) for b in range(3)
        )

    d_input, gain_grad = norm_backward(d_normed[...], hidden[...].astype(F32), gains[0:1])
    gain_grads[0:1] = gain_grad
    d_hidden[...] += d_input


def call(kernel, outs, args, scratch=(), megabytes=32):
    return pl.pallas_call(
        kernel,
        out_shape=[jax.ShapeDtypeStruct(shape, dtype) for shape, dtype in outs],
        scratch_shapes=[pltpu.VMEM(shape, dtype) for shape, dtype in scratch],
        compiler_params=pltpu.CompilerParams(vmem_limit_bytes=megabytes * 1024 * 1024),
    )(*args)


def after(x, *others):
    return lax.optimization_barrier((x,) + others)[0]


class Layout:
    def __init__(self, mesh):
        self.reps, self.shards = mesh.shape["rep"], mesh.shape["shard"]
        self.lines = self.shards // EF
        assert self.shards % EF == 0 and EF % self.reps == 0

    def pairs(self, move):
        found = []
        for rep in range(self.reps):
            for shard in range(self.shards):
                r, z, j = move(rep, shard // EF, shard % EF)
                found.append((rep * self.shards + shard, r * self.shards + z * EF + j))
        return found

    def send(self, x, move):
        return lax.ppermute(x, AXES, self.pairs(move))

    def expert_move(self, mask, shift):
        def move(r, z, j):
            number = r * EF + j
            e, f = (number // self.reps) ^ mask, (number % self.reps + shift) % self.reps
            number = e * self.reps + f
            return number // EF, z, number % EF

        return move

    def place(self):
        rep, shard = lax.axis_index("rep"), lax.axis_index("shard")
        j = shard % EF
        return rep, j, (rep * EF + j) // self.reps

    def quad_exchange(self, blocks, j):
        got = lax.dynamic_update_slice_in_dim(
            jnp.zeros_like(blocks), lax.dynamic_slice_in_dim(blocks, j, 1, 0), j, 0
        )
        for mask in range(1, EF):
            other = j ^ mask
            block = lax.dynamic_slice_in_dim(blocks, other, 1, 0)
            block = self.send(block, lambda r, z, q: (r, z, q ^ mask))
            got = lax.dynamic_update_slice_in_dim(got, block, other, 0)
        return got

    def part_exchange(self, blocks, j):
        count = EF // self.reps
        mine = j // self.reps
        got = lax.dynamic_update_slice_in_dim(
            jnp.zeros_like(blocks), lax.dynamic_slice_in_dim(blocks, mine, 1, 0), mine, 0
        )
        for mask in range(1, count):
            other = mine ^ mask
            block = lax.dynamic_slice_in_dim(blocks, other, 1, 0)
            block = self.send(block, lambda r, z, q: (r, z, q ^ (mask * self.reps)))
            got = lax.dynamic_update_slice_in_dim(got, block, other, 0)
        return got

    def rep_gather(self, x, rep):
        got = lax.dynamic_update_slice_in_dim(
            jnp.zeros((self.reps,) + x.shape, x.dtype), x[None], rep, 0
        )
        for shift in range(1, self.reps):
            block = self.send(x, lambda r, z, q: ((r + shift) % self.reps, z, q))
            got = lax.dynamic_update_slice_in_dim(
                got, block[None], (rep + self.reps - shift) % self.reps, 0
            )
        return got

    def line_groups(self):
        return [[z * EF + j for z in range(self.lines)] for j in range(EF)]

    def line_gather(self, x):
        return lax.all_gather(
            x, "shard", axis=0, tiled=True, axis_index_groups=self.line_groups()
        )

    def line_sum(self, x):
        return lax.psum_scatter(
            x, "shard", scatter_dimension=0, tiled=True, axis_index_groups=self.line_groups()
        )

    def dense_gather(self, x):
        reps, lines = self.reps, self.lines
        line = [x[None]]
        for shift in range(1, lines):
            line.append(self.send(x, lambda r, q, k: (r, (q + shift) % lines, k))[None])
        line = jnp.concatenate(line)
        cut = lines // 2

        def over_rep(block, shift):
            return self.send(block, lambda r, q, k: ((r + shift) % reps, q, k))

        def over_high(block):
            return self.send(block, lambda r, q, k: (r, q, k ^ 2))

        sides = [over_rep(line, shift) for shift in range(1, reps)]
        flip = over_high(line)
        pieces = [(line, 0, 0, 0), (flip, 0, 0, 1)]
        for shift, block in enumerate(sides, 1):
            pieces.append((block, 0, shift, 0))
            pieces.append((over_high(block[:cut]), 0, shift, 1))
            pieces.append((over_rep(flip[cut:], shift), cut, shift, 1))
        pieces = [piece + (0,) for piece in pieces if piece[0].shape[0]]
        others = [
            (self.send(piece[0], lambda r, q, k: (r, q, k ^ 1)),) + piece[1:4] + (1,)
            for piece in pieces
        ]
        return pieces + others

    def assemble(self, pieces, where, count):
        reps, lines = self.reps, self.lines
        rows, features = pieces[0][0].shape[1:]
        slim = features // self.shards
        extra = rows - count * slim
        notes = [piece[1:] for piece in pieces]

        def kernel(where_ref, *refs):
            out = refs[len(pieces)]
            rep, z, high, core = [where_ref[k] for k in range(4)]
            for ref, (start, back, flip, other) in zip(refs, notes):
                r = lax.rem(rep + reps - back, reps)
                hi = high if flip == 0 else 1 - high
                lo = core if other == 0 else 1 - core
                for step in range(ref.shape[0]):
                    at = lax.rem(z + lines - start - step, lines)
                    for k in range(count):
                        out[r, k, at, hi, lo] = ref[step, k * slim : (k + 1) * slim]
                    if extra and back == 0:
                        refs[-1][at, hi, lo] = ref[step, count * slim :]

        shapes = [jax.ShapeDtypeStruct((reps, count, lines, 2, 2, slim, features), BF16)]
        if extra:
            shapes.append(jax.ShapeDtypeStruct((lines, 2, 2, extra, features), BF16))
        return pl.pallas_call(
            kernel,
            out_shape=shapes,
            in_specs=[pl.BlockSpec(memory_space=pltpu.SMEM)]
            + [pl.BlockSpec(memory_space=pltpu.VMEM)] * len(pieces),
            out_specs=[pl.BlockSpec(memory_space=pltpu.VMEM)] * len(shapes),
            compiler_params=pltpu.CompilerParams(vmem_limit_bytes=32 * 1024 * 1024),
        )(where, *[piece[0] for piece in pieces])

    def over_rep(self, block, shift):
        return self.send(block, lambda r, q, k: ((r + shift) % self.reps, q, k))

    def sum_core(self, parts, j):
        core = j % 2
        other = self.send(parts(1 - core), lambda r, q, k: (r, q, k ^ 1))
        return (parts(core).astype(F32) + other.astype(F32)).astype(BF16)

    def sum_cross(self, both, rep, j):
        high = j // 2

        def rep_step(x):
            total = lax.dynamic_slice_in_dim(x, rep, 1, 0)[0].astype(F32)
            for shift in range(1, self.reps):
                block = lax.dynamic_slice_in_dim(x, (rep + shift) % self.reps, 1, 0)[0]
                total = total + self.over_rep(block, shift).astype(F32)
            return total.astype(BF16)

        def high_step(x, axis):
            mine = lax.dynamic_slice_in_dim(x, high, 1, axis)
            other = lax.dynamic_slice_in_dim(x, 1 - high, 1, axis)
            other = self.send(other, lambda r, q, k: (r, q, k ^ 2))
            return jnp.squeeze(mine.astype(F32) + other.astype(F32), axis).astype(BF16)

        cut = self.lines // 2
        first = rep_step(high_step(both[:, :cut], 2))
        second = high_step(rep_step(both[:, cut:]), 1)
        return jnp.concatenate([first, second])

    def sum_line(self, line, rep):
        z = lax.axis_index("shard") // EF
        lines = self.lines
        total = lax.dynamic_slice_in_dim(line, z, 1, 0)[0].astype(F32)
        for shift in range(1, lines):
            block = lax.dynamic_slice_in_dim(line, (z + shift) % lines, 1, 0)[0]
            block = self.send(block, lambda r, q, k: (r, (q + shift) % lines, k))
            total = total + block.astype(F32)
        return self.rep_gather(total.astype(BF16), rep)

    def dispatch(self, rows):
        blocks = rows.reshape(EF, CAP, -1)
        own = jnp.stack(
            [blocks[0]] + [self.send(blocks[m], self.expert_move(m, 0)) for m in range(1, EF)]
        )
        parts = [own] + [self.send(own, self.expert_move(0, g)) for g in range(1, self.reps)]
        return jnp.concatenate(parts).reshape(self.reps * EF * CAP, -1)

    def collect(self, own, others):
        total = own
        for g in range(1, self.reps):
            block = others[(g - 1) * EF * CAP : g * EF * CAP]
            total = total + self.send(block, self.expert_move(0, self.reps - g)).astype(F32)
        total = total.astype(BF16).reshape(EF, CAP, -1)
        return jnp.concatenate(
            [total[0]] + [self.send(total[m], self.expert_move(m, 0)) for m in range(1, EF)]
        )


def split_gate_up(layout, w_gate_up, layer, where):
    _, experts, rows, columns = w_gate_up.shape
    width = columns // (2 * layout.shards)
    parts = layout.reps
    per = layout.shards // parts

    def kernel(where_ref, x, o):
        for j in range(EF):
            e = where_ref[0] * (EF // layout.reps) + j // parts
            for b in range(2 * per):
                at = (b * parts + j % parts) * width
                o[j, :, b * width : (b + 1) * width] = x[0, e, :, at : at + width]

    return pl.pallas_call(
        kernel,
        grid=(1,),
        out_shape=jax.ShapeDtypeStruct((EF, rows, columns // parts), BF16),
        in_specs=[
            pl.BlockSpec(memory_space=pltpu.SMEM),
            pl.BlockSpec((1, experts, rows, columns), lambda _: (layer, 0, 0, 0)),
        ],
        out_specs=pl.BlockSpec((EF, rows, columns // parts), lambda _: (0, 0, 0)),
        compiler_params=pltpu.CompilerParams(vmem_limit_bytes=32 * 1024 * 1024),
    )(where, w_gate_up)


def expert_weights(layout, w_gate_up, w_down, layer, rep, j, where):
    count = EF // layout.reps
    mine = layout.quad_exchange(split_gate_up(layout, w_gate_up, layer, where), j)
    mine = mine.reshape(-1, mine.shape[-1])
    down = lax.dynamic_slice_in_dim(after(w_down[layer], mine), rep * count, count, 0)
    down = layout.part_exchange(down, j)
    down = down.reshape(-1, down.shape[-1])
    return layout.line_gather(mine), layout.line_gather(down), down


def place_down(layout, down, rep, j):
    down = layout.part_exchange(down.reshape(EF // layout.reps, -1, down.shape[-1]), j)
    return layout.rep_gather(down, rep).reshape((1, EF) + down.shape[1:])


def place_gate_up(layout, mine, rep, j):
    mine = layout.quad_exchange(mine.reshape(EF, -1, mine.shape[-1]), j)
    return layout.rep_gather(mine, rep).reshape((EF, layout.reps) + mine.shape[1:])


def store_layer(kernel, source, block, index, shape, layer, held):
    spec = pl.BlockSpec((1, 1) + shape[2:], lambda e: (layer, e) + (0,) * (len(shape) - 2))
    whole = [] if held is None else [held]
    return pl.pallas_call(
        (lambda x, o: kernel(x, o)) if held is None else (lambda x, h, o: kernel(x, o)),
        grid=(shape[1],),
        out_shape=jax.ShapeDtypeStruct(shape, F32),
        in_specs=[pl.BlockSpec(block, index)] + [pl.BlockSpec(memory_space=pl.ANY)] * len(whole),
        out_specs=spec,
        input_output_aliases={} if held is None else {1: 0},
        compiler_params=pltpu.CompilerParams(vmem_limit_bytes=32 * 1024 * 1024),
    )(source, *whole)


def store_gate_up(layout, source, shape, layer, held):
    width = shape[3] // (2 * layout.shards)
    per = layout.shards // layout.reps

    def kernel(x, o):
        for half in range(2):
            for b in range(per):
                for f in range(layout.reps):
                    start = ((half * per + b) * layout.reps + f) * width
                    at = (half * per + b) * width
                    o[0, 0, :, start : start + width] = x[0, f, :, at : at + width].astype(F32)

    block = (1,) + source.shape[1:]
    return store_layer(kernel, source, block, lambda e: (e, 0, 0, 0), shape, layer, held)


def store_down(source, shape, layer, held):
    def kernel(x, o):
        o[...] = x[...].astype(F32)

    block = (1, 1) + source.shape[2:]
    return store_layer(kernel, source, block, lambda e: (0, e, 0, 0), shape, layer, held)


def place_pairs(routes, priority, expert):
    flat = routes.reshape(-1)
    ahead = (flat[:, None] == flat[None, :]) & (priority[:, None] < priority[None, :])
    position = jnp.sum(ahead.astype(jnp.int32), axis=0)
    kept = (flat < EF) & (position < CAP)
    slot = jnp.where(kept, (flat ^ expert) * CAP + position, EF * CAP).reshape(-1, TOP).T
    places = jnp.arange(EF * CAP, dtype=jnp.int32)
    gather = (places[None, :, None] == slot[:, None, :]).astype(BF16)
    scatter = (places[None, None, :] == slot[:, :, None]).astype(BF16)
    return gather, scatter


def attention_forward(shared, dense, hidden, previous, routes, gather):
    gains, weights, mixing = dense
    tokens, features = hidden.shape
    cosine, sine, seg_col, seg_row = shared
    low = ((tokens, features), BF16)
    lanes = ((tokens, LANES), F32)
    return call(
        attention_forward_kernel,
        [low, low, low, low, lanes, low, ((tokens, features), F32), low, lanes, lanes]
        + [((EF * CAP, features), BF16)],
        (hidden, gains, weights, cosine, sine, seg_col, seg_row, mixing, previous, routes)
        + (gather[0] + gather[1],),
        [((tokens, tokens), F32)],
    )


def expert_forward(layout, inputs, w_gate_up, w_down):
    count, features = inputs.shape
    units = w_down.shape[0]
    return call(
        expert_forward_kernel,
        [((count, 2 * units), F32), ((count, units), BF16)]
        + [((EF * CAP, features), F32), ((count - EF * CAP, features), BF16)],
        (inputs, w_gate_up, w_down),
    )


def expert_backward(layout, d_expert, w_gate_up, w_down, gate_up):
    count, features = d_expert.shape
    units = w_down.shape[0]
    return call(
        expert_backward_kernel,
        [((count, 2 * units), BF16)]
        + [((EF * CAP, features), F32), ((count - EF * CAP, features), BF16)],
        (d_expert, w_gate_up, w_down, gate_up),
    )


def local(
    layout,
    hidden_in,
    gate_in,
    routes,
    priority,
    segments,
    norm_attn,
    w_qkv,
    w_out,
    norm_moe,
    w_router,
    w_const,
    const_vec,
    w_gate_up,
    w_down,
    grad_out,
):
    layers = w_qkv.shape[0]
    tokens, features = hidden_in.shape
    rep, j, expert = layout.place()
    slim = w_qkv.shape[1]
    small = [
        jnp.concatenate(
            [norm_attn[l][:, None], norm_moe[l][:, None], w_router[l], w_const[l], const_vec[l].T],
            axis=-1,
        ).reshape(1, -1)
        for l in range(layers)
    ]
    small = jnp.concatenate(small, axis=-1)
    extra = ROWS * features
    small = jnp.pad(small, ((0, 0), (0, extra - small.shape[1]))).reshape(ROWS, features)
    count = EF // layout.reps
    shard = lax.axis_index("shard")
    where = jnp.stack([rep, shard // EF, j // 2, j % 2]).astype(jnp.int32)

    group = rep.reshape(1).astype(jnp.int32)

    def share(l, *more):
        blocks = jnp.concatenate(
            [jnp.transpose(w_qkv[l].reshape(slim, 3, features), (1, 0, 2)), w_out[l][None]]
        )
        mine = lax.dynamic_slice_in_dim(blocks, rep * count, count, 0)
        return jnp.concatenate([mine.reshape(count * slim, features), *more])

    def dense_weights(x):
        full = layout.assemble(layout.dense_gather(x), where, count)
        return full[0].reshape(4, features, features), *full[1:]

    full, small_full = dense_weights(share(0, small))
    small_full = small_full.reshape(layout.shards, -1)
    dense, moe = [full], []
    raw = w_gate_up
    for l in range(layers):
        *found, last = expert_weights(layout, raw, w_down, l, rep, j, group)
        moe.append(found)
        raw = after(raw, last)
    packs, vectors, mixing_t = [], [], []
    for l in range(layers):
        part = small_full[:, l * slim * SMALL : (l + 1) * slim * SMALL]
        part = part.reshape(features, SMALL)
        mixing = part[:, 2 : SMALL - NCONST]
        mixing = jnp.pad(mixing, ((0, 0), (0, LANES - mixing.shape[1])))
        packs.append([part[:, :2].T.astype(F32), None, mixing])
        mixing_t.append(mixing.T)
        vectors.append(part[:, SMALL - NCONST :].T.astype(F32))

    shared = (*rope_tables(tokens), segments.reshape(-1, 1), segments)
    pairs = [place_pairs(routes[l], priority[l, 0], expert) for l in range(layers)]

    hidden = hidden_in
    previous = jnp.pad(gate_in, ((0, 0), (0, LANES - EXPERTS)))
    kept = []
    for l in range(layers):
        gather, scatter = pairs[l]
        packs[l][1] = dense[l]
        state = attention_forward(shared, packs[l], hidden, previous, routes[l], gather)
        normed, query, keys, values, log_total, attended, middle, low, logits, coefs, rows = state
        if l + 1 < layers:
            dense.append(dense_weights(after(share(l + 1), rows))[0])
        inputs = layout.dispatch(rows)
        gate_up, activated, own, others = expert_forward(layout, inputs, *moe[l])
        outputs = layout.collect(own, others)
        (result,) = call(
            combine_kernel,
            [((tokens, features), F32)],
            (coefs, middle, packs[l][0], scatter, outputs, vectors[l]),
        )
        kept.append((hidden, state, inputs, gate_up, activated, outputs))
        hidden, previous = result, logits

    grad_hidden = grad_out
    grad_gate = jnp.zeros_like(previous)
    dense_grads = [None] * layers
    waiting = None
    gate_up_out, down_out = None, None

    def store(wide, down, l, gate_up_out, down_out):
        down_out = store_down(
            place_down(layout, down, rep, j), (layers, EF) + w_down.shape[2:], l, down_out
        )
        gate_up_out = store_gate_up(
            layout,
            place_gate_up(layout, wide, rep, j),
            (layers, EF) + w_gate_up.shape[2:],
            l,
            gate_up_out,
        )
        return gate_up_out, down_out

    for l in reversed(range(layers)):
        gather, scatter = pairs[l]
        source, state, inputs, gate_up, activated, outputs = kept[l]
        normed, query, keys, values, log_total, attended, middle, low, logits, coefs, _ = state
        (rows,) = call(
            value_rows_kernel,
            [((EF * CAP, features), BF16)],
            (coefs, gather, grad_hidden),
        )
        d_expert = layout.dispatch(rows)
        grad_gate, d_mixed, mix_grads = call(
            gate_backward_kernel,
            [((tokens, LANES), F32), ((tokens, features), F32), ((SMALL - 2, features), F32)],
            (coefs, middle, packs[l][0], scatter, outputs, vectors[l], routes[l], low)
            + (mixing_t[l], grad_hidden, grad_gate),
        )
        if waiting is not None:
            d_expert, waiting = lax.optimization_barrier((d_expert, waiting))
            waiting = layout.sum_cross(waiting, rep, j)
        if l > 0:
            grad_down = dot(activated, d_expert, ((0,), (0,))).astype(BF16)
        d_gate_up, own, others = expert_backward(layout, d_expert, *moe[l], gate_up)
        d_rows = layout.collect(own, others)
        grad_gate_up = dot(inputs, d_gate_up, ((0,), (0,))).astype(BF16)
        wide = layout.line_sum(grad_gate_up)
        if l > 0:
            down = layout.line_sum(grad_down)
            gate_up_out, down_out = store(wide, down, l, gate_up_out, down_out)
        if waiting is not None:
            d_rows, waiting = lax.optimization_barrier((d_rows, waiting))
            dense_grads[l + 1] = layout.sum_line(waiting, rep)
        grad_hidden, d_branch, d_projected, gain_grads = call(
            attention_backward_kernel,
            [((tokens, features), F32), ((tokens, features), BF16)]
            + [((3, tokens, features), BF16), ((2, features), F32)],
            (grad_hidden, d_mixed, d_rows, scatter[0] + scatter[1], middle, source)
            + (packs[l][0], packs[l][1], *shared, query, keys, values, log_total),
            [((tokens, tokens), F32), ((tokens, features), BF16), ((tokens, features), F32)],
        )
        if l == 0:
            activated = after(activated, d_branch)
            grad_down = dot(activated, d_expert, ((0,), (0,))).astype(BF16)
            down = layout.line_sum(grad_down)
        grad_dense = jnp.stack(
            [dot(normed, d_projected[b], ((0,), (0,))).astype(BF16) for b in range(3)]
            + [dot(attended, d_branch, ((0,), (0,))).astype(BF16)]
        )
        small_grads = jnp.concatenate([gain_grads, mix_grads]).T.astype(BF16)
        lines = layout.lines
        blocks = grad_dense.reshape(layout.reps, count, lines, 2, 2, slim, features)
        small_grads = small_grads.reshape(lines, 2, 2, slim * SMALL)
        small_grads = jnp.pad(
            small_grads, ((0, 0),) * 3 + ((0, ROWS * features - slim * SMALL),)
        ).reshape(lines, 2, 2, ROWS, features)

        def parts(c):
            chosen = lax.dynamic_slice_in_dim(blocks, c, 1, 4)[:, :, :, :, 0]
            chosen = jnp.transpose(chosen, (0, 2, 3, 1, 4, 5)).reshape(
                layout.reps, lines, 2, count * slim, features
            )
            extra = lax.dynamic_slice_in_dim(small_grads, c, 1, 2)[:, :, 0]
            extra = jnp.broadcast_to(extra[None], (layout.reps,) + extra.shape)
            return jnp.concatenate([chosen, extra], axis=3)

        waiting = layout.sum_core(parts, j)

    waiting = layout.sum_cross(waiting, rep, j)
    waiting, gate_up_out, down_out = lax.optimization_barrier((waiting, gate_up_out, down_out))
    dense_grads[0] = layout.sum_line(waiting, rep)
    gate_up_out, down_out = store(wide, down, 0, gate_up_out, down_out)
    dense_all = jnp.stack(dense_grads).astype(F32)
    small_all = dense_all[:, 0, count * slim :].reshape(layers, -1)[:, : slim * SMALL]
    small_all = small_all.reshape(layers, slim, SMALL)
    dense_all = dense_all[:, :, : count * slim].reshape(layers, 4, slim, features)
    qkv_all = jnp.transpose(dense_all[:, :3], (0, 2, 1, 3)).reshape(layers, slim, 3 * features)
    return (
        hidden.astype(BF16),
        grad_hidden,
        grad_gate[:, :EXPERTS],
        small_all[:, :, 0],
        qkv_all,
        dense_all[:, 3],
        small_all[:, :, 1],
        small_all[:, :, 2 : 2 + EXPERTS],
        small_all[:, :, 2 + EXPERTS : SMALL - NCONST],
        jnp.transpose(small_all[:, :, SMALL - NCONST :], (0, 2, 1)),
        gate_up_out,
        down_out,
    )


def solution(mesh):
    return jax.shard_map(
        functools.partial(local, Layout(mesh)),
        mesh=mesh,
        in_specs=(
            P(("rep", "shard"), None),
            P(("rep", "shard"), None),
            P(None, ("rep", "shard"), None),
            P(None, ("rep", "shard"), None),
            P(("rep", "shard"), None),
            P(None, "shard"),
            P(None, "shard", None),
            P(None, "shard", None),
            P(None, "shard"),
            P(None, "shard", None),
            P(None, "shard", None),
            P(None, None, "shard"),
            P(None, None, "shard", None),
            P(None, None, "shard", None),
            P(("rep", "shard"), None),
        ),
        out_specs=(
            P(("rep", "shard"), None),
            P(("rep", "shard"), None),
            P(("rep", "shard"), None),
            P(None, "shard"),
            P(None, "shard", None),
            P(None, "shard", None),
            P(None, "shard"),
            P(None, "shard", None),
            P(None, "shard", None),
            P(None, None, "shard"),
            P(None, None, "shard", None),
            P(None, None, "shard", None),
        ),
        check_vma=False,
    )
```

```python
import functools
import math

import jax
import jax.numpy as jnp
from jax import lax
from jax.experimental import pallas as pl
from jax.experimental.pallas import tpu as pltpu
from jax.sharding import PartitionSpec as P

HEAD_DIM = 64
EF = 4
NCONST = 2
TOP = 2
EXPERTS = 8
CAP = 80
SMALL = 2 + EXPERTS + 2 * NCONST + NCONST
ROWS = 16
LANES = 128

EPSILON = 1e-06
SCALE = 0.125
MASKED = -1000000000.0
AXES = ("rep", "shard")
BF16 = jnp.bfloat16
F32 = jnp.float32


def dot(a, b, dims=((1,), (0,))):
    return lax.dot_general(a, b, (dims, ((), ())), preferred_element_type=F32)


def rope_tables(tokens):
    half = HEAD_DIM // 2
    places = jnp.arange(tokens, dtype=jnp.int32).astype(F32)[:, None]
    powers = jnp.arange(half, dtype=jnp.int32).astype(F32) / half
    angles = places * jnp.exp(-math.log(10000.0) * powers)[None, :]
    cosine, sine = jnp.cos(angles), jnp.sin(angles)
    heads = LANES // HEAD_DIM
    return jnp.tile(cosine, (1, 2 * heads)), jnp.tile(
        jnp.concatenate([-sine, sine], axis=-1), (1, heads)
    )


def turn(block, cosine, sine):
    half = HEAD_DIM // 2
    lane = lax.broadcasted_iota(jnp.int32, block.shape, 1)
    width = block.shape[1]
    partner = jnp.where(
        lane % HEAD_DIM < half,
        pltpu.roll(block, width - half, 1),
        pltpu.roll(block, half, 1),
    )
    return block * cosine + partner * sine


def lane_pick(array, lane, index):
    return jnp.sum(jnp.where(lane == index, array, 0.0), axis=-1, keepdims=True)


def inverse_rms(x):
    return lax.rsqrt(jnp.mean(x * x, axis=-1, keepdims=True) + EPSILON)


def attention_bias(seg_col, seg_row):
    shape = (seg_col.shape[0], seg_row.shape[1])
    rows = lax.broadcasted_iota(jnp.int32, shape, 0)
    columns = lax.broadcasted_iota(jnp.int32, shape, 1)
    allowed = (seg_col[...] == seg_row[...]) & (columns <= rows)
    return jnp.where(allowed, 0.0, MASKED)


def head_masks(shape):
    lane = lax.broadcasted_iota(jnp.int32, shape, 1)
    return [(lane // HEAD_DIM) == half for half in range(LANES // HEAD_DIM)]


def columns_of(step, width):
    return pl.ds(pl.multiple_of(step * width, width), width)


def attention_forward_kernel(joined, last, *refs):
    refs = iter(refs)

    def take(number):
        return [next(refs) for _ in range(number)]

    parts = take(6 if joined else 1)
    gains, weights, cosine, sine, seg_col, seg_row, mixing, previous, routes, gather = take(10)
    d_result = take(1) if last else None
    hidden = take(1)[0] if joined else parts[0]
    normed, query, keys, values, log_total, attended, middle, mixed_low = take(8)
    logits, coefs, rows, bias, held, arrived = take(6)
    copies = [
        pltpu.make_async_copy(weights.at[block], held.at[block], arrived.at[block])
        for block in range(4)
    ]
    for copy in copies:
        copy.start()
    weights = held
    if joined:
        combine_kernel(*parts, hidden)
    tokens, features = hidden.shape
    h = hidden[...].astype(F32)
    normed[...] = (h * inverse_rms(h) * gains[0:1]).astype(BF16)
    bias[...] = attention_bias(seg_col, seg_row)
    wide = 2 * LANES
    for block, out in ((0, query), (1, keys)):
        copies[block].wait()

        @pl.loop(0, features // wide)
        def _(step):
            part = dot(normed[...], weights[block, :, columns_of(step, wide)])
            for k in range(2):
                turned = turn(part[:, k * LANES : (k + 1) * LANES], cosine[...], sine[...])
                out[:, columns_of(2 * step + k, LANES)] = turned.astype(BF16)

    copies[2].wait()

    @pl.loop(0, features // wide)
    def _(step):
        at = columns_of(step, wide)
        values[:, at] = dot(normed[...], weights[2, :, at]).astype(BF16)

    log_total[...] = jnp.zeros_like(log_total)

    @pl.loop(0, features // LANES)
    def _(step):
        at = columns_of(step, LANES)
        q, k, v = query[:, at], keys[:, at], values[:, at]
        lane = lax.broadcasted_iota(jnp.int32, log_total.shape, 1)
        total_out = jnp.zeros((tokens, LANES), F32)
        for half, mask in enumerate(head_masks(q.shape)):
            scores = dot(jnp.where(mask, q, 0), k, ((1,), (1,))) * SCALE + bias[...]
            top = jnp.max(scores, axis=-1, keepdims=True)
            weight = jnp.exp(scores - top)
            total = jnp.sum(weight, axis=-1, keepdims=True)
            probs = (weight * (1.0 / total)).astype(BF16)
            total_out += dot(probs, jnp.where(mask, v, 0))
            log_total[...] = jnp.where(
                lane == step * (LANES // HEAD_DIM) + half, top + jnp.log(total), log_total[...]
            )
        attended[:, at] = total_out.astype(BF16)

    copies[3].wait()

    @pl.loop(0, features // wide)
    def _(step):
        at = columns_of(step, wide)
        middle[:, at] = hidden[:, at].astype(F32) + dot(attended[...], weights[3, :, at])

    m = middle[...]
    low = (m * inverse_rms(m) * gains[1:2]).astype(BF16)
    mixed_low[...] = low
    rows[:, :features] = dot(gather[0] + gather[1], low).astype(BF16)
    raw = dot(low, mixing[...])
    lane = lax.broadcasted_iota(jnp.int32, raw.shape, 1)
    now = jnp.where(lane < EXPERTS, raw + previous[...], 0.0)
    logits[...] = now
    route = [routes[:, k : k + 1] for k in range(TOP)]
    chosen = [lane_pick(now, lane, route[k]) for k in range(TOP)]
    best = jnp.maximum(chosen[0], chosen[1])
    chosen = [jnp.exp(c - best) for c in chosen]
    gates = [c / (chosen[0] + chosen[1]) for c in chosen]
    shares = []
    for c in range(NCONST):
        pair = [lane_pick(raw, lane, EXPERTS + 2 * c + i) for i in range(2)]
        best = jnp.maximum(pair[0], pair[1])
        pair = [jnp.exp(p - best) for p in pair]
        shares.append([p / (pair[0] + pair[1]) for p in pair])
    copies = [(route[k] == EF + 1).astype(F32) for k in range(TOP)]
    consts = [[(route[k] == EF + 2 + c).astype(F32) for c in range(NCONST)] for k in range(TOP)]
    weight = [sum(consts[k][c] * gates[k] for k in range(TOP)) for c in range(NCONST)]
    columns = list(gates)
    columns += [
        copies[k] + sum(consts[k][c] * shares[c][0] for c in range(NCONST)) for k in range(TOP)
    ]
    columns += [consts[k][c] * shares[c][1] for k in range(TOP) for c in range(NCONST)]
    columns += [shares[c][i] for c in range(NCONST) for i in range(2)]
    columns += weight
    columns += [
        sum(copies[k] * gates[k] for k in range(TOP))
        + sum(shares[c][0] * weight[c] for c in range(NCONST))
    ]
    columns += [shares[c][1] * weight[c] for c in range(NCONST)]
    packed = jnp.zeros_like(raw)
    for index, column in enumerate(columns):
        packed = jnp.where(lane == index, column, packed)
    coefs[...] = packed
    if last:
        rows[:, features:] = value_rows(gates, gather, d_result[0])


GATE, MIXED, VECTOR, SHARE, WEIGHT, DIRECT, CONST = 0, 2, 4, 8, 12, 14, 15


def combine_kernel(coefs, middle, gains, scatter, outputs, vectors, result):
    coef = coefs[...]
    m = middle[...]
    total = m + coef[:, DIRECT : DIRECT + 1] * (m * inverse_rms(m) * gains[1:2])
    for k in range(TOP):
        total += coef[:, GATE + k : GATE + k + 1] * dot(scatter[k], outputs[:, : m.shape[1]])
    for c in range(NCONST):
        total += coef[:, CONST + c : CONST + c + 1] * vectors[c : c + 1]
    result[...] = total


def value_rows(gates, gather, d_result):
    return sum(
        dot(gather[k], (gates[k] * d_result[...]).astype(BF16)) for k in range(TOP)
    ).astype(BF16)


def two_parts(x):
    high = x.astype(BF16)
    return high, (x - high.astype(F32)).astype(BF16)


def gate_backward_kernel(
    coefs, middle, gains, scatter, outputs, vectors, routes, mixed_low, mixing_t, d_result, d_next,
    d_logits, d_mixed, grads,
):
    coef = coefs[...]
    m = middle[...]
    dh = d_result[...]
    lane = lax.broadcasted_iota(jnp.int32, coef.shape, 1)

    def column(index):
        return coef[:, index : index + 1]

    along = jnp.sum(m * inverse_rms(m) * gains[1:2] * dh, axis=-1, keepdims=True)
    with_vector = [
        jnp.sum(dh * vectors[c : c + 1], axis=-1, keepdims=True) for c in range(NCONST)
    ]
    d_gates = []
    for k in range(TOP):
        value = jnp.sum(dot(scatter[k], outputs[:, : dh.shape[1]]) * dh, axis=-1, keepdims=True)
        value += column(MIXED + k) * along
        value += sum(column(VECTOR + k * NCONST + c) * with_vector[c] for c in range(NCONST))
        d_gates.append(value)
    mean = sum(column(GATE + k) * d_gates[k] for k in range(TOP))
    terms = d_next[...]
    for k in range(TOP):
        chosen = column(GATE + k) * (d_gates[k] - mean)
        terms += jnp.where(lane == routes[:, k : k + 1], chosen, 0.0)
    d_logits[...] = terms
    vector_terms = jnp.zeros_like(terms)
    for c in range(NCONST):
        share = [column(SHARE + 2 * c + i) for i in range(2)]
        d_share = [column(WEIGHT + c) * along, column(WEIGHT + c) * with_vector[c]]
        mean = share[0] * d_share[0] + share[1] * d_share[1]
        for i in range(2):
            terms = jnp.where(
                lane == EXPERTS + 2 * c + i, share[i] * (d_share[i] - mean), terms
            )
        vector_terms = jnp.where(
            lane == EXPERTS + 2 * NCONST + c, column(CONST + c), vector_terms
        )
    high, lowest = two_parts(terms)
    d_mixed[...] = column(DIRECT) * dh + dot(high, mixing_t[...]) + dot(lowest, mixing_t[...])
    both = ((0,), (0,))
    total = dot(high, mixed_low[...], both) + dot(lowest, mixed_low[...], both)
    high, lowest = two_parts(vector_terms)
    dh_high, dh_low = two_parts(dh)
    total += dot(high, dh_high, both) + dot(lowest, dh_high, both) + dot(high, dh_low, both)
    grads[...] = total[: grads.shape[0]]


def expert_forward_kernel(inputs, w_gate_up, w_down, gate_up, activated, own, others):
    units = w_down.shape[0]
    wide = min(2 * LANES, units)
    kept = own.shape[0]

    @pl.loop(0, units // wide)
    def _(step):
        at = columns_of(step, wide)
        gate = dot(inputs[...], w_gate_up[:, at])
        up_at = pl.ds(pl.multiple_of(units + step * wide, wide), wide)
        up = dot(inputs[...], w_gate_up[:, up_at])
        gate_up[:, at] = gate
        gate_up[:, up_at] = up
        activated[:, at] = (gate / (1.0 + jnp.exp(-gate)) * up).astype(BF16)

    @pl.loop(0, w_down.shape[1] // (2 * LANES))
    def _(step):
        at = columns_of(step, 2 * LANES)
        out = dot(activated[...], w_down[:, at])
        own[:, at] = out[:kept]
        others[:, at] = out[kept:].astype(BF16)


def expert_backward_kernel(d_expert, w_gate_up, w_down, gate_up, d_gate_up, own, others):
    units = w_down.shape[0]
    wide = min(2 * LANES, units)
    kept = own.shape[0]

    @pl.loop(0, units // wide)
    def _(step):
        at = columns_of(step, wide)
        up_at = pl.ds(pl.multiple_of(units + step * wide, wide), wide)
        d_active = dot(d_expert[...], w_down[at, :], ((1,), (1,)))
        gate, up = gate_up[:, at], gate_up[:, up_at]
        sigmoid = 1.0 / (1.0 + jnp.exp(-gate))
        d_gate_up[:, at] = (
            d_active * up * sigmoid * (1.0 + gate * (1.0 - sigmoid))
        ).astype(BF16)
        d_gate_up[:, up_at] = (d_active * gate * sigmoid).astype(BF16)

    @pl.loop(0, w_gate_up.shape[0] // (2 * LANES))
    def _(step):
        at = columns_of(step, 2 * LANES)
        out = dot(d_gate_up[...], w_gate_up[at, :], ((1,), (1,)))
        own[:, at] = out[:kept]
        others[:, at] = out[kept:].astype(BF16)


def expert_both_kernel(
    rows, w_gate_up, w_down, d_gate_up, activated, own, others, gate_up
):
    features, units = w_gate_up.shape[0], w_down.shape[0]
    wide = min(2 * LANES, units)
    kept = own.shape[0]

    @pl.loop(0, units // wide)
    def _(step):
        at = columns_of(step, wide)
        up_at = pl.ds(pl.multiple_of(units + step * wide, wide), wide)
        gate_up[:, :wide] = dot(rows[:, :features], w_gate_up[:, at])
        gate_up[:, wide:] = dot(rows[:, :features], w_gate_up[:, up_at])
        d_active = dot(rows[:, features:], w_down[at, :], ((1,), (1,)))
        gate, up = gate_up[:, :wide], gate_up[:, wide:]
        sigmoid = 1.0 / (1.0 + jnp.exp(-gate))
        activated[:, at] = (gate * sigmoid * up).astype(BF16)
        d_gate_up[:, at] = (
            d_active * up * sigmoid * (1.0 + gate * (1.0 - sigmoid))
        ).astype(BF16)
        d_gate_up[:, up_at] = (d_active * gate * sigmoid).astype(BF16)

    @pl.loop(0, features // (2 * LANES))
    def _(step):
        at = columns_of(step, 2 * LANES)
        out = dot(activated[...], w_down[:, at])
        own[:, at] = out[:kept]
        others[:, at] = out[kept:].astype(BF16)
        out = dot(d_gate_up[...], w_gate_up[at, :], ((1,), (1,)))
        to = pl.ds(pl.multiple_of(features + step * 2 * LANES, 2 * LANES), 2 * LANES)
        own[:, to] = out[:kept]
        others[:, to] = out[kept:].astype(BF16)


def norm_backward(grad, source, gain):
    inverse = inverse_rms(source)
    scaled = grad * gain
    gain_grad = jnp.sum(grad * source * inverse, axis=0, keepdims=True)
    mean = jnp.mean(scaled * source, axis=-1, keepdims=True)
    return inverse * scaled - source * (inverse * inverse * inverse * mean), gain_grad


def attention_backward_kernel(more, *refs):
    refs = iter(refs)

    def take(number):
        return [next(refs) for _ in range(number)]

    d_result, d_mixed, d_rows, scatter, middle, hidden, gains, weights = take(8)
    cosine, sine, seg_col, seg_row, query, keys, values, log_total = take(8)
    coefs, gather = take(2) if more else (None, None)
    d_hidden, d_branch, d_projected, gain_grads = take(4)
    rows = take(1)[0] if more else None
    bias, d_attended, d_normed, held, arrived = take(5)
    copies = [
        pltpu.make_async_copy(weights.at[block], held.at[block], arrived.at[block])
        for block in range(4)
    ]
    for copy in copies[::-1]:
        copy.start()
    weights = held
    tokens, features = hidden.shape
    wide = 2 * LANES
    total = d_mixed[...] + dot(
        scatter[0] + scatter[1], d_rows[:, d_rows.shape[1] - features :]
    )
    d_middle, gain_grad = norm_backward(total, middle[...], gains[1:2])
    d_middle = d_middle + d_result[...]
    gain_grads[1:2] = gain_grad
    d_hidden[...] = d_middle
    d_branch[...] = d_middle.astype(BF16)
    bias[...] = attention_bias(seg_col, seg_row)
    copies[3].wait()

    @pl.loop(0, features // wide)
    def _(step):
        at = columns_of(step, wide)
        d_attended[:, at] = dot(d_branch[...], weights[3, at, :], ((1,), (1,))).astype(BF16)

    @pl.loop(0, features // LANES)
    def _(step):
        at = columns_of(step, LANES)
        q, k, v, da = query[:, at], keys[:, at], values[:, at], d_attended[:, at]
        lane = lax.broadcasted_iota(jnp.int32, log_total.shape, 1)
        zero = jnp.zeros((tokens, LANES), F32)
        dq, dk, dv = zero, zero, zero
        for half, mask in enumerate(head_masks(q.shape)):
            q_half, da_half = jnp.where(mask, q, 0), jnp.where(mask, da, 0)
            scores = dot(q_half, k, ((1,), (1,))) * SCALE + bias[...]
            shift = lane_pick(log_total[...], lane, step * (LANES // HEAD_DIM) + half)
            probs = jnp.exp(scores - shift)
            dv += dot(probs.astype(BF16), da_half, ((0,), (0,)))
            d_probs = dot(da_half, v, ((1,), (1,)))
            mean = jnp.sum(d_probs * probs, axis=-1, keepdims=True)
            d_scores = (probs * (d_probs - mean)).astype(BF16)
            dq += dot(d_scores, jnp.where(mask, k, 0))
            dk += dot(d_scores, q_half, ((0,), (0,)))
        d_projected[0, :, at] = turn(dq * SCALE, cosine[...], -sine[...]).astype(BF16)
        d_projected[1, :, at] = turn(dk * SCALE, cosine[...], -sine[...]).astype(BF16)
        d_projected[2, :, at] = dv.astype(BF16)

    for copy in copies[:3]:
        copy.wait()

    @pl.loop(0, features // wide)
    def _(step):
        at = columns_of(step, wide)
        d_normed[:, at] = sum(
            dot(d_projected[b], weights[b, at, :], ((1,), (1,))) for b in range(3)
        )

    d_input, gain_grad = norm_backward(d_normed[...], hidden[...].astype(F32), gains[0:1])
    gain_grads[0:1] = gain_grad
    d_hidden[...] += d_input
    if more:
        gates = [coefs[:, GATE + k : GATE + k + 1] for k in range(TOP)]
        rows[...] = value_rows(gates, gather, d_hidden)


def call(kernel, outs, args, scratch=(), apart=None):
    specs = [
        pl.BlockSpec(memory_space=pl.ANY) if k == apart else pl.BlockSpec()
        for k in range(len(args))
    ]
    scratch = [pltpu.VMEM(shape, dtype) for shape, dtype in scratch]
    if apart is not None:
        scratch += [
            pltpu.VMEM(args[apart].shape, args[apart].dtype),
            pltpu.SemaphoreType.DMA((4,)),
        ]
    return pl.pallas_call(
        kernel,
        out_shape=[jax.ShapeDtypeStruct(shape, dtype) for shape, dtype in outs],
        in_specs=specs,
        scratch_shapes=scratch,
        compiler_params=pltpu.CompilerParams(vmem_limit_bytes=60 * 1024 * 1024),
        cost_estimate=pl.CostEstimate(flops=1, bytes_accessed=1, transcendentals=0),
    )(*args)


def after(x, *others):
    return lax.optimization_barrier((x,) + others)[0]


class Layout:
    def __init__(self, mesh):
        self.reps, self.shards = mesh.shape["rep"], mesh.shape["shard"]
        self.lines = self.shards // EF
        assert self.shards % EF == 0 and EF % self.reps == 0

    def pairs(self, move):
        found = []
        for rep in range(self.reps):
            for shard in range(self.shards):
                r, z, j = move(rep, shard // EF, shard % EF)
                found.append((rep * self.shards + shard, r * self.shards + z * EF + j))
        return found

    def send(self, x, move):
        return lax.ppermute(x, AXES, self.pairs(move))

    def expert_move(self, mask, shift):
        def move(r, z, j):
            number = r * EF + j
            e, f = (number // self.reps) ^ mask, (number % self.reps + shift) % self.reps
            number = e * self.reps + f
            return number // EF, z, number % EF

        return move

    def place(self):
        rep, shard = lax.axis_index("rep"), lax.axis_index("shard")
        j = shard % EF
        return rep, j, (rep * EF + j) // self.reps

    def quad_exchange(self, blocks, j):
        got = lax.dynamic_update_slice_in_dim(
            jnp.zeros_like(blocks), lax.dynamic_slice_in_dim(blocks, j, 1, 0), j, 0
        )
        for mask in range(1, EF):
            other = j ^ mask
            block = lax.dynamic_slice_in_dim(blocks, other, 1, 0)
            block = self.send(block, lambda r, z, q: (r, z, q ^ mask))
            got = lax.dynamic_update_slice_in_dim(got, block, other, 0)
        return got

    def part_exchange(self, blocks, j):
        count = EF // self.reps
        mine = j // self.reps
        got = lax.dynamic_update_slice_in_dim(
            jnp.zeros_like(blocks), lax.dynamic_slice_in_dim(blocks, mine, 1, 0), mine, 0
        )
        for mask in range(1, count):
            other = mine ^ mask
            block = lax.dynamic_slice_in_dim(blocks, other, 1, 0)
            block = self.send(block, lambda r, z, q: (r, z, q ^ (mask * self.reps)))
            got = lax.dynamic_update_slice_in_dim(got, block, other, 0)
        return got

    def rep_gather(self, x, rep):
        got = lax.dynamic_update_slice_in_dim(
            jnp.zeros((self.reps,) + x.shape, x.dtype), x[None], rep, 0
        )
        for shift in range(1, self.reps):
            block = self.send(x, lambda r, z, q: ((r + shift) % self.reps, z, q))
            got = lax.dynamic_update_slice_in_dim(
                got, block[None], (rep + self.reps - shift) % self.reps, 0
            )
        return got

    def trade(self, blocks, chosen):
        groups = [
            [(n // EF) * self.shards + z * EF + n % EF for n in numbers]
            for z in range(self.lines)
            for numbers in chosen
        ]
        return lax.all_to_all(blocks, AXES, 0, 0, axis_index_groups=groups, tiled=True)

    def return_gate_up(self, blocks):
        return self.trade(
            jnp.concatenate([blocks] * self.reps), [list(range(self.reps * EF))]
        )

    def return_down(self, blocks):
        return self.trade(
            jnp.concatenate([blocks] * self.reps),
            [[e * self.reps + f for e in range(EF)] for f in range(self.reps)],
        )

    def line_groups(self):
        return [[z * EF + j for z in range(self.lines)] for j in range(EF)]

    def line_gather(self, x):
        return lax.all_gather(
            x, "shard", axis=0, tiled=True, axis_index_groups=self.line_groups()
        )

    def line_sum(self, x):
        return lax.psum_scatter(
            x, "shard", scatter_dimension=0, tiled=True, axis_index_groups=self.line_groups()
        )

    def dense_line(self, x):
        line = [x[None]]
        for shift in range(1, self.lines):
            line.append(self.send(x, lambda r, q, k: (r, (q + shift) % self.lines, k))[None])
        return jnp.concatenate(line)

    def dense_gather(self, line):
        reps, lines = self.reps, self.lines
        cut = lines // 2

        def over_rep(block, shift):
            return self.send(block, lambda r, q, k: ((r + shift) % reps, q, k))

        def over_high(block):
            return self.send(block, lambda r, q, k: (r, q, k ^ 2))

        sides = [over_rep(line, shift) for shift in range(1, reps)]
        flip = over_high(line)
        pieces = [(line, 0, 0, 0), (flip, 0, 0, 1)]
        for shift, block in enumerate(sides, 1):
            pieces.append((block, 0, shift, 0))
            pieces.append((over_high(block[:cut]), 0, shift, 1))
            pieces.append((over_rep(flip[cut:], shift), cut, shift, 1))
        pieces = [piece + (0,) for piece in pieces if piece[0].shape[0]]
        others = [
            (self.send(piece[0], lambda r, q, k: (r, q, k ^ 1)),) + piece[1:4] + (1,)
            for piece in pieces
        ]
        return pieces + others

    def assemble(self, pieces, where, count):
        reps, lines = self.reps, self.lines
        rows, features = pieces[0][0].shape[1:]
        slim = features // self.shards
        extra = rows - count * slim
        notes = [piece[1:] for piece in pieces]

        def kernel(where_ref, *refs):
            out = refs[len(pieces)]
            rep, z, high, core = [where_ref[k] for k in range(4)]
            for ref, (start, back, flip, other) in zip(refs, notes):
                r = lax.rem(rep + reps - back, reps)
                hi = high if flip == 0 else 1 - high
                lo = core if other == 0 else 1 - core
                for step in range(ref.shape[0]):
                    at = lax.rem(z + lines - start - step, lines)
                    for k in range(count):
                        out[r, k, at, hi, lo] = ref[step, k * slim : (k + 1) * slim]
                    if extra and back == 0:
                        refs[-1][at, hi, lo] = ref[step, count * slim :]

        shapes = [jax.ShapeDtypeStruct((reps, count, lines, 2, 2, slim, features), BF16)]
        if extra:
            shapes.append(jax.ShapeDtypeStruct((lines, 2, 2, extra, features), BF16))
        return pl.pallas_call(
            kernel,
            out_shape=shapes,
            in_specs=[pl.BlockSpec(memory_space=pltpu.SMEM)]
            + [pl.BlockSpec(memory_space=pltpu.VMEM)] * len(pieces),
            out_specs=[pl.BlockSpec(memory_space=pltpu.VMEM)] * len(shapes),
            compiler_params=pltpu.CompilerParams(vmem_limit_bytes=60 * 1024 * 1024),
        )(where, *[piece[0] for piece in pieces])

    def over_rep(self, block, shift):
        return self.send(block, lambda r, q, k: ((r + shift) % self.reps, q, k))

    def sum_core(self, terms, core):
        mine = lax.dynamic_slice_in_dim(terms, core, 1, 0)[0]
        other = lax.dynamic_slice_in_dim(terms, 1 - core, 1, 0)[0]
        other = self.send(other, lambda r, q, k: (r, q, k ^ 1))
        return (mine.astype(F32) + other.astype(F32)).astype(BF16)

    def rep_step(self, x, rep):
        total = lax.dynamic_slice_in_dim(x, rep, 1, 0)[0].astype(F32)
        for shift in range(1, self.reps):
            block = lax.dynamic_slice_in_dim(x, (rep + shift) % self.reps, 1, 0)[0]
            total = total + self.over_rep(block, shift).astype(F32)
        return total.astype(BF16)

    def high_step(self, x, high, axis):
        mine = lax.dynamic_slice_in_dim(x, high, 1, axis)
        other = lax.dynamic_slice_in_dim(x, 1 - high, 1, axis)
        other = self.send(other, lambda r, q, k: (r, q, k ^ 2))
        return jnp.squeeze(mine.astype(F32) + other.astype(F32), axis).astype(BF16)

    def sum_cross(self, both, rep, j):
        cut = self.lines // 2
        return self.high_step(both[:, :cut], j // 2, 2), self.rep_step(both[:, cut:], rep)

    def sum_cross_end(self, first, second, rep, j):
        return jnp.concatenate([self.rep_step(first, rep), self.high_step(second, j // 2, 1)])

    def sum_line(self, line):
        z = lax.axis_index("shard") // EF
        lines = self.lines
        total = lax.dynamic_slice_in_dim(line, z, 1, 0)[0].astype(F32)
        for shift in range(1, lines):
            block = lax.dynamic_slice_in_dim(line, (z + shift) % lines, 1, 0)[0]
            block = self.send(block, lambda r, q, k: (r, (q + shift) % lines, k))
            total = total + block.astype(F32)
        return total.astype(BF16)

    def dispatch(self, rows):
        blocks = rows.reshape(EF, CAP, -1)
        own = jnp.stack(
            [blocks[0]] + [self.send(blocks[m], self.expert_move(m, 0)) for m in range(1, EF)]
        )
        parts = [own] + [self.send(own, self.expert_move(0, g)) for g in range(1, self.reps)]
        return jnp.concatenate(parts).reshape(self.reps * EF * CAP, -1)

    def collect(self, own, others):
        total = own
        for g in range(1, self.reps):
            block = others[(g - 1) * EF * CAP : g * EF * CAP]
            total = total + self.send(block, self.expert_move(0, self.reps - g)).astype(F32)
        total = total.astype(BF16).reshape(EF, CAP, -1)
        return jnp.concatenate(
            [total[0]] + [self.send(total[m], self.expert_move(m, 0)) for m in range(1, EF)]
        )


def split_gate_up(layout, w_gate_up, layer, where):
    _, experts, rows, columns = w_gate_up.shape
    width = columns // (2 * layout.shards)
    parts = layout.reps
    per = layout.shards // parts

    def kernel(where_ref, x, o):
        for j in range(EF):
            e = where_ref[0] * (EF // layout.reps) + j // parts
            for b in range(2 * per):
                at = (b * parts + j % parts) * width
                o[j, :, b * width : (b + 1) * width] = x[0, e, :, at : at + width]

    return pl.pallas_call(
        kernel,
        grid=(1,),
        out_shape=jax.ShapeDtypeStruct((EF, rows, columns // parts), BF16),
        in_specs=[
            pl.BlockSpec(memory_space=pltpu.SMEM),
            pl.BlockSpec((1, experts, rows, columns), lambda _: (layer, 0, 0, 0)),
        ],
        out_specs=pl.BlockSpec((EF, rows, columns // parts), lambda _: (0, 0, 0)),
        compiler_params=pltpu.CompilerParams(vmem_limit_bytes=60 * 1024 * 1024),
    )(where, w_gate_up)


def expert_weights(layout, w_gate_up, w_down, layer, rep, j, where):
    count = EF // layout.reps
    mine = layout.quad_exchange(split_gate_up(layout, w_gate_up, layer, where), j)
    mine = mine.reshape(-1, mine.shape[-1])
    down = lax.dynamic_slice_in_dim(after(w_down[layer], mine), rep * count, count, 0)
    down = layout.part_exchange(down, j)
    down = down.reshape(-1, down.shape[-1])
    return layout.line_gather(mine), layout.line_gather(down), down


def dense_gradients(layout, terms, small, count):
    tokens, features = terms[0].shape
    lines, slim = layout.lines, features // layout.shards
    wide = 2 * LANES

    def kernel(normed, attended, d_projected, d_branch, small_ref, out, turned):
        turned[0] = normed[...].T
        turned[1] = attended[...].T
        for block in range(4):
            r, k = block // count, block % count

            @pl.loop(0, features // wide)
            def _(step):
                at = columns_of(step, wide)
                grad = d_branch[:, at] if block == 3 else d_projected[block, :, at]
                term = dot(turned[block // 3], grad).astype(BF16)
                for s in range(layout.shards):
                    out[s % 2, r, s // EF, s // 2 % 2, k * slim : (k + 1) * slim, at] = term[
                        s * slim : (s + 1) * slim
                    ]

        for s in range(layout.shards):
            for r in range(layout.reps):
                out[s % 2, r, s // EF, s // 2 % 2, count * slim :] = small_ref[s]

    shape = (2, layout.reps, lines, 2, count * slim + ROWS, features)
    return call(kernel, [(shape, BF16)], (*terms, small), [((2, features, tokens), BF16)])[0]


def store_layer(kernel, source, block, index, shape, layer, held):
    spec = pl.BlockSpec((1, 1) + shape[2:], lambda e: (layer, e) + (0,) * (len(shape) - 2))
    whole = [] if held is None else [held]
    return pl.pallas_call(
        (lambda x, o: kernel(x, o)) if held is None else (lambda x, h, o: kernel(x, o)),
        grid=(shape[1],),
        out_shape=jax.ShapeDtypeStruct(shape, F32),
        in_specs=[pl.BlockSpec(block, index)] + [pl.BlockSpec(memory_space=pl.ANY)] * len(whole),
        out_specs=spec,
        input_output_aliases={} if held is None else {1: 0},
        compiler_params=pltpu.CompilerParams(vmem_limit_bytes=60 * 1024 * 1024),
    )(source, *whole)


def store_gate_up(layout, source, shape, layer, held):
    width = shape[3] // (2 * layout.shards)
    per = layout.shards // layout.reps

    def kernel(x, o):
        for half in range(2):
            for b in range(per):
                for f in range(layout.reps):
                    start = ((half * per + b) * layout.reps + f) * width
                    at = (half * per + b) * width
                    o[0, 0, :, start : start + width] = x[0, f, :, at : at + width].astype(F32)

    block = (1,) + source.shape[1:]
    return store_layer(kernel, source, block, lambda e: (e, 0, 0, 0), shape, layer, held)


def store_down(source, shape, layer, held):
    def kernel(x, o):
        o[...] = x[...].astype(F32)

    block = (1, 1) + source.shape[2:]
    return store_layer(kernel, source, block, lambda e: (0, e, 0, 0), shape, layer, held)


def place_pairs(routes, priority, expert):
    flat = routes.reshape(-1)
    ahead = (flat[:, None] == flat[None, :]) & (priority[:, None] < priority[None, :])
    position = jnp.sum(ahead.astype(jnp.int32), axis=0)
    kept = (flat < EF) & (position < CAP)
    slot = jnp.where(kept, (flat ^ expert) * CAP + position, EF * CAP).reshape(-1, TOP).T
    places = jnp.arange(EF * CAP, dtype=jnp.int32)
    gather = (places[None, :, None] == slot[:, None, :]).astype(BF16)
    scatter = (places[None, None, :] == slot[:, :, None]).astype(BF16)
    return gather, scatter


def attention_forward(shared, dense, source, previous, routes, gather, d_result):
    gains, weights, mixing = dense
    tokens, features = source[1 if len(source) > 1 else 0].shape
    joined, last = len(source) > 1, d_result is not None
    low = ((tokens, features), BF16)
    full = ((tokens, features), F32)
    lanes = ((tokens, LANES), F32)
    found = call(
        functools.partial(attention_forward_kernel, joined, last),
        [full] * joined
        + [low, low, low, low, lanes, low, full, low, lanes, lanes]
        + [((gather.shape[1], features * (2 if last else 1)), BF16)],
        (*source, gains, weights, *shared, mixing, previous, routes, gather)
        + ((d_result,) if last else ()),
        [((tokens, tokens), F32)],
        len(source) + 1,
    )
    return found if joined else [source[0], *found]


def expert_both(rows, w_gate_up, w_down):
    count, double = rows.shape
    units = w_down.shape[0]
    return call(
        expert_both_kernel,
        [((count, 2 * units), BF16), ((count, units), BF16)]
        + [((EF * CAP, double), F32), ((count - EF * CAP, double), BF16)],
        (rows, w_gate_up, w_down),
        [((count, 2 * min(2 * LANES, units)), F32)],
    )


def expert_forward(layout, inputs, w_gate_up, w_down):
    count, features = inputs.shape
    units = w_down.shape[0]
    return call(
        expert_forward_kernel,
        [((count, 2 * units), F32), ((count, units), BF16)]
        + [((EF * CAP, features), F32), ((count - EF * CAP, features), BF16)],
        (inputs, w_gate_up, w_down),
    )


def expert_backward(layout, d_expert, w_gate_up, w_down, gate_up):
    count, features = d_expert.shape
    units = w_down.shape[0]
    return call(
        expert_backward_kernel,
        [((count, 2 * units), BF16)]
        + [((EF * CAP, features), F32), ((count - EF * CAP, features), BF16)],
        (d_expert, w_gate_up, w_down, gate_up),
    )


def local(
    layout,
    hidden_in,
    gate_in,
    routes,
    priority,
    segments,
    norm_attn,
    w_qkv,
    w_out,
    norm_moe,
    w_router,
    w_const,
    const_vec,
    w_gate_up,
    w_down,
    grad_out,
):
    layers = w_qkv.shape[0]
    tokens, features = hidden_in.shape
    rep, j, expert = layout.place()
    slim = w_qkv.shape[1]
    small = [
        jnp.concatenate(
            [norm_attn[l][:, None], norm_moe[l][:, None], w_router[l], w_const[l], const_vec[l].T],
            axis=-1,
        ).reshape(1, -1)
        for l in range(layers)
    ]
    small = jnp.concatenate(small, axis=-1)
    extra = ROWS * features
    small = jnp.pad(small, ((0, 0), (0, extra - small.shape[1]))).reshape(ROWS, features)
    count = EF // layout.reps
    shard = lax.axis_index("shard")
    where = jnp.stack([rep, shard // EF, j // 2, j % 2]).astype(jnp.int32)

    group = rep.reshape(1).astype(jnp.int32)

    def share(l, *more):
        blocks = jnp.concatenate(
            [jnp.transpose(w_qkv[l].reshape(slim, 3, features), (1, 0, 2)), w_out[l][None]]
        )
        mine = lax.dynamic_slice_in_dim(blocks, rep * count, count, 0)
        return jnp.concatenate([mine.reshape(count * slim, features), *more])

    def dense_weights(x):
        full = layout.assemble(layout.dense_gather(x), where, count)
        return full[0].reshape(4, features, features), *full[1:]

    line = layout.dense_line(share(0, small))
    *found, last = expert_weights(layout, w_gate_up, w_down, 0, rep, j, group)
    moe = [found]
    full, small_full = dense_weights(after(line, last))
    small_full = small_full.reshape(layout.shards, -1)
    dense = [full]
    raw = after(w_gate_up, full)
    for l in range(1, layers):
        *found, last = expert_weights(layout, raw, w_down, l, rep, j, group)
        moe.append(found)
        raw = after(raw, last)
    packs, vectors, mixing_t = [], [], []
    for l in range(layers):
        part = small_full[:, l * slim * SMALL : (l + 1) * slim * SMALL]
        part = part.reshape(features, SMALL)
        mixing = part[:, 2 : SMALL - NCONST]
        mixing = jnp.pad(mixing, ((0, 0), (0, LANES - mixing.shape[1])))
        packs.append([part[:, :2].T.astype(F32), None, mixing])
        mixing_t.append(mixing.T)
        vectors.append(part[:, SMALL - NCONST :].T.astype(F32))

    shared = (*rope_tables(tokens), segments.reshape(-1, 1), segments)
    pairs = [place_pairs(routes[l], priority[l, 0], expert) for l in range(layers)]

    source = (hidden_in,)
    previous = jnp.pad(gate_in, ((0, 0), (0, LANES - EXPERTS)))
    kept = []
    for l in range(layers):
        gather, scatter = pairs[l]
        packs[l][1] = dense[l]
        last = l + 1 == layers
        state = attention_forward(
            shared, packs[l], source, previous, routes[l], gather, grad_out if last else None
        )
        middle, logits, coefs, rows = state[7], state[9], state[10], state[11]
        if last:
            inputs = layout.dispatch(rows)
            d_gate_up, activated, own, others = expert_both(inputs, *moe[l])
            wide = dot(inputs[:, :features], d_gate_up, ((0,), (0,))).astype(BF16)
            down = dot(activated, inputs[:, features:], ((0,), (0,))).astype(BF16)
        else:
            dense.append(dense_weights(layout.dense_line(after(share(l + 1), rows)))[0])
            inputs = layout.dispatch(rows)
            gate_up, activated, own, others = expert_forward(layout, inputs, *moe[l])
        outputs = layout.collect(own, others)
        if last:
            outputs, wide, down = lax.optimization_barrier((outputs, wide, down))
        source = (coefs, middle, packs[l][0], scatter, outputs, vectors[l])
        previous = logits
        kept.append((state, inputs, gate_up, activated, outputs))
    (result,) = call(combine_kernel, [((tokens, features), F32)], source)

    grad_hidden = grad_out
    grad_gate = jnp.zeros_like(previous)
    join = lax.optimization_barrier

    def back_down(x):
        return layout.return_down(x.reshape(count, -1, features))

    def back_gate_up(x):
        return layout.return_gate_up(x.reshape(EF, -1, x.shape[-1]))

    def put_down(x, l, held):
        return store_down(x[None], (layers, EF) + w_down.shape[2:], l, held)

    def put_gate_up(x, l, held):
        x = x.reshape((EF, layout.reps) + x.shape[1:])
        return store_gate_up(layout, x, (layers, EF) + w_gate_up.shape[2:], l, held)

    boths, wides, downs = [None] * layers, [None] * layers, [None] * layers
    gate_up_out, down_out = None, None
    for l in reversed(range(layers)):
        gather, scatter = pairs[l]
        state, inputs, gate_up, activated, outputs = kept[l]
        hidden, normed, query, keys, values, log_total, attended, middle, low = state[:9]
        coefs = state[10]
        last = l + 1 == layers
        if not last:
            d_expert = layout.dispatch(rows)
        grad_gate, d_mixed, mix_grads = call(
            gate_backward_kernel,
            [((tokens, LANES), F32), ((tokens, features), F32), ((SMALL - 2, features), F32)],
            (coefs, middle, packs[l][0], scatter, outputs, vectors[l], routes[l], low)
            + (mixing_t[l], grad_hidden, grad_gate),
        )
        if last:
            d_rows = outputs
            wides[l], downs[l] = layout.line_sum(wide), layout.line_sum(down)
        else:
            d_expert, d_mixed = join((d_expert, d_mixed))
            down = back_down(after(downs[l + 1], d_expert))
            d_gate_up, own, others = expert_backward(layout, d_expert, *moe[l], gate_up)
            own, down = join((own, down))
            down_out = put_down(down, l + 1, down_out)
            grad_gate_up = dot(inputs, d_gate_up, ((0,), (0,))).astype(BF16)
            d_rows = layout.collect(own, others)
            boths[l + 1] = layout.sum_core(
                dense_gradients(layout, *after(ready, d_expert), count), j % 2
            )
            grad_down = dot(activated, d_expert, ((0,), (0,))).astype(BF16)
            d_rows, grad_gate_up, grad_down, boths[l + 1], down_out = join(
                (d_rows, grad_gate_up, grad_down, boths[l + 1], down_out)
            )
            wides[l], downs[l] = layout.line_sum(grad_gate_up), layout.line_sum(grad_down)
            d_rows, wides[l + 1] = join((d_rows, wides[l + 1]))
            wide = back_gate_up(wides[l + 1])
        more = () if l == 0 else (kept[l - 1][0][10], pairs[l - 1][0])
        grad_hidden, d_branch, d_projected, gain_grads, *rows = call(
            functools.partial(attention_backward_kernel, l > 0),
            [((tokens, features), F32), ((tokens, features), BF16)]
            + [((3, tokens, features), BF16), ((2, features), F32)]
            + [((gather.shape[1], features), BF16)] * (l > 0),
            (grad_hidden, d_mixed, d_rows, scatter, middle, hidden, packs[l][0], packs[l][1])
            + (*shared, query, keys, values, log_total, *more),
            [((tokens, tokens), F32), ((tokens, features), BF16), ((tokens, features), F32)],
            7,
        )
        rows = rows[0] if rows else None
        if not last:
            d_branch, wide = join((d_branch, wide))
            gate_up_out = put_gate_up(wide, l + 1, gate_up_out)
        small_grads = jnp.concatenate([gain_grads, mix_grads]).T.astype(BF16)
        small_grads = small_grads.reshape(layout.shards, slim * SMALL)
        small_grads = jnp.pad(small_grads, ((0, 0), (0, ROWS * features - slim * SMALL)))
        ready = (
            (normed, attended, d_projected, d_branch),
            small_grads.reshape(layout.shards, ROWS, features),
        )

    boths[0] = layout.sum_core(dense_gradients(layout, *ready, count), j % 2)
    both, gate_up_out = join((jnp.concatenate(boths, axis=3), gate_up_out))
    cross, down = join((layout.sum_cross(both, rep, j), back_down(after(downs[0], both))))
    down_out = put_down(down, 0, down_out)
    line = layout.sum_cross_end(*cross, rep, j)
    line, wides[0] = join((line, wides[0]))
    line, wide = join((layout.sum_line(line), back_gate_up(wides[0])))
    gate_up_out = put_gate_up(wide, 0, gate_up_out)
    dense_all = layout.rep_gather(line, rep).reshape(layout.reps, layers, -1, features)
    dense_grads = jnp.swapaxes(dense_all, 0, 1)
    dense_all = dense_grads.astype(F32)
    small_all = dense_all[:, 0, count * slim :].reshape(layers, -1)[:, : slim * SMALL]
    small_all = small_all.reshape(layers, slim, SMALL)
    dense_all = dense_all[:, :, : count * slim].reshape(layers, 4, slim, features)
    qkv_all = jnp.transpose(dense_all[:, :3], (0, 2, 1, 3)).reshape(layers, slim, 3 * features)
    return (
        result.astype(BF16),
        grad_hidden,
        grad_gate[:, :EXPERTS],
        small_all[:, :, 0],
        qkv_all,
        dense_all[:, 3],
        small_all[:, :, 1],
        small_all[:, :, 2 : 2 + EXPERTS],
        small_all[:, :, 2 + EXPERTS : SMALL - NCONST],
        jnp.transpose(small_all[:, :, SMALL - NCONST :], (0, 2, 1)),
        gate_up_out,
        down_out,
    )


def solution(mesh):
    return jax.shard_map(
        functools.partial(local, Layout(mesh)),
        mesh=mesh,
        in_specs=(
            P(("rep", "shard"), None),
            P(("rep", "shard"), None),
            P(None, ("rep", "shard"), None),
            P(None, ("rep", "shard"), None),
            P(("rep", "shard"), None),
            P(None, "shard"),
            P(None, "shard", None),
            P(None, "shard", None),
            P(None, "shard"),
            P(None, "shard", None),
            P(None, "shard", None),
            P(None, None, "shard"),
            P(None, None, "shard", None),
            P(None, None, "shard", None),
            P(("rep", "shard"), None),
        ),
        out_specs=(
            P(("rep", "shard"), None),
            P(("rep", "shard"), None),
            P(("rep", "shard"), None),
            P(None, "shard"),
            P(None, "shard", None),
            P(None, "shard", None),
            P(None, "shard"),
            P(None, "shard", None),
            P(None, "shard", None),
            P(None, None, "shard"),
            P(None, None, "shard", None),
            P(None, None, "shard", None),
        ),
        check_vma=False,
    )
```

```python
import functools
import math

import jax
import jax.numpy as jnp
from jax import lax
from jax.experimental import pallas as pl
from jax.experimental.pallas import tpu as pltpu
from jax.sharding import PartitionSpec as P

HEAD_DIM = 64
EF = 4
NCONST = 2
TOP = 2
EXPERTS = 8
CAP = 80
SMALL = 2 + EXPERTS + 2 * NCONST + NCONST
ROWS = 16
LANES = 128

EPSILON = 1e-06
SCALE = 0.125
MASKED = -1000000000.0
AXES = ("rep", "shard")
BF16 = jnp.bfloat16
F32 = jnp.float32


def dot(a, b, dims=((1,), (0,))):
    return lax.dot_general(a, b, (dims, ((), ())), preferred_element_type=F32)


def rope_tables(tokens):
    half = HEAD_DIM // 2
    places = jnp.arange(tokens, dtype=jnp.int32).astype(F32)[:, None]
    powers = jnp.arange(half, dtype=jnp.int32).astype(F32) / half
    angles = places * jnp.exp(-math.log(10000.0) * powers)[None, :]
    cosine, sine = jnp.cos(angles), jnp.sin(angles)
    heads = LANES // HEAD_DIM
    return jnp.tile(cosine, (1, 2 * heads)), jnp.tile(
        jnp.concatenate([-sine, sine], axis=-1), (1, heads)
    )


def turn(block, cosine, sine):
    half = HEAD_DIM // 2
    lane = lax.broadcasted_iota(jnp.int32, block.shape, 1)
    width = block.shape[1]
    partner = jnp.where(
        lane % HEAD_DIM < half,
        pltpu.roll(block, width - half, 1),
        pltpu.roll(block, half, 1),
    )
    return block * cosine + partner * sine


def lane_pick(array, lane, index):
    return jnp.sum(jnp.where(lane == index, array, 0.0), axis=-1, keepdims=True)


def inverse_rms(x):
    return lax.rsqrt(jnp.mean(x * x, axis=-1, keepdims=True) + EPSILON)


def attention_bias(seg_col, seg_row):
    shape = (seg_col.shape[0], seg_row.shape[1])
    rows = lax.broadcasted_iota(jnp.int32, shape, 0)
    columns = lax.broadcasted_iota(jnp.int32, shape, 1)
    allowed = (seg_col[...] == seg_row[...]) & (columns <= rows)
    return jnp.where(allowed, 0.0, MASKED)


def head_masks(shape):
    lane = lax.broadcasted_iota(jnp.int32, shape, 1)
    return [(lane // HEAD_DIM) == half for half in range(LANES // HEAD_DIM)]


def columns_of(step, width):
    return pl.ds(pl.multiple_of(step * width, width), width)


def attention_forward_kernel(joined, last, *refs):
    refs = iter(refs)

    def take(number):
        return [next(refs) for _ in range(number)]

    parts = take(6 if joined else 1)
    gains, weights, cosine, sine, seg_col, seg_row, mixing, previous, routes, gather = take(10)
    d_result = take(1) if last else None
    hidden = take(1)[0] if joined else parts[0]
    normed, query, keys, values, log_total, attended, middle, mixed_low = take(8)
    logits, coefs, rows, bias, held, arrived = take(6)
    copies = [
        pltpu.make_async_copy(weights.at[block], held.at[block], arrived.at[block])
        for block in range(4)
    ]
    for copy in copies:
        copy.start()
    weights = held
    if joined:
        combine_kernel(*parts, hidden)
    tokens, features = hidden.shape
    h = hidden[...].astype(F32)
    normed[...] = (h * inverse_rms(h) * gains[0:1]).astype(BF16)
    bias[...] = attention_bias(seg_col, seg_row)
    wide = 2 * LANES
    for block, out in ((0, query), (1, keys)):
        copies[block].wait()

        @pl.loop(0, features // wide)
        def _(step):
            part = dot(normed[...], weights[block, :, columns_of(step, wide)])
            for k in range(2):
                turned = turn(part[:, k * LANES : (k + 1) * LANES], cosine[...], sine[...])
                out[:, columns_of(2 * step + k, LANES)] = turned.astype(BF16)

    copies[2].wait()

    @pl.loop(0, features // wide)
    def _(step):
        at = columns_of(step, wide)
        values[:, at] = dot(normed[...], weights[2, :, at]).astype(BF16)

    log_total[...] = jnp.zeros_like(log_total)

    @pl.loop(0, features // LANES)
    def _(step):
        at = columns_of(step, LANES)
        q, k, v = query[:, at], keys[:, at], values[:, at]
        lane = lax.broadcasted_iota(jnp.int32, log_total.shape, 1)
        total_out = jnp.zeros((tokens, LANES), F32)
        for half, mask in enumerate(head_masks(q.shape)):
            scores = dot(jnp.where(mask, q, 0), k, ((1,), (1,))) * SCALE + bias[...]
            top = jnp.max(scores, axis=-1, keepdims=True)
            weight = jnp.exp(scores - top)
            total = jnp.sum(weight, axis=-1, keepdims=True)
            probs = (weight * (1.0 / total)).astype(BF16)
            total_out += dot(probs, jnp.where(mask, v, 0))
            log_total[...] = jnp.where(
                lane == step * (LANES // HEAD_DIM) + half, top + jnp.log(total), log_total[...]
            )
        attended[:, at] = total_out.astype(BF16)

    copies[3].wait()

    @pl.loop(0, features // wide)
    def _(step):
        at = columns_of(step, wide)
        middle[:, at] = hidden[:, at].astype(F32) + dot(attended[...], weights[3, :, at])

    m = middle[...]
    low = (m * inverse_rms(m) * gains[1:2]).astype(BF16)
    mixed_low[...] = low
    rows[:, :features] = dot(gather[0] + gather[1], low).astype(BF16)
    raw = dot(low, mixing[...])
    lane = lax.broadcasted_iota(jnp.int32, raw.shape, 1)
    now = jnp.where(lane < EXPERTS, raw + previous[...], 0.0)
    logits[...] = now
    route = [routes[:, k : k + 1] for k in range(TOP)]
    chosen = [lane_pick(now, lane, route[k]) for k in range(TOP)]
    best = jnp.maximum(chosen[0], chosen[1])
    chosen = [jnp.exp(c - best) for c in chosen]
    gates = [c / (chosen[0] + chosen[1]) for c in chosen]
    shares = []
    for c in range(NCONST):
        pair = [lane_pick(raw, lane, EXPERTS + 2 * c + i) for i in range(2)]
        best = jnp.maximum(pair[0], pair[1])
        pair = [jnp.exp(p - best) for p in pair]
        shares.append([p / (pair[0] + pair[1]) for p in pair])
    copies = [(route[k] == EF + 1).astype(F32) for k in range(TOP)]
    consts = [[(route[k] == EF + 2 + c).astype(F32) for c in range(NCONST)] for k in range(TOP)]
    weight = [sum(consts[k][c] * gates[k] for k in range(TOP)) for c in range(NCONST)]
    columns = list(gates)
    columns += [
        copies[k] + sum(consts[k][c] * shares[c][0] for c in range(NCONST)) for k in range(TOP)
    ]
    columns += [consts[k][c] * shares[c][1] for k in range(TOP) for c in range(NCONST)]
    columns += [shares[c][i] for c in range(NCONST) for i in range(2)]
    columns += weight
    columns += [
        sum(copies[k] * gates[k] for k in range(TOP))
        + sum(shares[c][0] * weight[c] for c in range(NCONST))
    ]
    columns += [shares[c][1] * weight[c] for c in range(NCONST)]
    packed = jnp.zeros_like(raw)
    for index, column in enumerate(columns):
        packed = jnp.where(lane == index, column, packed)
    coefs[...] = packed
    if last:
        rows[:, features:] = value_rows(gates, gather, d_result[0])


GATE, MIXED, VECTOR, SHARE, WEIGHT, DIRECT, CONST = 0, 2, 4, 8, 12, 14, 15


def combine_kernel(coefs, middle, gains, scatter, outputs, vectors, result):
    coef = coefs[...]
    m = middle[...]
    total = m + coef[:, DIRECT : DIRECT + 1] * (m * inverse_rms(m) * gains[1:2])
    for k in range(TOP):
        total += coef[:, GATE + k : GATE + k + 1] * dot(scatter[k], outputs[:, : m.shape[1]])
    for c in range(NCONST):
        total += coef[:, CONST + c : CONST + c + 1] * vectors[c : c + 1]
    result[...] = total


def value_rows(gates, gather, d_result):
    return sum(
        dot(gather[k], (gates[k] * d_result[...]).astype(BF16)) for k in range(TOP)
    ).astype(BF16)


def two_parts(x):
    high = x.astype(BF16)
    return high, (x - high.astype(F32)).astype(BF16)


def gate_backward_kernel(
    coefs, middle, gains, scatter, outputs, vectors, routes, mixed_low, mixing_t, d_result, d_next,
    d_logits, d_mixed, grads,
):
    coef = coefs[...]
    m = middle[...]
    dh = d_result[...]
    lane = lax.broadcasted_iota(jnp.int32, coef.shape, 1)

    def column(index):
        return coef[:, index : index + 1]

    along = jnp.sum(m * inverse_rms(m) * gains[1:2] * dh, axis=-1, keepdims=True)
    with_vector = [
        jnp.sum(dh * vectors[c : c + 1], axis=-1, keepdims=True) for c in range(NCONST)
    ]
    d_gates = []
    for k in range(TOP):
        value = jnp.sum(dot(scatter[k], outputs[:, : dh.shape[1]]) * dh, axis=-1, keepdims=True)
        value += column(MIXED + k) * along
        value += sum(column(VECTOR + k * NCONST + c) * with_vector[c] for c in range(NCONST))
        d_gates.append(value)
    mean = sum(column(GATE + k) * d_gates[k] for k in range(TOP))
    terms = d_next[...]
    for k in range(TOP):
        chosen = column(GATE + k) * (d_gates[k] - mean)
        terms += jnp.where(lane == routes[:, k : k + 1], chosen, 0.0)
    d_logits[...] = terms
    vector_terms = jnp.zeros_like(terms)
    for c in range(NCONST):
        share = [column(SHARE + 2 * c + i) for i in range(2)]
        d_share = [column(WEIGHT + c) * along, column(WEIGHT + c) * with_vector[c]]
        mean = share[0] * d_share[0] + share[1] * d_share[1]
        for i in range(2):
            terms = jnp.where(
                lane == EXPERTS + 2 * c + i, share[i] * (d_share[i] - mean), terms
            )
        vector_terms = jnp.where(
            lane == EXPERTS + 2 * NCONST + c, column(CONST + c), vector_terms
        )
    high, lowest = two_parts(terms)
    d_mixed[...] = column(DIRECT) * dh + dot(high, mixing_t[...]) + dot(lowest, mixing_t[...])
    both = ((0,), (0,))
    total = dot(high, mixed_low[...], both) + dot(lowest, mixed_low[...], both)
    high, lowest = two_parts(vector_terms)
    dh_high, dh_low = two_parts(dh)
    total += dot(high, dh_high, both) + dot(lowest, dh_high, both) + dot(high, dh_low, both)
    grads[...] = total[: grads.shape[0]]


def expert_forward_kernel(inputs, w_gate_up, w_down, gate_up, activated, own, others):
    units = w_down.shape[0]
    wide = min(2 * LANES, units)
    kept = own.shape[0]

    @pl.loop(0, units // wide)
    def _(step):
        at = columns_of(step, wide)
        gate = dot(inputs[...], w_gate_up[:, at])
        up_at = pl.ds(pl.multiple_of(units + step * wide, wide), wide)
        up = dot(inputs[...], w_gate_up[:, up_at])
        gate_up[:, at] = gate
        gate_up[:, up_at] = up
        activated[:, at] = (gate / (1.0 + jnp.exp(-gate)) * up).astype(BF16)

    @pl.loop(0, w_down.shape[1] // (2 * LANES))
    def _(step):
        at = columns_of(step, 2 * LANES)
        out = dot(activated[...], w_down[:, at])
        own[:, at] = out[:kept]
        others[:, at] = out[kept:].astype(BF16)


def expert_backward_kernel(d_expert, w_gate_up, w_down, gate_up, d_gate_up, own, others):
    units = w_down.shape[0]
    wide = min(2 * LANES, units)
    kept = own.shape[0]

    @pl.loop(0, units // wide)
    def _(step):
        at = columns_of(step, wide)
        up_at = pl.ds(pl.multiple_of(units + step * wide, wide), wide)
        d_active = dot(d_expert[...], w_down[at, :], ((1,), (1,)))
        gate, up = gate_up[:, at], gate_up[:, up_at]
        sigmoid = 1.0 / (1.0 + jnp.exp(-gate))
        d_gate_up[:, at] = (
            d_active * up * sigmoid * (1.0 + gate * (1.0 - sigmoid))
        ).astype(BF16)
        d_gate_up[:, up_at] = (d_active * gate * sigmoid).astype(BF16)

    @pl.loop(0, w_gate_up.shape[0] // (2 * LANES))
    def _(step):
        at = columns_of(step, 2 * LANES)
        out = dot(d_gate_up[...], w_gate_up[at, :], ((1,), (1,)))
        own[:, at] = out[:kept]
        others[:, at] = out[kept:].astype(BF16)


def expert_both_kernel(
    rows, w_gate_up, w_down, d_gate_up, activated, own, others, gate_up
):
    features, units = w_gate_up.shape[0], w_down.shape[0]
    wide = min(2 * LANES, units)
    kept = own.shape[0]

    @pl.loop(0, units // wide)
    def _(step):
        at = columns_of(step, wide)
        up_at = pl.ds(pl.multiple_of(units + step * wide, wide), wide)
        gate_up[:, :wide] = dot(rows[:, :features], w_gate_up[:, at])
        gate_up[:, wide:] = dot(rows[:, :features], w_gate_up[:, up_at])
        d_active = dot(rows[:, features:], w_down[at, :], ((1,), (1,)))
        gate, up = gate_up[:, :wide], gate_up[:, wide:]
        sigmoid = 1.0 / (1.0 + jnp.exp(-gate))
        activated[:, at] = (gate * sigmoid * up).astype(BF16)
        d_gate_up[:, at] = (
            d_active * up * sigmoid * (1.0 + gate * (1.0 - sigmoid))
        ).astype(BF16)
        d_gate_up[:, up_at] = (d_active * gate * sigmoid).astype(BF16)

    @pl.loop(0, features // (2 * LANES))
    def _(step):
        at = columns_of(step, 2 * LANES)
        out = dot(activated[...], w_down[:, at])
        own[:, at] = out[:kept]
        others[:, at] = out[kept:].astype(BF16)
        out = dot(d_gate_up[...], w_gate_up[at, :], ((1,), (1,)))
        to = pl.ds(pl.multiple_of(features + step * 2 * LANES, 2 * LANES), 2 * LANES)
        own[:, to] = out[:kept]
        others[:, to] = out[kept:].astype(BF16)


def norm_backward(grad, source, gain):
    inverse = inverse_rms(source)
    scaled = grad * gain
    gain_grad = jnp.sum(grad * source * inverse, axis=0, keepdims=True)
    mean = jnp.mean(scaled * source, axis=-1, keepdims=True)
    return inverse * scaled - source * (inverse * inverse * inverse * mean), gain_grad


def attention_backward_kernel(more, *refs):
    refs = iter(refs)

    def take(number):
        return [next(refs) for _ in range(number)]

    d_result, d_mixed, d_rows, scatter, middle, hidden, gains, weights = take(8)
    cosine, sine, seg_col, seg_row, query, keys, values, log_total = take(8)
    coefs, gather = take(2) if more else (None, None)
    d_hidden, d_branch, d_projected, gain_grads = take(4)
    rows = take(1)[0] if more else None
    bias, d_attended, d_normed, held, arrived = take(5)
    copies = [
        pltpu.make_async_copy(weights.at[block], held.at[block], arrived.at[block])
        for block in range(4)
    ]
    for copy in copies[::-1]:
        copy.start()
    weights = held
    tokens, features = hidden.shape
    wide = 2 * LANES
    total = d_mixed[...] + dot(
        scatter[0] + scatter[1], d_rows[:, d_rows.shape[1] - features :]
    )
    d_middle, gain_grad = norm_backward(total, middle[...], gains[1:2])
    d_middle = d_middle + d_result[...]
    gain_grads[1:2] = gain_grad
    d_hidden[...] = d_middle
    d_branch[...] = d_middle.astype(BF16)
    bias[...] = attention_bias(seg_col, seg_row)
    copies[3].wait()

    @pl.loop(0, features // wide)
    def _(step):
        at = columns_of(step, wide)
        d_attended[:, at] = dot(d_branch[...], weights[3, at, :], ((1,), (1,))).astype(BF16)

    @pl.loop(0, features // LANES)
    def _(step):
        at = columns_of(step, LANES)
        q, k, v, da = query[:, at], keys[:, at], values[:, at], d_attended[:, at]
        lane = lax.broadcasted_iota(jnp.int32, log_total.shape, 1)
        zero = jnp.zeros((tokens, LANES), F32)
        dq, dk, dv = zero, zero, zero
        for half, mask in enumerate(head_masks(q.shape)):
            q_half, da_half = jnp.where(mask, q, 0), jnp.where(mask, da, 0)
            scores = dot(q_half, k, ((1,), (1,))) * SCALE + bias[...]
            shift = lane_pick(log_total[...], lane, step * (LANES // HEAD_DIM) + half)
            probs = jnp.exp(scores - shift)
            dv += dot(probs.astype(BF16), da_half, ((0,), (0,)))
            d_probs = dot(da_half, v, ((1,), (1,)))
            mean = jnp.sum(d_probs * probs, axis=-1, keepdims=True)
            d_scores = (probs * (d_probs - mean)).astype(BF16)
            dq += dot(d_scores, jnp.where(mask, k, 0))
            dk += dot(d_scores, q_half, ((0,), (0,)))
        d_projected[0, :, at] = turn(dq * SCALE, cosine[...], -sine[...]).astype(BF16)
        d_projected[1, :, at] = turn(dk * SCALE, cosine[...], -sine[...]).astype(BF16)
        d_projected[2, :, at] = dv.astype(BF16)

    for copy in copies[:3]:
        copy.wait()

    @pl.loop(0, features // wide)
    def _(step):
        at = columns_of(step, wide)
        d_normed[:, at] = sum(
            dot(d_projected[b], weights[b, at, :], ((1,), (1,))) for b in range(3)
        )

    d_input, gain_grad = norm_backward(d_normed[...], hidden[...].astype(F32), gains[0:1])
    gain_grads[0:1] = gain_grad
    d_hidden[...] += d_input
    if more:
        gates = [coefs[:, GATE + k : GATE + k + 1] for k in range(TOP)]
        rows[...] = value_rows(gates, gather, d_hidden)


def cost(micros):
    return pl.CostEstimate(flops=0, bytes_accessed=int(micros * 3.6e6), transcendentals=0)


def call(kernel, outs, args, scratch=(), apart=None, micros=5):
    specs = [
        pl.BlockSpec(memory_space=pl.ANY) if k == apart else pl.BlockSpec()
        for k in range(len(args))
    ]
    scratch = [pltpu.VMEM(shape, dtype) for shape, dtype in scratch]
    if apart is not None:
        scratch += [
            pltpu.VMEM(args[apart].shape, args[apart].dtype),
            pltpu.SemaphoreType.DMA((4,)),
        ]
    return pl.pallas_call(
        kernel,
        out_shape=[jax.ShapeDtypeStruct(shape, dtype) for shape, dtype in outs],
        in_specs=specs,
        scratch_shapes=scratch,
        compiler_params=pltpu.CompilerParams(vmem_limit_bytes=60 * 1024 * 1024),
        cost_estimate=cost(micros),
    )(*args)


def after(x, *others):
    return lax.optimization_barrier((x,) + others)[0]


class Layout:
    def __init__(self, mesh):
        self.reps, self.shards = mesh.shape["rep"], mesh.shape["shard"]
        self.lines = self.shards // EF
        assert self.shards % EF == 0 and EF % self.reps == 0

    def pairs(self, move):
        found = []
        for rep in range(self.reps):
            for shard in range(self.shards):
                r, z, j = move(rep, shard // EF, shard % EF)
                found.append((rep * self.shards + shard, r * self.shards + z * EF + j))
        return found

    def send(self, x, move):
        return lax.ppermute(x, AXES, self.pairs(move))

    def expert_move(self, mask, shift):
        def move(r, z, j):
            number = r * EF + j
            e, f = (number // self.reps) ^ mask, (number % self.reps + shift) % self.reps
            number = e * self.reps + f
            return number // EF, z, number % EF

        return move

    def place(self):
        rep, shard = lax.axis_index("rep"), lax.axis_index("shard")
        j = shard % EF
        return rep, j, (rep * EF + j) // self.reps

    def quad_exchange(self, blocks, j):
        got = lax.dynamic_update_slice_in_dim(
            jnp.zeros_like(blocks), lax.dynamic_slice_in_dim(blocks, j, 1, 0), j, 0
        )
        for mask in range(1, EF):
            other = j ^ mask
            block = lax.dynamic_slice_in_dim(blocks, other, 1, 0)
            block = self.send(block, lambda r, z, q: (r, z, q ^ mask))
            got = lax.dynamic_update_slice_in_dim(got, block, other, 0)
        return got

    def part_exchange(self, blocks, j):
        count = EF // self.reps
        mine = j // self.reps
        got = lax.dynamic_update_slice_in_dim(
            jnp.zeros_like(blocks), lax.dynamic_slice_in_dim(blocks, mine, 1, 0), mine, 0
        )
        for mask in range(1, count):
            other = mine ^ mask
            block = lax.dynamic_slice_in_dim(blocks, other, 1, 0)
            block = self.send(block, lambda r, z, q: (r, z, q ^ (mask * self.reps)))
            got = lax.dynamic_update_slice_in_dim(got, block, other, 0)
        return got

    def rep_gather(self, x, rep):
        got = lax.dynamic_update_slice_in_dim(
            jnp.zeros((self.reps,) + x.shape, x.dtype), x[None], rep, 0
        )
        for shift in range(1, self.reps):
            block = self.send(x, lambda r, z, q: ((r + shift) % self.reps, z, q))
            got = lax.dynamic_update_slice_in_dim(
                got, block[None], (rep + self.reps - shift) % self.reps, 0
            )
        return got

    def trade(self, blocks, chosen):
        groups = [
            [(n // EF) * self.shards + z * EF + n % EF for n in numbers]
            for z in range(self.lines)
            for numbers in chosen
        ]
        return lax.all_to_all(blocks, AXES, 0, 0, axis_index_groups=groups, tiled=True)

    def return_gate_up(self, blocks):
        return self.trade(
            jnp.concatenate([blocks] * self.reps), [list(range(self.reps * EF))]
        )

    def return_down(self, blocks):
        return self.trade(
            jnp.concatenate([blocks] * self.reps),
            [[e * self.reps + f for e in range(EF)] for f in range(self.reps)],
        )

    def line_groups(self):
        return [[z * EF + j for z in range(self.lines)] for j in range(EF)]

    def line_gather(self, x):
        return lax.all_gather(
            x, "shard", axis=0, tiled=True, axis_index_groups=self.line_groups()
        )

    def line_sum(self, x):
        return lax.psum_scatter(
            x, "shard", scatter_dimension=0, tiled=True, axis_index_groups=self.line_groups()
        )

    def dense_line(self, x):
        line = [x[None]]
        for shift in range(1, self.lines):
            line.append(self.send(x, lambda r, q, k: (r, (q + shift) % self.lines, k))[None])
        return jnp.concatenate(line)

    def dense_gather(self, line):
        reps, lines = self.reps, self.lines
        cut = lines // 2

        def over_rep(block, shift):
            return self.send(block, lambda r, q, k: ((r + shift) % reps, q, k))

        def over_high(block):
            return self.send(block, lambda r, q, k: (r, q, k ^ 2))

        sides = [over_rep(line, shift) for shift in range(1, reps)]
        flip = over_high(line)
        pieces = [(line, 0, 0, 0), (flip, 0, 0, 1)]
        for shift, block in enumerate(sides, 1):
            pieces.append((block, 0, shift, 0))
            pieces.append((over_high(block[:cut]), 0, shift, 1))
            pieces.append((over_rep(flip[cut:], shift), cut, shift, 1))
        pieces = [piece + (0,) for piece in pieces if piece[0].shape[0]]
        others = [
            (self.send(piece[0], lambda r, q, k: (r, q, k ^ 1)),) + piece[1:4] + (1,)
            for piece in pieces
        ]
        return pieces + others

    def assemble(self, pieces, where, count):
        reps, lines = self.reps, self.lines
        rows, features = pieces[0][0].shape[1:]
        slim = features // self.shards
        extra = rows - count * slim
        notes = [piece[1:] for piece in pieces]

        def kernel(where_ref, *refs):
            out = refs[len(pieces)]
            rep, z, high, core = [where_ref[k] for k in range(4)]
            for ref, (start, back, flip, other) in zip(refs, notes):
                r = lax.rem(rep + reps - back, reps)
                hi = high if flip == 0 else 1 - high
                lo = core if other == 0 else 1 - core
                for step in range(ref.shape[0]):
                    at = lax.rem(z + lines - start - step, lines)
                    for k in range(count):
                        out[r, k, at, hi, lo] = ref[step, k * slim : (k + 1) * slim]
                    if extra and back == 0:
                        refs[-1][at, hi, lo] = ref[step, count * slim :]

        shapes = [jax.ShapeDtypeStruct((reps, count, lines, 2, 2, slim, features), BF16)]
        if extra:
            shapes.append(jax.ShapeDtypeStruct((lines, 2, 2, extra, features), BF16))
        return pl.pallas_call(
            kernel,
            out_shape=shapes,
            in_specs=[pl.BlockSpec(memory_space=pltpu.SMEM)]
            + [pl.BlockSpec(memory_space=pltpu.VMEM)] * len(pieces),
            out_specs=[pl.BlockSpec(memory_space=pltpu.VMEM)] * len(shapes),
            compiler_params=pltpu.CompilerParams(vmem_limit_bytes=60 * 1024 * 1024),
            cost_estimate=cost(4),
        )(where, *[piece[0] for piece in pieces])

    def over_rep(self, block, shift):
        return self.send(block, lambda r, q, k: ((r + shift) % self.reps, q, k))

    def sum_core(self, terms, core):
        mine = lax.dynamic_slice_in_dim(terms, core, 1, 0)[0]
        other = lax.dynamic_slice_in_dim(terms, 1 - core, 1, 0)[0]
        other = self.send(other, lambda r, q, k: (r, q, k ^ 1))
        return (mine.astype(F32) + other.astype(F32)).astype(BF16)

    def rep_step(self, x, rep):
        total = lax.dynamic_slice_in_dim(x, rep, 1, 0)[0].astype(F32)
        for shift in range(1, self.reps):
            block = lax.dynamic_slice_in_dim(x, (rep + shift) % self.reps, 1, 0)[0]
            total = total + self.over_rep(block, shift).astype(F32)
        return total.astype(BF16)

    def high_step(self, x, high, axis):
        mine = lax.dynamic_slice_in_dim(x, high, 1, axis)
        other = lax.dynamic_slice_in_dim(x, 1 - high, 1, axis)
        other = self.send(other, lambda r, q, k: (r, q, k ^ 2))
        return jnp.squeeze(mine.astype(F32) + other.astype(F32), axis).astype(BF16)

    def sum_cross(self, both, rep, j):
        cut = self.lines // 2
        return self.high_step(both[:, :cut], j // 2, 2), self.rep_step(both[:, cut:], rep)

    def sum_cross_end(self, first, second, rep, j):
        return jnp.concatenate([self.rep_step(first, rep), self.high_step(second, j // 2, 1)])

    def sum_line(self, line):
        z = lax.axis_index("shard") // EF
        lines = self.lines
        total = lax.dynamic_slice_in_dim(line, z, 1, 0)[0].astype(F32)
        for shift in range(1, lines):
            block = lax.dynamic_slice_in_dim(line, (z + shift) % lines, 1, 0)[0]
            block = self.send(block, lambda r, q, k: (r, (q + shift) % lines, k))
            total = total + block.astype(F32)
        return total.astype(BF16)

    def dispatch(self, rows):
        blocks = rows.reshape(EF, CAP, -1)
        own = jnp.stack(
            [blocks[0]] + [self.send(blocks[m], self.expert_move(m, 0)) for m in range(1, EF)]
        )
        parts = [own] + [self.send(own, self.expert_move(0, g)) for g in range(1, self.reps)]
        return jnp.concatenate(parts).reshape(self.reps * EF * CAP, -1)

    def collect(self, own, others):
        total = own
        for g in range(1, self.reps):
            block = others[(g - 1) * EF * CAP : g * EF * CAP]
            total = total + self.send(block, self.expert_move(0, self.reps - g)).astype(F32)
        total = total.astype(BF16).reshape(EF, CAP, -1)
        return jnp.concatenate(
            [total[0]] + [self.send(total[m], self.expert_move(m, 0)) for m in range(1, EF)]
        )


def split_gate_up(layout, w_gate_up, layer, where):
    _, experts, rows, columns = w_gate_up.shape
    width = columns // (2 * layout.shards)
    parts = layout.reps
    per = layout.shards // parts

    def kernel(where_ref, x, o):
        for j in range(EF):
            e = where_ref[0] * (EF // layout.reps) + j // parts
            for b in range(2 * per):
                at = (b * parts + j % parts) * width
                o[j, :, b * width : (b + 1) * width] = x[0, e, :, at : at + width]

    return pl.pallas_call(
        kernel,
        grid=(1,),
        out_shape=jax.ShapeDtypeStruct((EF, rows, columns // parts), BF16),
        in_specs=[
            pl.BlockSpec(memory_space=pltpu.SMEM),
            pl.BlockSpec((1, experts, rows, columns), lambda _: (layer, 0, 0, 0)),
        ],
        out_specs=pl.BlockSpec((EF, rows, columns // parts), lambda _: (0, 0, 0)),
        compiler_params=pltpu.CompilerParams(vmem_limit_bytes=60 * 1024 * 1024),
        cost_estimate=cost(4),
    )(where, w_gate_up)


def expert_weights(layout, w_gate_up, w_down, layer, rep, j, where):
    count = EF // layout.reps
    mine = layout.quad_exchange(split_gate_up(layout, w_gate_up, layer, where), j)
    mine = mine.reshape(-1, mine.shape[-1])
    down = lax.dynamic_slice_in_dim(w_down[layer], rep * count, count, 0)
    down = layout.part_exchange(down, j)
    down = down.reshape(-1, down.shape[-1])
    return layout.line_gather(mine), layout.line_gather(down), down


def dense_gradients(layout, terms, small, count):
    tokens, features = terms[0].shape
    lines, slim = layout.lines, features // layout.shards
    wide = 2 * LANES

    def kernel(normed, attended, d_projected, d_branch, small_ref, out, turned):
        turned[0] = normed[...].T
        turned[1] = attended[...].T
        for block in range(4):
            r, k = block // count, block % count

            @pl.loop(0, features // wide)
            def _(step):
                at = columns_of(step, wide)
                grad = d_branch[:, at] if block == 3 else d_projected[block, :, at]
                term = dot(turned[block // 3], grad).astype(BF16)
                for s in range(layout.shards):
                    out[s % 2, r, s // EF, s // 2 % 2, k * slim : (k + 1) * slim, at] = term[
                        s * slim : (s + 1) * slim
                    ]

        for s in range(layout.shards):
            for r in range(layout.reps):
                out[s % 2, r, s // EF, s // 2 % 2, count * slim :] = small_ref[s]

    shape = (2, layout.reps, lines, 2, count * slim + ROWS, features)
    return call(kernel, [(shape, BF16)], (*terms, small), [((2, features, tokens), BF16)], micros=8)[0]


def store_layer(kernel, source, block, index, shape, layer, held):
    spec = pl.BlockSpec((1, 1) + shape[2:], lambda e: (layer, e) + (0,) * (len(shape) - 2))
    whole = [] if held is None else [held]
    return pl.pallas_call(
        (lambda x, o: kernel(x, o)) if held is None else (lambda x, h, o: kernel(x, o)),
        grid=(shape[1],),
        out_shape=jax.ShapeDtypeStruct(shape, F32),
        in_specs=[pl.BlockSpec(block, index)] + [pl.BlockSpec(memory_space=pl.ANY)] * len(whole),
        out_specs=spec,
        input_output_aliases={} if held is None else {1: 0},
        compiler_params=pltpu.CompilerParams(vmem_limit_bytes=60 * 1024 * 1024),
        cost_estimate=cost(4),
    )(source, *whole)


def store_gate_up(layout, source, shape, layer, held):
    width = shape[3] // (2 * layout.shards)
    per = layout.shards // layout.reps

    def kernel(x, o):
        for half in range(2):
            for b in range(per):
                for f in range(layout.reps):
                    start = ((half * per + b) * layout.reps + f) * width
                    at = (half * per + b) * width
                    o[0, 0, :, start : start + width] = x[0, f, :, at : at + width].astype(F32)

    block = (1,) + source.shape[1:]
    return store_layer(kernel, source, block, lambda e: (e, 0, 0, 0), shape, layer, held)


def store_down(source, shape, layer, held):
    def kernel(x, o):
        o[...] = x[...].astype(F32)

    block = (1, 1) + source.shape[2:]
    return store_layer(kernel, source, block, lambda e: (0, e, 0, 0), shape, layer, held)


def place_pairs(routes, priority, expert):
    flat = routes.reshape(-1)
    ahead = (flat[:, None] == flat[None, :]) & (priority[:, None] < priority[None, :])
    position = jnp.sum(ahead.astype(jnp.int32), axis=0)
    kept = (flat < EF) & (position < CAP)
    slot = jnp.where(kept, (flat ^ expert) * CAP + position, EF * CAP).reshape(-1, TOP).T
    places = jnp.arange(EF * CAP, dtype=jnp.int32)
    gather = (places[None, :, None] == slot[:, None, :]).astype(BF16)
    scatter = (places[None, None, :] == slot[:, :, None]).astype(BF16)
    return gather, scatter


def attention_forward(shared, dense, source, previous, routes, gather, d_result):
    gains, weights, mixing = dense
    tokens, features = source[1 if len(source) > 1 else 0].shape
    joined, last = len(source) > 1, d_result is not None
    low = ((tokens, features), BF16)
    full = ((tokens, features), F32)
    lanes = ((tokens, LANES), F32)
    found = call(
        functools.partial(attention_forward_kernel, joined, last),
        [full] * joined
        + [low, low, low, low, lanes, low, full, low, lanes, lanes]
        + [((gather.shape[1], features * (2 if last else 1)), BF16)],
        (*source, gains, weights, *shared, mixing, previous, routes, gather)
        + ((d_result,) if last else ()),
        [((tokens, tokens), F32)],
        len(source) + 1,
        12,
    )
    return found if joined else [source[0], *found]


def expert_both(rows, w_gate_up, w_down):
    count, double = rows.shape
    units = w_down.shape[0]
    return call(
        expert_both_kernel,
        [((count, 2 * units), BF16), ((count, units), BF16)]
        + [((EF * CAP, double), F32), ((count - EF * CAP, double), BF16)],
        (rows, w_gate_up, w_down),
        [((count, 2 * min(2 * LANES, units)), F32)],
        micros=12,
    )


def expert_forward(layout, inputs, w_gate_up, w_down):
    count, features = inputs.shape
    units = w_down.shape[0]
    return call(
        expert_forward_kernel,
        [((count, 2 * units), F32), ((count, units), BF16)]
        + [((EF * CAP, features), F32), ((count - EF * CAP, features), BF16)],
        (inputs, w_gate_up, w_down),
        micros=10,
    )


def expert_backward(layout, d_expert, w_gate_up, w_down, gate_up):
    count, features = d_expert.shape
    units = w_down.shape[0]
    return call(
        expert_backward_kernel,
        [((count, 2 * units), BF16)]
        + [((EF * CAP, features), F32), ((count - EF * CAP, features), BF16)],
        (d_expert, w_gate_up, w_down, gate_up),
        micros=10,
    )


def local(
    layout,
    hidden_in,
    gate_in,
    routes,
    priority,
    segments,
    norm_attn,
    w_qkv,
    w_out,
    norm_moe,
    w_router,
    w_const,
    const_vec,
    w_gate_up,
    w_down,
    grad_out,
):
    layers = w_qkv.shape[0]
    tokens, features = hidden_in.shape
    rep, j, expert = layout.place()
    slim = w_qkv.shape[1]
    small = [
        jnp.concatenate(
            [norm_attn[l][:, None], norm_moe[l][:, None], w_router[l], w_const[l], const_vec[l].T],
            axis=-1,
        ).reshape(1, -1)
        for l in range(layers)
    ]
    small = jnp.concatenate(small, axis=-1)
    extra = ROWS * features
    small = jnp.pad(small, ((0, 0), (0, extra - small.shape[1]))).reshape(ROWS, features)
    count = EF // layout.reps
    shard = lax.axis_index("shard")
    where = jnp.stack([rep, shard // EF, j // 2, j % 2]).astype(jnp.int32)

    group = rep.reshape(1).astype(jnp.int32)

    def share(l, *more):
        blocks = jnp.concatenate(
            [jnp.transpose(w_qkv[l].reshape(slim, 3, features), (1, 0, 2)), w_out[l][None]]
        )
        mine = lax.dynamic_slice_in_dim(blocks, rep * count, count, 0)
        return jnp.concatenate([mine.reshape(count * slim, features), *more])

    def dense_weights(x):
        full = layout.assemble(layout.dense_gather(x), where, count)
        return full[0].reshape(4, features, features), *full[1:]

    line = layout.dense_line(share(0, small))
    *found, last = expert_weights(layout, after(w_gate_up, line), w_down, 0, rep, j, group)
    moe = [found]
    full, small_full = dense_weights(after(line, last))
    small_full = small_full.reshape(layout.shards, -1)
    dense = [full]
    packs, vectors, mixing_t = [], [], []
    for l in range(layers):
        part = small_full[:, l * slim * SMALL : (l + 1) * slim * SMALL]
        part = part.reshape(features, SMALL)
        mixing = part[:, 2 : SMALL - NCONST]
        mixing = jnp.pad(mixing, ((0, 0), (0, LANES - mixing.shape[1])))
        packs.append([part[:, :2].T.astype(F32), None, mixing])
        mixing_t.append(mixing.T)
        vectors.append(part[:, SMALL - NCONST :].T.astype(F32))

    shared = (*rope_tables(tokens), segments.reshape(-1, 1), segments)
    pairs = [place_pairs(routes[l], priority[l, 0], expert) for l in range(layers)]

    source = (hidden_in,)
    previous = jnp.pad(gate_in, ((0, 0), (0, LANES - EXPERTS)))
    kept = []
    for l in range(layers):
        gather, scatter = pairs[l]
        packs[l][1] = dense[l]
        last = l + 1 == layers
        state = attention_forward(
            shared, packs[l], source, previous, routes[l], gather, grad_out if last else None
        )
        middle, logits, coefs, rows = state[7], state[9], state[10], state[11]
        inputs = layout.dispatch(rows)
        if last:
            d_gate_up, activated, own, others = expert_both(inputs, *moe[l])
            wide = dot(inputs[:, :features], d_gate_up, ((0,), (0,))).astype(BF16)
            down = dot(activated, inputs[:, features:], ((0,), (0,))).astype(BF16)
        else:
            dense.append(dense_weights(layout.dense_line(after(share(l + 1), rows)))[0])
            raw = after((w_gate_up, w_down), rows)
            moe.append(expert_weights(layout, *raw, l + 1, rep, j, group)[:2])
            gate_up, activated, own, others = expert_forward(layout, inputs, *moe[l])
        outputs = layout.collect(own, others)
        if last:
            outputs, wide, down = lax.optimization_barrier((outputs, wide, down))
        source = (coefs, middle, packs[l][0], scatter, outputs, vectors[l])
        previous = logits
        kept.append((state, inputs, gate_up, activated, outputs))
    (result,) = call(combine_kernel, [((tokens, features), F32)], source)

    grad_hidden = grad_out
    grad_gate = jnp.zeros_like(previous)
    join = lax.optimization_barrier

    def back_down(x):
        return layout.return_down(x.reshape(count, -1, features))

    def back_gate_up(x):
        return layout.return_gate_up(x.reshape(EF, -1, x.shape[-1]))

    def put_down(x, l, held):
        return store_down(x[None], (layers, EF) + w_down.shape[2:], l, held)

    def put_gate_up(x, l, held):
        x = x.reshape((EF, layout.reps) + x.shape[1:])
        return store_gate_up(layout, x, (layers, EF) + w_gate_up.shape[2:], l, held)

    boths, wides, downs = [None] * layers, [None] * layers, [None] * layers
    gate_up_out, down_out = None, None
    for l in reversed(range(layers)):
        gather, scatter = pairs[l]
        state, inputs, gate_up, activated, outputs = kept[l]
        hidden, normed, query, keys, values, log_total, attended, middle, low = state[:9]
        coefs = state[10]
        last = l + 1 == layers
        if not last:
            d_expert = layout.dispatch(rows)
        grad_gate, d_mixed, mix_grads = call(
            gate_backward_kernel,
            [((tokens, LANES), F32), ((tokens, features), F32), ((SMALL - 2, features), F32)],
            (coefs, middle, packs[l][0], scatter, outputs, vectors[l], routes[l], low)
            + (mixing_t[l], grad_hidden, grad_gate),
            micros=6,
        )
        if last:
            d_rows = outputs
            wides[l], downs[l] = layout.line_sum(wide), layout.line_sum(down)
        else:
            d_expert, d_mixed = join((d_expert, d_mixed))
            down = back_down(after(downs[l + 1], d_expert))
            d_gate_up, own, others = expert_backward(layout, d_expert, *moe[l], gate_up)
            own, down = join((own, down))
            down_out = put_down(down, l + 1, down_out)
            grad_gate_up = dot(inputs, d_gate_up, ((0,), (0,))).astype(BF16)
            d_rows = layout.collect(own, others)
            boths[l + 1] = layout.sum_core(
                dense_gradients(layout, *after(ready, own), count), j % 2
            )
            grad_down = dot(activated, d_expert, ((0,), (0,))).astype(BF16)
            d_rows, grad_gate_up, grad_down, boths[l + 1], down_out = join(
                (d_rows, grad_gate_up, grad_down, boths[l + 1], down_out)
            )
            wides[l], downs[l] = layout.line_sum(grad_gate_up), layout.line_sum(grad_down)
        more = () if l == 0 else (kept[l - 1][0][10], pairs[l - 1][0])
        grad_hidden, d_branch, d_projected, gain_grads, *rows = call(
            functools.partial(attention_backward_kernel, l > 0),
            [((tokens, features), F32), ((tokens, features), BF16)]
            + [((3, tokens, features), BF16), ((2, features), F32)]
            + [((gather.shape[1], features), BF16)] * (l > 0),
            (grad_hidden, d_mixed, d_rows, scatter, middle, hidden, packs[l][0], packs[l][1])
            + (*shared, query, keys, values, log_total, *more),
            [((tokens, tokens), F32), ((tokens, features), BF16), ((tokens, features), F32)],
            7,
            14,
        )
        rows = rows[0] if rows else None
        if not last:
            wide = back_gate_up(after(wides[l + 1], d_branch))
        small_grads = jnp.concatenate([gain_grads, mix_grads]).T.astype(BF16)
        small_grads = small_grads.reshape(layout.shards, slim * SMALL)
        small_grads = jnp.pad(small_grads, ((0, 0), (0, ROWS * features - slim * SMALL)))
        ready = (
            (normed, attended, d_projected, d_branch),
            small_grads.reshape(layout.shards, ROWS, features),
        )

    boths[0] = layout.sum_core(dense_gradients(layout, *ready, count), j % 2)
    boths[0], wide = join((boths[0], wide))
    gate_up_out = put_gate_up(wide, 1, gate_up_out)
    both = jnp.concatenate(boths, axis=3)
    cross, gate_up_out, down = join(
        (layout.sum_cross(both, rep, j), gate_up_out, back_down(after(downs[0], both)))
    )
    line = layout.sum_cross_end(*cross, rep, j)
    line, wides[0] = join((line, wides[0]))
    down_out = put_down(down, 0, down_out)
    line, wide, gate_up_out, down_out, result = join(
        (layout.sum_line(line), back_gate_up(wides[0]), gate_up_out, down_out, result)
    )
    gate_up_out = put_gate_up(wide, 0, gate_up_out)
    dense_all = layout.rep_gather(line, rep).reshape(layout.reps, layers, -1, features)
    dense_grads = jnp.swapaxes(dense_all, 0, 1)
    dense_all = dense_grads.astype(F32)
    small_all = dense_all[:, 0, count * slim :].reshape(layers, -1)[:, : slim * SMALL]
    small_all = small_all.reshape(layers, slim, SMALL)
    dense_all = dense_all[:, :, : count * slim].reshape(layers, 4, slim, features)
    qkv_all = jnp.transpose(dense_all[:, :3], (0, 2, 1, 3)).reshape(layers, slim, 3 * features)
    return (
        result.astype(BF16),
        grad_hidden,
        grad_gate[:, :EXPERTS],
        small_all[:, :, 0],
        qkv_all,
        dense_all[:, 3],
        small_all[:, :, 1],
        small_all[:, :, 2 : 2 + EXPERTS],
        small_all[:, :, 2 + EXPERTS : SMALL - NCONST],
        jnp.transpose(small_all[:, :, SMALL - NCONST :], (0, 2, 1)),
        gate_up_out,
        down_out,
    )


def solution(mesh):
    return jax.shard_map(
        functools.partial(local, Layout(mesh)),
        mesh=mesh,
        in_specs=(
            P(("rep", "shard"), None),
            P(("rep", "shard"), None),
            P(None, ("rep", "shard"), None),
            P(None, ("rep", "shard"), None),
            P(("rep", "shard"), None),
            P(None, "shard"),
            P(None, "shard", None),
            P(None, "shard", None),
            P(None, "shard"),
            P(None, "shard", None),
            P(None, "shard", None),
            P(None, None, "shard"),
            P(None, None, "shard", None),
            P(None, None, "shard", None),
            P(("rep", "shard"), None),
        ),
        out_specs=(
            P(("rep", "shard"), None),
            P(("rep", "shard"), None),
            P(("rep", "shard"), None),
            P(None, "shard"),
            P(None, "shard", None),
            P(None, "shard", None),
            P(None, "shard"),
            P(None, "shard", None),
            P(None, "shard", None),
            P(None, None, "shard"),
            P(None, None, "shard", None),
            P(None, None, "shard", None),
        ),
        check_vma=False,
    )
```

```python
import functools
import math

import jax
import jax.numpy as jnp
from jax import lax
from jax.experimental import pallas as pl
from jax.experimental.pallas import tpu as pltpu
from jax.sharding import PartitionSpec as P

HEAD_DIM = 64
EF = 4
NCONST = 2
TOP = 2
EXPERTS = 8
CAP = 80
SMALL = 2 + EXPERTS + 2 * NCONST + NCONST
ROWS = 16
LANES = 128

EPSILON = 1e-06
SCALE = 0.125
MASKED = -1000000000.0
AXES = ("rep", "shard")
BF16 = jnp.bfloat16
F32 = jnp.float32


def dot(a, b, dims=((1,), (0,))):
    return lax.dot_general(a, b, (dims, ((), ())), preferred_element_type=F32)


def rope_tables(tokens):
    half = HEAD_DIM // 2
    places = jnp.arange(tokens, dtype=jnp.int32).astype(F32)[:, None]
    powers = jnp.arange(half, dtype=jnp.int32).astype(F32) / half
    angles = places * jnp.exp(-math.log(10000.0) * powers)[None, :]
    cosine, sine = jnp.cos(angles), jnp.sin(angles)
    heads = LANES // HEAD_DIM
    return jnp.tile(cosine, (1, 2 * heads)), jnp.tile(
        jnp.concatenate([-sine, sine], axis=-1), (1, heads)
    )


def turn(block, cosine, sine):
    half = HEAD_DIM // 2
    lane = lax.broadcasted_iota(jnp.int32, block.shape, 1)
    width = block.shape[1]
    partner = jnp.where(
        lane % HEAD_DIM < half,
        pltpu.roll(block, width - half, 1),
        pltpu.roll(block, half, 1),
    )
    return block * cosine + partner * sine


def lane_pick(array, lane, index):
    return jnp.sum(jnp.where(lane == index, array, 0.0), axis=-1, keepdims=True)


def inverse_rms(x):
    return lax.rsqrt(jnp.mean(x * x, axis=-1, keepdims=True) + EPSILON)


def attention_bias(seg_col, seg_row):
    shape = (seg_col.shape[0], seg_row.shape[1])
    rows = lax.broadcasted_iota(jnp.int32, shape, 0)
    columns = lax.broadcasted_iota(jnp.int32, shape, 1)
    allowed = (seg_col[...] == seg_row[...]) & (columns <= rows)
    return jnp.where(allowed, 0.0, MASKED)


def head_masks(shape):
    lane = lax.broadcasted_iota(jnp.int32, shape, 1)
    return [(lane // HEAD_DIM) == half for half in range(LANES // HEAD_DIM)]


def columns_of(step, width):
    return pl.ds(pl.multiple_of(step * width, width), width)


def attention_forward_kernel(joined, last, *refs):
    refs = iter(refs)

    def take(number):
        return [next(refs) for _ in range(number)]

    parts = take(6 if joined else 1)
    gains, weights, cosine, sine, seg_col, seg_row, mixing, previous, routes, gather = take(10)
    d_result = take(1) if last else None
    hidden = take(1)[0] if joined else parts[0]
    normed, query, keys, values, log_total, attended, middle, mixed_low = take(8)
    logits, coefs, rows, bias, held, arrived = take(6)
    copies = [
        pltpu.make_async_copy(weights.at[block], held.at[block], arrived.at[block])
        for block in range(4)
    ]
    for copy in copies:
        copy.start()
    weights = held
    if joined:
        combine_kernel(*parts, hidden)
    tokens, features = hidden.shape
    h = hidden[...].astype(F32)
    normed[...] = (h * inverse_rms(h) * gains[0:1]).astype(BF16)
    bias[...] = attention_bias(seg_col, seg_row)
    wide = 2 * LANES
    for block, out in ((0, query), (1, keys)):
        copies[block].wait()

        @pl.loop(0, features // wide)
        def _(step):
            part = dot(normed[...], weights[block, :, columns_of(step, wide)])
            for k in range(2):
                turned = turn(part[:, k * LANES : (k + 1) * LANES], cosine[...], sine[...])
                out[:, columns_of(2 * step + k, LANES)] = turned.astype(BF16)

    copies[2].wait()

    @pl.loop(0, features // wide)
    def _(step):
        at = columns_of(step, wide)
        values[:, at] = dot(normed[...], weights[2, :, at]).astype(BF16)

    log_total[...] = jnp.zeros_like(log_total)

    @pl.loop(0, features // LANES)
    def _(step):
        at = columns_of(step, LANES)
        q, k, v = query[:, at], keys[:, at], values[:, at]
        lane = lax.broadcasted_iota(jnp.int32, log_total.shape, 1)
        total_out = jnp.zeros((tokens, LANES), F32)
        for half, mask in enumerate(head_masks(q.shape)):
            scores = dot(jnp.where(mask, q, 0), k, ((1,), (1,))) * SCALE + bias[...]
            top = jnp.max(scores, axis=-1, keepdims=True)
            weight = jnp.exp(scores - top)
            total = jnp.sum(weight, axis=-1, keepdims=True)
            probs = (weight * (1.0 / total)).astype(BF16)
            total_out += dot(probs, jnp.where(mask, v, 0))
            log_total[...] = jnp.where(
                lane == step * (LANES // HEAD_DIM) + half, top + jnp.log(total), log_total[...]
            )
        attended[:, at] = total_out.astype(BF16)

    copies[3].wait()

    @pl.loop(0, features // wide)
    def _(step):
        at = columns_of(step, wide)
        middle[:, at] = hidden[:, at].astype(F32) + dot(attended[...], weights[3, :, at])

    m = middle[...]
    low = (m * inverse_rms(m) * gains[1:2]).astype(BF16)
    mixed_low[...] = low
    rows[:, :features] = dot(gather[0] + gather[1], low).astype(BF16)
    raw = dot(low, mixing[...])
    lane = lax.broadcasted_iota(jnp.int32, raw.shape, 1)
    now = jnp.where(lane < EXPERTS, raw + previous[...], 0.0)
    logits[...] = now
    route = [routes[:, k : k + 1] for k in range(TOP)]
    chosen = [lane_pick(now, lane, route[k]) for k in range(TOP)]
    best = jnp.maximum(chosen[0], chosen[1])
    chosen = [jnp.exp(c - best) for c in chosen]
    gates = [c / (chosen[0] + chosen[1]) for c in chosen]
    shares = []
    for c in range(NCONST):
        pair = [lane_pick(raw, lane, EXPERTS + 2 * c + i) for i in range(2)]
        best = jnp.maximum(pair[0], pair[1])
        pair = [jnp.exp(p - best) for p in pair]
        shares.append([p / (pair[0] + pair[1]) for p in pair])
    copies = [(route[k] == EF + 1).astype(F32) for k in range(TOP)]
    consts = [[(route[k] == EF + 2 + c).astype(F32) for c in range(NCONST)] for k in range(TOP)]
    weight = [sum(consts[k][c] * gates[k] for k in range(TOP)) for c in range(NCONST)]
    columns = list(gates)
    columns += [
        copies[k] + sum(consts[k][c] * shares[c][0] for c in range(NCONST)) for k in range(TOP)
    ]
    columns += [consts[k][c] * shares[c][1] for k in range(TOP) for c in range(NCONST)]
    columns += [shares[c][i] for c in range(NCONST) for i in range(2)]
    columns += weight
    columns += [
        sum(copies[k] * gates[k] for k in range(TOP))
        + sum(shares[c][0] * weight[c] for c in range(NCONST))
    ]
    columns += [shares[c][1] * weight[c] for c in range(NCONST)]
    packed = jnp.zeros_like(raw)
    for index, column in enumerate(columns):
        packed = jnp.where(lane == index, column, packed)
    coefs[...] = packed
    if last:
        rows[:, features:] = value_rows(gates, gather, d_result[0])


GATE, MIXED, VECTOR, SHARE, WEIGHT, DIRECT, CONST = 0, 2, 4, 8, 12, 14, 15


def combine_kernel(coefs, middle, gains, scatter, outputs, vectors, result):
    coef = coefs[...]
    m = middle[...]
    total = m + coef[:, DIRECT : DIRECT + 1] * (m * inverse_rms(m) * gains[1:2])
    for k in range(TOP):
        total += coef[:, GATE + k : GATE + k + 1] * dot(scatter[k], outputs[:, : m.shape[1]])
    for c in range(NCONST):
        total += coef[:, CONST + c : CONST + c + 1] * vectors[c : c + 1]
    result[...] = total


def value_rows(gates, gather, d_result):
    return sum(
        dot(gather[k], (gates[k] * d_result[...]).astype(BF16)) for k in range(TOP)
    ).astype(BF16)


def two_parts(x):
    high = x.astype(BF16)
    return high, (x - high.astype(F32)).astype(BF16)


def gate_backward_kernel(
    coefs, middle, gains, scatter, outputs, vectors, routes, mixed_low, mixing_t, d_result, d_next,
    d_logits, d_mixed, grads,
):
    coef = coefs[...]
    m = middle[...]
    dh = d_result[...]
    lane = lax.broadcasted_iota(jnp.int32, coef.shape, 1)

    def column(index):
        return coef[:, index : index + 1]

    along = jnp.sum(m * inverse_rms(m) * gains[1:2] * dh, axis=-1, keepdims=True)
    with_vector = [
        jnp.sum(dh * vectors[c : c + 1], axis=-1, keepdims=True) for c in range(NCONST)
    ]
    d_gates = []
    for k in range(TOP):
        value = jnp.sum(dot(scatter[k], outputs[:, : dh.shape[1]]) * dh, axis=-1, keepdims=True)
        value += column(MIXED + k) * along
        value += sum(column(VECTOR + k * NCONST + c) * with_vector[c] for c in range(NCONST))
        d_gates.append(value)
    mean = sum(column(GATE + k) * d_gates[k] for k in range(TOP))
    terms = d_next[...]
    for k in range(TOP):
        chosen = column(GATE + k) * (d_gates[k] - mean)
        terms += jnp.where(lane == routes[:, k : k + 1], chosen, 0.0)
    d_logits[...] = terms
    vector_terms = jnp.zeros_like(terms)
    for c in range(NCONST):
        share = [column(SHARE + 2 * c + i) for i in range(2)]
        d_share = [column(WEIGHT + c) * along, column(WEIGHT + c) * with_vector[c]]
        mean = share[0] * d_share[0] + share[1] * d_share[1]
        for i in range(2):
            terms = jnp.where(
                lane == EXPERTS + 2 * c + i, share[i] * (d_share[i] - mean), terms
            )
        vector_terms = jnp.where(
            lane == EXPERTS + 2 * NCONST + c, column(CONST + c), vector_terms
        )
    high, lowest = two_parts(terms)
    d_mixed[...] = column(DIRECT) * dh + dot(high, mixing_t[...]) + dot(lowest, mixing_t[...])
    both = ((0,), (0,))
    total = dot(high, mixed_low[...], both) + dot(lowest, mixed_low[...], both)
    high, lowest = two_parts(vector_terms)
    dh_high, dh_low = two_parts(dh)
    total += dot(high, dh_high, both) + dot(lowest, dh_high, both) + dot(high, dh_low, both)
    grads[...] = total[: grads.shape[0]]


def expert_forward_kernel(inputs, w_gate_up, w_down, gate_up, activated, own, others):
    units = w_down.shape[0]
    wide = min(2 * LANES, units)
    kept = own.shape[0]

    @pl.loop(0, units // wide)
    def _(step):
        at = columns_of(step, wide)
        gate = dot(inputs[...], w_gate_up[:, at])
        up_at = pl.ds(pl.multiple_of(units + step * wide, wide), wide)
        up = dot(inputs[...], w_gate_up[:, up_at])
        gate_up[:, at] = gate
        gate_up[:, up_at] = up
        activated[:, at] = (gate / (1.0 + jnp.exp(-gate)) * up).astype(BF16)

    @pl.loop(0, w_down.shape[1] // (2 * LANES))
    def _(step):
        at = columns_of(step, 2 * LANES)
        out = dot(activated[...], w_down[:, at])
        own[:, at] = out[:kept]
        others[:, at] = out[kept:].astype(BF16)


def expert_backward_kernel(d_expert, w_gate_up, w_down, gate_up, d_gate_up, own, others):
    units = w_down.shape[0]
    wide = min(2 * LANES, units)
    kept = own.shape[0]

    @pl.loop(0, units // wide)
    def _(step):
        at = columns_of(step, wide)
        up_at = pl.ds(pl.multiple_of(units + step * wide, wide), wide)
        d_active = dot(d_expert[...], w_down[at, :], ((1,), (1,)))
        gate, up = gate_up[:, at], gate_up[:, up_at]
        sigmoid = 1.0 / (1.0 + jnp.exp(-gate))
        d_gate_up[:, at] = (
            d_active * up * sigmoid * (1.0 + gate * (1.0 - sigmoid))
        ).astype(BF16)
        d_gate_up[:, up_at] = (d_active * gate * sigmoid).astype(BF16)

    @pl.loop(0, w_gate_up.shape[0] // (2 * LANES))
    def _(step):
        at = columns_of(step, 2 * LANES)
        out = dot(d_gate_up[...], w_gate_up[at, :], ((1,), (1,)))
        own[:, at] = out[:kept]
        others[:, at] = out[kept:].astype(BF16)


def expert_both_kernel(
    rows, w_gate_up, w_down, d_gate_up, activated, own, others, gate_up
):
    features, units = w_gate_up.shape[0], w_down.shape[0]
    wide = min(2 * LANES, units)
    kept = own.shape[0]

    @pl.loop(0, units // wide)
    def _(step):
        at = columns_of(step, wide)
        up_at = pl.ds(pl.multiple_of(units + step * wide, wide), wide)
        gate_up[:, :wide] = dot(rows[:, :features], w_gate_up[:, at])
        gate_up[:, wide:] = dot(rows[:, :features], w_gate_up[:, up_at])
        d_active = dot(rows[:, features:], w_down[at, :], ((1,), (1,)))
        gate, up = gate_up[:, :wide], gate_up[:, wide:]
        sigmoid = 1.0 / (1.0 + jnp.exp(-gate))
        activated[:, at] = (gate * sigmoid * up).astype(BF16)
        d_gate_up[:, at] = (
            d_active * up * sigmoid * (1.0 + gate * (1.0 - sigmoid))
        ).astype(BF16)
        d_gate_up[:, up_at] = (d_active * gate * sigmoid).astype(BF16)

    @pl.loop(0, features // (2 * LANES))
    def _(step):
        at = columns_of(step, 2 * LANES)
        out = dot(activated[...], w_down[:, at])
        own[:, at] = out[:kept]
        others[:, at] = out[kept:].astype(BF16)
        out = dot(d_gate_up[...], w_gate_up[at, :], ((1,), (1,)))
        to = pl.ds(pl.multiple_of(features + step * 2 * LANES, 2 * LANES), 2 * LANES)
        own[:, to] = out[:kept]
        others[:, to] = out[kept:].astype(BF16)


def norm_backward(grad, source, gain):
    inverse = inverse_rms(source)
    scaled = grad * gain
    gain_grad = jnp.sum(grad * source * inverse, axis=0, keepdims=True)
    mean = jnp.mean(scaled * source, axis=-1, keepdims=True)
    return inverse * scaled - source * (inverse * inverse * inverse * mean), gain_grad


def attention_backward_kernel(more, *refs):
    refs = iter(refs)

    def take(number):
        return [next(refs) for _ in range(number)]

    d_result, d_mixed, d_rows, scatter, middle, hidden, gains, weights = take(8)
    cosine, sine, seg_col, seg_row, query, keys, values, log_total = take(8)
    coefs, gather = take(2) if more else (None, None)
    d_hidden, d_branch, d_projected, gain_grads = take(4)
    rows = take(1)[0] if more else None
    bias, d_attended, d_normed, held, arrived = take(5)
    copies = [
        pltpu.make_async_copy(weights.at[block], held.at[block], arrived.at[block])
        for block in range(4)
    ]
    for copy in copies[::-1]:
        copy.start()
    weights = held
    tokens, features = hidden.shape
    wide = 2 * LANES
    total = d_mixed[...] + dot(
        scatter[0] + scatter[1], d_rows[:, d_rows.shape[1] - features :]
    )
    d_middle, gain_grad = norm_backward(total, middle[...], gains[1:2])
    d_middle = d_middle + d_result[...]
    gain_grads[1:2] = gain_grad
    d_hidden[...] = d_middle
    d_branch[...] = d_middle.astype(BF16)
    bias[...] = attention_bias(seg_col, seg_row)
    copies[3].wait()

    @pl.loop(0, features // wide)
    def _(step):
        at = columns_of(step, wide)
        d_attended[:, at] = dot(d_branch[...], weights[3, at, :], ((1,), (1,))).astype(BF16)

    @pl.loop(0, features // LANES)
    def _(step):
        at = columns_of(step, LANES)
        q, k, v, da = query[:, at], keys[:, at], values[:, at], d_attended[:, at]
        lane = lax.broadcasted_iota(jnp.int32, log_total.shape, 1)
        zero = jnp.zeros((tokens, LANES), F32)
        dq, dk, dv = zero, zero, zero
        for half, mask in enumerate(head_masks(q.shape)):
            q_half, da_half = jnp.where(mask, q, 0), jnp.where(mask, da, 0)
            scores = dot(q_half, k, ((1,), (1,))) * SCALE + bias[...]
            shift = lane_pick(log_total[...], lane, step * (LANES // HEAD_DIM) + half)
            probs = jnp.exp(scores - shift)
            dv += dot(probs.astype(BF16), da_half, ((0,), (0,)))
            d_probs = dot(da_half, v, ((1,), (1,)))
            mean = jnp.sum(d_probs * probs, axis=-1, keepdims=True)
            d_scores = (probs * (d_probs - mean)).astype(BF16)
            dq += dot(d_scores, jnp.where(mask, k, 0))
            dk += dot(d_scores, q_half, ((0,), (0,)))
        d_projected[0, :, at] = turn(dq * SCALE, cosine[...], -sine[...]).astype(BF16)
        d_projected[1, :, at] = turn(dk * SCALE, cosine[...], -sine[...]).astype(BF16)
        d_projected[2, :, at] = dv.astype(BF16)

    for copy in copies[:3]:
        copy.wait()

    @pl.loop(0, features // wide)
    def _(step):
        at = columns_of(step, wide)
        d_normed[:, at] = sum(
            dot(d_projected[b], weights[b, at, :], ((1,), (1,))) for b in range(3)
        )

    d_input, gain_grad = norm_backward(d_normed[...], hidden[...].astype(F32), gains[0:1])
    gain_grads[0:1] = gain_grad
    d_hidden[...] += d_input
    if more:
        gates = [coefs[:, GATE + k : GATE + k + 1] for k in range(TOP)]
        rows[...] = value_rows(gates, gather, d_hidden)


def cost(micros):
    return pl.CostEstimate(flops=0, bytes_accessed=int(micros * 3.6e6), transcendentals=0)


def call(kernel, outs, args, scratch=(), apart=None, micros=5):
    specs = [
        pl.BlockSpec(memory_space=pl.ANY) if k == apart else pl.BlockSpec()
        for k in range(len(args))
    ]
    scratch = [pltpu.VMEM(shape, dtype) for shape, dtype in scratch]
    if apart is not None:
        scratch += [
            pltpu.VMEM(args[apart].shape, args[apart].dtype),
            pltpu.SemaphoreType.DMA((4,)),
        ]
    return pl.pallas_call(
        kernel,
        out_shape=[jax.ShapeDtypeStruct(shape, dtype) for shape, dtype in outs],
        in_specs=specs,
        scratch_shapes=scratch,
        compiler_params=pltpu.CompilerParams(vmem_limit_bytes=60 * 1024 * 1024),
        cost_estimate=cost(micros),
    )(*args)


def after(x, *others):
    return lax.optimization_barrier((x,) + others)[0]


class Layout:
    def __init__(self, mesh):
        self.reps, self.shards = mesh.shape["rep"], mesh.shape["shard"]
        self.lines = self.shards // EF
        assert self.shards % EF == 0 and EF % self.reps == 0

    def pairs(self, move):
        found = []
        for rep in range(self.reps):
            for shard in range(self.shards):
                r, z, j = move(rep, shard // EF, shard % EF)
                found.append((rep * self.shards + shard, r * self.shards + z * EF + j))
        return found

    def send(self, x, move):
        return lax.ppermute(x, AXES, self.pairs(move))

    def expert_move(self, mask, shift):
        def move(r, z, j):
            number = r * EF + j
            e, f = (number // self.reps) ^ mask, (number % self.reps + shift) % self.reps
            number = e * self.reps + f
            return number // EF, z, number % EF

        return move

    def place(self):
        rep, shard = lax.axis_index("rep"), lax.axis_index("shard")
        j = shard % EF
        return rep, j, (rep * EF + j) // self.reps

    def quad_exchange(self, blocks, j):
        got = lax.dynamic_update_slice_in_dim(
            jnp.zeros_like(blocks), lax.dynamic_slice_in_dim(blocks, j, 1, 0), j, 0
        )
        for mask in range(1, EF):
            other = j ^ mask
            block = lax.dynamic_slice_in_dim(blocks, other, 1, 0)
            block = self.send(block, lambda r, z, q: (r, z, q ^ mask))
            got = lax.dynamic_update_slice_in_dim(got, block, other, 0)
        return got

    def part_exchange(self, blocks, j):
        count = EF // self.reps
        mine = j // self.reps
        got = lax.dynamic_update_slice_in_dim(
            jnp.zeros_like(blocks), lax.dynamic_slice_in_dim(blocks, mine, 1, 0), mine, 0
        )
        for mask in range(1, count):
            other = mine ^ mask
            block = lax.dynamic_slice_in_dim(blocks, other, 1, 0)
            block = self.send(block, lambda r, z, q: (r, z, q ^ (mask * self.reps)))
            got = lax.dynamic_update_slice_in_dim(got, block, other, 0)
        return got

    def rep_gather(self, x, rep):
        got = lax.dynamic_update_slice_in_dim(
            jnp.zeros((self.reps,) + x.shape, x.dtype), x[None], rep, 0
        )
        for shift in range(1, self.reps):
            block = self.send(x, lambda r, z, q: ((r + shift) % self.reps, z, q))
            got = lax.dynamic_update_slice_in_dim(
                got, block[None], (rep + self.reps - shift) % self.reps, 0
            )
        return got

    def trade(self, blocks, chosen):
        groups = [
            [(n // EF) * self.shards + z * EF + n % EF for n in numbers]
            for z in range(self.lines)
            for numbers in chosen
        ]
        return lax.all_to_all(blocks, AXES, 0, 0, axis_index_groups=groups, tiled=True)

    def return_gate_up(self, blocks):
        return self.trade(
            jnp.concatenate([blocks] * self.reps), [list(range(self.reps * EF))]
        )

    def return_down(self, blocks):
        return self.trade(
            jnp.concatenate([blocks] * self.reps),
            [[e * self.reps + f for e in range(EF)] for f in range(self.reps)],
        )

    def line_groups(self):
        return [[z * EF + j for z in range(self.lines)] for j in range(EF)]

    def line_gather(self, x):
        return lax.all_gather(
            x, "shard", axis=0, tiled=True, axis_index_groups=self.line_groups()
        )

    def line_sum(self, x):
        return lax.psum_scatter(
            x, "shard", scatter_dimension=0, tiled=True, axis_index_groups=self.line_groups()
        )

    def dense_line(self, x):
        line = [x[None]]
        for shift in range(1, self.lines):
            line.append(self.send(x, lambda r, q, k: (r, (q + shift) % self.lines, k))[None])
        return jnp.concatenate(line)

    def dense_gather(self, line):
        reps, lines = self.reps, self.lines
        cut = lines // 2

        def over_rep(block, shift):
            return self.send(block, lambda r, q, k: ((r + shift) % reps, q, k))

        def over_high(block):
            return self.send(block, lambda r, q, k: (r, q, k ^ 2))

        sides = [over_rep(line, shift) for shift in range(1, reps)]
        flip = over_high(line)
        pieces = [(line, 0, 0, 0), (flip, 0, 0, 1)]
        for shift, block in enumerate(sides, 1):
            pieces.append((block, 0, shift, 0))
            pieces.append((over_high(block[:cut]), 0, shift, 1))
            pieces.append((over_rep(flip[cut:], shift), cut, shift, 1))
        pieces = [piece + (0,) for piece in pieces if piece[0].shape[0]]
        others = [
            (self.send(piece[0], lambda r, q, k: (r, q, k ^ 1)),) + piece[1:4] + (1,)
            for piece in pieces
        ]
        return pieces + others

    def assemble(self, pieces, where, count):
        reps, lines = self.reps, self.lines
        rows, features = pieces[0][0].shape[1:]
        slim = features // self.shards
        extra = rows - count * slim
        notes = [piece[1:] for piece in pieces]

        def kernel(where_ref, *refs):
            out = refs[len(pieces)]
            rep, z, high, core = [where_ref[k] for k in range(4)]
            for ref, (start, back, flip, other) in zip(refs, notes):
                r = lax.rem(rep + reps - back, reps)
                hi = high if flip == 0 else 1 - high
                lo = core if other == 0 else 1 - core
                for step in range(ref.shape[0]):
                    at = lax.rem(z + lines - start - step, lines)
                    for k in range(count):
                        out[r, k, at, hi, lo] = ref[step, k * slim : (k + 1) * slim]
                    if extra and back == 0:
                        refs[-1][at, hi, lo] = ref[step, count * slim :]

        shapes = [jax.ShapeDtypeStruct((reps, count, lines, 2, 2, slim, features), BF16)]
        if extra:
            shapes.append(jax.ShapeDtypeStruct((lines, 2, 2, extra, features), BF16))
        return pl.pallas_call(
            kernel,
            out_shape=shapes,
            in_specs=[pl.BlockSpec(memory_space=pltpu.SMEM)]
            + [pl.BlockSpec(memory_space=pltpu.VMEM)] * len(pieces),
            out_specs=[pl.BlockSpec(memory_space=pltpu.VMEM)] * len(shapes),
            compiler_params=pltpu.CompilerParams(vmem_limit_bytes=60 * 1024 * 1024),
            cost_estimate=cost(4),
        )(where, *[piece[0] for piece in pieces])

    def over_rep(self, block, shift):
        return self.send(block, lambda r, q, k: ((r + shift) % self.reps, q, k))

    def sum_core(self, terms, core):
        mine = lax.dynamic_slice_in_dim(terms, core, 1, 0)[0]
        other = lax.dynamic_slice_in_dim(terms, 1 - core, 1, 0)[0]
        other = self.send(other, lambda r, q, k: (r, q, k ^ 1))
        return (mine.astype(F32) + other.astype(F32)).astype(BF16)

    def rep_step(self, x, rep):
        total = lax.dynamic_slice_in_dim(x, rep, 1, 0)[0].astype(F32)
        for shift in range(1, self.reps):
            block = lax.dynamic_slice_in_dim(x, (rep + shift) % self.reps, 1, 0)[0]
            total = total + self.over_rep(block, shift).astype(F32)
        return total.astype(BF16)

    def high_step(self, x, high, axis):
        mine = lax.dynamic_slice_in_dim(x, high, 1, axis)
        other = lax.dynamic_slice_in_dim(x, 1 - high, 1, axis)
        other = self.send(other, lambda r, q, k: (r, q, k ^ 2))
        return jnp.squeeze(mine.astype(F32) + other.astype(F32), axis).astype(BF16)

    def sum_cross(self, both, rep, j):
        cut = self.lines // 2
        return self.high_step(both[:, :cut], j // 2, 2), self.rep_step(both[:, cut:], rep)

    def sum_cross_end(self, first, second, rep, j):
        return jnp.concatenate([self.rep_step(first, rep), self.high_step(second, j // 2, 1)])

    def sum_line(self, line):
        z = lax.axis_index("shard") // EF
        lines = self.lines
        total = lax.dynamic_slice_in_dim(line, z, 1, 0)[0].astype(F32)
        for shift in range(1, lines):
            block = lax.dynamic_slice_in_dim(line, (z + shift) % lines, 1, 0)[0]
            block = self.send(block, lambda r, q, k: (r, (q + shift) % lines, k))
            total = total + block.astype(F32)
        return total.astype(BF16)

    def dispatch(self, rows):
        blocks = rows.reshape(EF, CAP, -1)
        own = jnp.stack(
            [blocks[0]] + [self.send(blocks[m], self.expert_move(m, 0)) for m in range(1, EF)]
        )
        parts = [own] + [self.send(own, self.expert_move(0, g)) for g in range(1, self.reps)]
        return jnp.concatenate(parts).reshape(self.reps * EF * CAP, -1)

    def collect(self, own, others):
        total = own
        for g in range(1, self.reps):
            block = others[(g - 1) * EF * CAP : g * EF * CAP]
            total = total + self.send(block, self.expert_move(0, self.reps - g)).astype(F32)
        total = total.astype(BF16).reshape(EF, CAP, -1)
        return jnp.concatenate(
            [total[0]] + [self.send(total[m], self.expert_move(m, 0)) for m in range(1, EF)]
        )


def split_gate_up(layout, w_gate_up, layer, where):
    _, experts, rows, columns = w_gate_up.shape
    width = columns // (2 * layout.shards)
    parts = layout.reps
    per = layout.shards // parts

    def kernel(where_ref, x, o):
        for j in range(EF):
            e = where_ref[0] * (EF // layout.reps) + j // parts
            for b in range(2 * per):
                at = (b * parts + j % parts) * width
                o[j, :, b * width : (b + 1) * width] = x[0, e, :, at : at + width]

    return pl.pallas_call(
        kernel,
        grid=(1,),
        out_shape=jax.ShapeDtypeStruct((EF, rows, columns // parts), BF16),
        in_specs=[
            pl.BlockSpec(memory_space=pltpu.SMEM),
            pl.BlockSpec((1, experts, rows, columns), lambda _: (layer, 0, 0, 0)),
        ],
        out_specs=pl.BlockSpec((EF, rows, columns // parts), lambda _: (0, 0, 0)),
        compiler_params=pltpu.CompilerParams(vmem_limit_bytes=60 * 1024 * 1024),
        cost_estimate=cost(4),
    )(where, w_gate_up)


def expert_weights(layout, w_gate_up, w_down, layer, rep, j, where):
    count = EF // layout.reps
    mine = layout.quad_exchange(split_gate_up(layout, w_gate_up, layer, where), j)
    mine = mine.reshape(-1, mine.shape[-1])
    down = lax.dynamic_slice_in_dim(w_down[layer], rep * count, count, 0)
    down = layout.part_exchange(down, j)
    down = down.reshape(-1, down.shape[-1])
    return layout.line_gather(mine), layout.line_gather(down), down


def dense_gradients(layout, terms, small, count):
    tokens, features = terms[0].shape
    lines, slim = layout.lines, features // layout.shards
    wide = 2 * LANES
    extra = () if small is None else (small,)

    def kernel(normed, attended, d_projected, d_branch, *refs):
        out, turned = refs[-2:]
        turned[0] = normed[...].T
        turned[1] = attended[...].T
        for block in range(4):
            r, k = block // count, block % count

            @pl.loop(0, features // wide)
            def _(step):
                at = columns_of(step, wide)
                grad = d_branch[:, at] if block == 3 else d_projected[block, :, at]
                term = dot(turned[block // 3], grad).astype(BF16)
                for s in range(layout.shards):
                    out[s % 2, r, s // EF, s // 2 % 2, k * slim : (k + 1) * slim, at] = term[
                        s * slim : (s + 1) * slim
                    ]

        for s in range(layout.shards if extra else 0):
            for r in range(layout.reps):
                out[s % 2, r, s // EF, s // 2 % 2, count * slim :] = refs[0][s]

    shape = (2, layout.reps, lines, 2, count * slim + ROWS * len(extra), features)
    return call(kernel, [(shape, BF16)], (*terms, *extra), [((2, features, tokens), BF16)], micros=8)[0]


def store_layer(kernel, source, block, index, shape, layer, held):
    spec = pl.BlockSpec((1, 1) + shape[2:], lambda e: (layer, e) + (0,) * (len(shape) - 2))
    whole = [] if held is None else [held]
    return pl.pallas_call(
        (lambda x, o: kernel(x, o)) if held is None else (lambda x, h, o: kernel(x, o)),
        grid=(shape[1],),
        out_shape=jax.ShapeDtypeStruct(shape, F32),
        in_specs=[pl.BlockSpec(block, index)] + [pl.BlockSpec(memory_space=pl.ANY)] * len(whole),
        out_specs=spec,
        input_output_aliases={} if held is None else {1: 0},
        compiler_params=pltpu.CompilerParams(vmem_limit_bytes=60 * 1024 * 1024),
        cost_estimate=cost(4),
    )(source, *whole)


def store_gate_up(layout, source, shape, layer, held):
    width = shape[3] // (2 * layout.shards)
    per = layout.shards // layout.reps

    def kernel(x, o):
        for half in range(2):
            for b in range(per):
                for f in range(layout.reps):
                    start = ((half * per + b) * layout.reps + f) * width
                    at = (half * per + b) * width
                    o[0, 0, :, start : start + width] = x[0, f, :, at : at + width].astype(F32)

    block = (1,) + source.shape[1:]
    return store_layer(kernel, source, block, lambda e: (e, 0, 0, 0), shape, layer, held)


def store_down(source, shape, layer, held):
    def kernel(x, o):
        o[...] = x[...].astype(F32)

    block = (1, 1) + source.shape[2:]
    return store_layer(kernel, source, block, lambda e: (0, e, 0, 0), shape, layer, held)


def place_pairs(routes, priority, expert):
    flat = routes.reshape(-1)
    ahead = (flat[:, None] == flat[None, :]) & (priority[:, None] < priority[None, :])
    position = jnp.sum(ahead.astype(jnp.int32), axis=0)
    kept = (flat < EF) & (position < CAP)
    slot = jnp.where(kept, (flat ^ expert) * CAP + position, EF * CAP).reshape(-1, TOP).T
    places = jnp.arange(EF * CAP, dtype=jnp.int32)
    gather = (places[None, :, None] == slot[:, None, :]).astype(BF16)
    scatter = (places[None, None, :] == slot[:, :, None]).astype(BF16)
    return gather, scatter


def attention_forward(shared, dense, source, previous, routes, gather, d_result):
    gains, weights, mixing = dense
    tokens, features = source[1 if len(source) > 1 else 0].shape
    joined, last = len(source) > 1, d_result is not None
    low = ((tokens, features), BF16)
    full = ((tokens, features), F32)
    lanes = ((tokens, LANES), F32)
    found = call(
        functools.partial(attention_forward_kernel, joined, last),
        [full] * joined
        + [low, low, low, low, lanes, low, full, low, lanes, lanes]
        + [((gather.shape[1], features * (2 if last else 1)), BF16)],
        (*source, gains, weights, *shared, mixing, previous, routes, gather)
        + ((d_result,) if last else ()),
        [((tokens, tokens), F32)],
        len(source) + 1,
        12,
    )
    return found if joined else [source[0], *found]


def expert_both(rows, w_gate_up, w_down):
    count, double = rows.shape
    units = w_down.shape[0]
    return call(
        expert_both_kernel,
        [((count, 2 * units), BF16), ((count, units), BF16)]
        + [((EF * CAP, double), F32), ((count - EF * CAP, double), BF16)],
        (rows, w_gate_up, w_down),
        [((count, 2 * min(2 * LANES, units)), F32)],
        micros=12,
    )


def expert_forward(layout, inputs, w_gate_up, w_down):
    count, features = inputs.shape
    units = w_down.shape[0]
    return call(
        expert_forward_kernel,
        [((count, 2 * units), F32), ((count, units), BF16)]
        + [((EF * CAP, features), F32), ((count - EF * CAP, features), BF16)],
        (inputs, w_gate_up, w_down),
        micros=10,
    )


def expert_backward(layout, d_expert, w_gate_up, w_down, gate_up):
    count, features = d_expert.shape
    units = w_down.shape[0]
    return call(
        expert_backward_kernel,
        [((count, 2 * units), BF16)]
        + [((EF * CAP, features), F32), ((count - EF * CAP, features), BF16)],
        (d_expert, w_gate_up, w_down, gate_up),
        micros=10,
    )


def local(
    layout,
    hidden_in,
    gate_in,
    routes,
    priority,
    segments,
    norm_attn,
    w_qkv,
    w_out,
    norm_moe,
    w_router,
    w_const,
    const_vec,
    w_gate_up,
    w_down,
    grad_out,
):
    layers = w_qkv.shape[0]
    tokens, features = hidden_in.shape
    rep, j, expert = layout.place()
    slim = w_qkv.shape[1]
    small = [
        jnp.concatenate(
            [norm_attn[l][:, None], norm_moe[l][:, None], w_router[l], w_const[l], const_vec[l].T],
            axis=-1,
        ).reshape(1, -1)
        for l in range(layers)
    ]
    small = jnp.concatenate(small, axis=-1)
    extra = ROWS * features
    small = jnp.pad(small, ((0, 0), (0, extra - small.shape[1]))).reshape(ROWS, features)
    count = EF // layout.reps
    shard = lax.axis_index("shard")
    where = jnp.stack([rep, shard // EF, j // 2, j % 2]).astype(jnp.int32)

    group = rep.reshape(1).astype(jnp.int32)

    def share(l, *more):
        blocks = jnp.concatenate(
            [jnp.transpose(w_qkv[l].reshape(slim, 3, features), (1, 0, 2)), w_out[l][None]]
        )
        mine = lax.dynamic_slice_in_dim(blocks, rep * count, count, 0)
        return jnp.concatenate([mine.reshape(count * slim, features), *more])

    def dense_weights(x):
        full = layout.assemble(layout.dense_gather(x), where, count)
        return full[0].reshape(4, features, features), *full[1:]

    line = layout.dense_line(share(0, small))
    *found, last = expert_weights(layout, after(w_gate_up, line), w_down, 0, rep, j, group)
    moe = [found]
    full, small_full = dense_weights(after(line, last))
    small_full = small_full.reshape(layout.shards, -1)
    dense = [full]
    packs, vectors, mixing_t = [], [], []
    for l in range(layers):
        part = small_full[:, l * slim * SMALL : (l + 1) * slim * SMALL]
        part = part.reshape(features, SMALL)
        mixing = part[:, 2 : SMALL - NCONST]
        mixing = jnp.pad(mixing, ((0, 0), (0, LANES - mixing.shape[1])))
        packs.append([part[:, :2].T.astype(F32), None, mixing])
        mixing_t.append(mixing.T)
        vectors.append(part[:, SMALL - NCONST :].T.astype(F32))

    shared = (*rope_tables(tokens), segments.reshape(-1, 1), segments)
    pairs = [place_pairs(routes[l], priority[l, 0], expert) for l in range(layers)]

    source = (hidden_in,)
    previous = jnp.pad(gate_in, ((0, 0), (0, LANES - EXPERTS)))
    kept = []
    for l in range(layers):
        gather, scatter = pairs[l]
        packs[l][1] = dense[l]
        last = l + 1 == layers
        state = attention_forward(
            shared, packs[l], source, previous, routes[l], gather, grad_out if last else None
        )
        middle, logits, coefs, rows = state[7], state[9], state[10], state[11]
        inputs = layout.dispatch(rows)
        if last:
            d_gate_up, activated, own, others = expert_both(inputs, *moe[l])
            wide = dot(inputs[:, :features], d_gate_up, ((0,), (0,))).astype(BF16)
            down = dot(activated, inputs[:, features:], ((0,), (0,))).astype(BF16)
        else:
            dense.append(dense_weights(layout.dense_line(after(share(l + 1), rows)))[0])
            raw = after((w_gate_up, w_down), rows)
            moe.append(expert_weights(layout, *raw, l + 1, rep, j, group)[:2])
            gate_up, activated, own, others = expert_forward(layout, inputs, *moe[l])
        outputs = layout.collect(own, others)
        if last:
            outputs, wide, down = lax.optimization_barrier((outputs, wide, down))
        source = (coefs, middle, packs[l][0], scatter, outputs, vectors[l])
        previous = logits
        kept.append((state, inputs, gate_up, activated, outputs))
    (result,) = call(combine_kernel, [((tokens, features), F32)], source)

    grad_hidden = grad_out
    grad_gate = jnp.zeros_like(previous)
    join = lax.optimization_barrier

    def back_down(x):
        return layout.return_down(x.reshape(count, -1, features))

    def back_gate_up(x):
        return layout.return_gate_up(x.reshape(EF, -1, x.shape[-1]))

    def put_down(x, l, held):
        return store_down(x[None], (layers, EF) + w_down.shape[2:], l, held)

    def put_gate_up(x, l, held):
        x = x.reshape((EF, layout.reps) + x.shape[1:])
        return store_gate_up(layout, x, (layers, EF) + w_gate_up.shape[2:], l, held)

    boths, wides, downs = [None] * layers, [None] * layers, [None] * layers
    gate_up_out, down_out = None, None
    smalls = [None] * layers
    for l in reversed(range(layers)):
        gather, scatter = pairs[l]
        state, inputs, gate_up, activated, outputs = kept[l]
        hidden, normed, query, keys, values, log_total, attended, middle, low = state[:9]
        coefs = state[10]
        last = l + 1 == layers
        if not last:
            d_expert = layout.dispatch(rows)
        grad_gate, d_mixed, mix_grads = call(
            gate_backward_kernel,
            [((tokens, LANES), F32), ((tokens, features), F32), ((SMALL - 2, features), F32)],
            (coefs, middle, packs[l][0], scatter, outputs, vectors[l], routes[l], low)
            + (mixing_t[l], grad_hidden, grad_gate),
            micros=6,
        )
        if last:
            d_rows = outputs
            wides[l], downs[l] = layout.line_sum(wide), layout.line_sum(down)
        else:
            d_expert, d_mixed = join((d_expert, d_mixed))
            down = back_down(after(downs[l + 1], d_expert))
            d_gate_up, own, others = expert_backward(layout, d_expert, *moe[l], gate_up)
            own, down = join((own, down))
            down_out = put_down(down, l + 1, down_out)
            grad_gate_up = dot(inputs, d_gate_up, ((0,), (0,))).astype(BF16)
            d_rows = layout.collect(own, others)
            boths[l + 1] = layout.sum_core(
                dense_gradients(layout, *after(ready, own), count), j % 2
            )
            grad_down = dot(activated, d_expert, ((0,), (0,))).astype(BF16)
            d_rows, grad_gate_up, grad_down, boths[l + 1], down_out = join(
                (d_rows, grad_gate_up, grad_down, boths[l + 1], down_out)
            )
            wides[l], downs[l] = layout.line_sum(grad_gate_up), layout.line_sum(grad_down)
        more = () if l == 0 else (kept[l - 1][0][10], pairs[l - 1][0])
        grad_hidden, d_branch, d_projected, gain_grads, *rows = call(
            functools.partial(attention_backward_kernel, l > 0),
            [((tokens, features), F32), ((tokens, features), BF16)]
            + [((3, tokens, features), BF16), ((2, features), F32)]
            + [((gather.shape[1], features), BF16)] * (l > 0),
            (grad_hidden, d_mixed, d_rows, scatter, middle, hidden, packs[l][0], packs[l][1])
            + (*shared, query, keys, values, log_total, *more),
            [((tokens, tokens), F32), ((tokens, features), BF16), ((tokens, features), F32)],
            7,
            14,
        )
        rows = rows[0] if rows else None
        if not last:
            wide = back_gate_up(after(wides[l + 1], d_branch))
        small_grads = jnp.concatenate([gain_grads, mix_grads]).T.astype(BF16)
        smalls[l] = small_grads.reshape(layout.shards, slim * SMALL)
        ready = ((normed, attended, d_projected, d_branch), None)

    smalls = jnp.concatenate(smalls, axis=1)
    smalls = jnp.pad(smalls, ((0, 0), (0, ROWS * features - smalls.shape[1])))
    ready = (ready[0], smalls.reshape(layout.shards, ROWS, features))
    boths[0] = layout.sum_core(dense_gradients(layout, *ready, count), j % 2)
    boths[0], wide = join((boths[0], wide))
    gate_up_out = put_gate_up(wide, 1, gate_up_out)
    both = jnp.concatenate(boths, axis=3)
    cross, gate_up_out, down = join(
        (layout.sum_cross(both, rep, j), gate_up_out, back_down(after(downs[0], both)))
    )
    line = layout.sum_cross_end(*cross, rep, j)
    line, wides[0] = join((line, wides[0]))
    down_out = put_down(down, 0, down_out)
    line, wide, gate_up_out, down_out, result = join(
        (layout.sum_line(line), back_gate_up(wides[0]), gate_up_out, down_out, result)
    )
    gate_up_out = put_gate_up(wide, 0, gate_up_out)
    dense_all = layout.rep_gather(line, rep)
    small_all = dense_all[0, count * slim : count * slim + ROWS].reshape(-1)
    small_all = small_all[: layers * slim * SMALL].astype(F32).reshape(layers, slim, SMALL)
    starts = [0] + [l * count * slim + ROWS for l in range(1, layers)]
    dense_all = jnp.stack([dense_all[:, at : at + count * slim] for at in starts])
    dense_all = dense_all.astype(F32).reshape(layers, 4, slim, features)
    qkv_all = jnp.transpose(dense_all[:, :3], (0, 2, 1, 3)).reshape(layers, slim, 3 * features)
    return (
        result.astype(BF16),
        grad_hidden,
        grad_gate[:, :EXPERTS],
        small_all[:, :, 0],
        qkv_all,
        dense_all[:, 3],
        small_all[:, :, 1],
        small_all[:, :, 2 : 2 + EXPERTS],
        small_all[:, :, 2 + EXPERTS : SMALL - NCONST],
        jnp.transpose(small_all[:, :, SMALL - NCONST :], (0, 2, 1)),
        gate_up_out,
        down_out,
    )


def solution(mesh):
    return jax.shard_map(
        functools.partial(local, Layout(mesh)),
        mesh=mesh,
        in_specs=(
            P(("rep", "shard"), None),
            P(("rep", "shard"), None),
            P(None, ("rep", "shard"), None),
            P(None, ("rep", "shard"), None),
            P(("rep", "shard"), None),
            P(None, "shard"),
            P(None, "shard", None),
            P(None, "shard", None),
            P(None, "shard"),
            P(None, "shard", None),
            P(None, "shard", None),
            P(None, None, "shard"),
            P(None, None, "shard", None),
            P(None, None, "shard", None),
            P(("rep", "shard"), None),
        ),
        out_specs=(
            P(("rep", "shard"), None),
            P(("rep", "shard"), None),
            P(("rep", "shard"), None),
            P(None, "shard"),
            P(None, "shard", None),
            P(None, "shard", None),
            P(None, "shard"),
            P(None, "shard", None),
            P(None, "shard", None),
            P(None, None, "shard"),
            P(None, None, "shard", None),
            P(None, None, "shard", None),
        ),
        check_vma=False,
    )
```

```python
import functools
import math

import jax
import jax.numpy as jnp
from jax import lax
from jax.experimental import pallas as pl
from jax.experimental.pallas import tpu as pltpu
from jax.sharding import PartitionSpec as P

HEAD_DIM = 64
EF = 4
NCONST = 2
TOP = 2
EXPERTS = 8
CAP = 80
SMALL = 2 + EXPERTS + 2 * NCONST + NCONST
ROWS = 16
LANES = 128

EPSILON = 1e-06
SCALE = 0.125
MASKED = -1000000000.0
AXES = ("rep", "shard")
BF16 = jnp.bfloat16
F32 = jnp.float32


def dot(a, b, dims=((1,), (0,))):
    return lax.dot_general(a, b, (dims, ((), ())), preferred_element_type=F32)


def rope_tables(tokens):
    half = HEAD_DIM // 2
    places = jnp.arange(tokens, dtype=jnp.int32).astype(F32)[:, None]
    powers = jnp.arange(half, dtype=jnp.int32).astype(F32) / half
    angles = places * jnp.exp(-math.log(10000.0) * powers)[None, :]
    cosine, sine = jnp.cos(angles), jnp.sin(angles)
    heads = LANES // HEAD_DIM
    return jnp.tile(cosine, (1, 2 * heads)), jnp.tile(
        jnp.concatenate([-sine, sine], axis=-1), (1, heads)
    )


def turn(block, cosine, sine):
    half = HEAD_DIM // 2
    lane = lax.broadcasted_iota(jnp.int32, block.shape, 1)
    width = block.shape[1]
    partner = jnp.where(
        lane % HEAD_DIM < half,
        pltpu.roll(block, width - half, 1),
        pltpu.roll(block, half, 1),
    )
    return block * cosine + partner * sine


def lane_pick(array, lane, index):
    return jnp.sum(jnp.where(lane == index, array, 0.0), axis=-1, keepdims=True)


def inverse_rms(x):
    return lax.rsqrt(jnp.mean(x * x, axis=-1, keepdims=True) + EPSILON)


def attention_bias(seg_col, seg_row):
    shape = (seg_col.shape[0], seg_row.shape[1])
    rows = lax.broadcasted_iota(jnp.int32, shape, 0)
    columns = lax.broadcasted_iota(jnp.int32, shape, 1)
    allowed = (seg_col[...] == seg_row[...]) & (columns <= rows)
    return jnp.where(allowed, 0.0, MASKED)


def head_masks(shape):
    lane = lax.broadcasted_iota(jnp.int32, shape, 1)
    return [(lane // HEAD_DIM) == half for half in range(LANES // HEAD_DIM)]


def columns_of(step, width):
    return pl.ds(pl.multiple_of(step * width, width), width)


def attention_forward_kernel(joined, last, *refs):
    refs = iter(refs)

    def take(number):
        return [next(refs) for _ in range(number)]

    parts = take(6 if joined else 1)
    gains, weights, cosine, sine, seg_col, seg_row, mixing, previous, routes, gather = take(10)
    d_result = take(1) if last else None
    hidden = take(1)[0] if joined else parts[0]
    normed, query, keys, values, log_total, attended, middle, mixed_low = take(8)
    logits, coefs, rows, bias, held, arrived = take(6)
    copies = [
        pltpu.make_async_copy(weights.at[block], held.at[block], arrived.at[block])
        for block in range(4)
    ]
    for copy in copies:
        copy.start()
    weights = held
    if joined:
        combine_kernel(*parts, hidden)
    tokens, features = hidden.shape
    h = hidden[...].astype(F32)
    normed[...] = (h * inverse_rms(h) * gains[0:1]).astype(BF16)
    bias[...] = attention_bias(seg_col, seg_row)
    wide = 2 * LANES
    for block, out in ((0, query), (1, keys)):
        copies[block].wait()

        @pl.loop(0, features // wide)
        def _(step):
            part = dot(normed[...], weights[block, :, columns_of(step, wide)])
            for k in range(2):
                turned = turn(part[:, k * LANES : (k + 1) * LANES], cosine[...], sine[...])
                out[:, columns_of(2 * step + k, LANES)] = turned.astype(BF16)

    copies[2].wait()

    @pl.loop(0, features // wide)
    def _(step):
        at = columns_of(step, wide)
        values[:, at] = dot(normed[...], weights[2, :, at]).astype(BF16)

    log_total[...] = jnp.zeros_like(log_total)

    @pl.loop(0, features // LANES)
    def _(step):
        at = columns_of(step, LANES)
        q, k, v = query[:, at], keys[:, at], values[:, at]
        lane = lax.broadcasted_iota(jnp.int32, log_total.shape, 1)
        total_out = jnp.zeros((tokens, LANES), F32)
        for half, mask in enumerate(head_masks(q.shape)):
            scores = dot(jnp.where(mask, q, 0), k, ((1,), (1,))) * SCALE + bias[...]
            top = jnp.max(scores, axis=-1, keepdims=True)
            weight = jnp.exp(scores - top)
            total = jnp.sum(weight, axis=-1, keepdims=True)
            probs = (weight * (1.0 / total)).astype(BF16)
            total_out += dot(probs, jnp.where(mask, v, 0))
            log_total[...] = jnp.where(
                lane == step * (LANES // HEAD_DIM) + half, top + jnp.log(total), log_total[...]
            )
        attended[:, at] = total_out.astype(BF16)

    copies[3].wait()

    @pl.loop(0, features // wide)
    def _(step):
        at = columns_of(step, wide)
        middle[:, at] = hidden[:, at].astype(F32) + dot(attended[...], weights[3, :, at])

    m = middle[...]
    low = (m * inverse_rms(m) * gains[1:2]).astype(BF16)
    mixed_low[...] = low
    rows[:, :features] = dot(gather[0] + gather[1], low).astype(BF16)
    raw = dot(low, mixing[...])
    lane = lax.broadcasted_iota(jnp.int32, raw.shape, 1)
    now = jnp.where(lane < EXPERTS, raw + previous[...], 0.0)
    logits[...] = now
    route = [routes[:, k : k + 1] for k in range(TOP)]
    chosen = [lane_pick(now, lane, route[k]) for k in range(TOP)]
    best = jnp.maximum(chosen[0], chosen[1])
    chosen = [jnp.exp(c - best) for c in chosen]
    gates = [c / (chosen[0] + chosen[1]) for c in chosen]
    shares = []
    for c in range(NCONST):
        pair = [lane_pick(raw, lane, EXPERTS + 2 * c + i) for i in range(2)]
        best = jnp.maximum(pair[0], pair[1])
        pair = [jnp.exp(p - best) for p in pair]
        shares.append([p / (pair[0] + pair[1]) for p in pair])
    copies = [(route[k] == EF + 1).astype(F32) for k in range(TOP)]
    consts = [[(route[k] == EF + 2 + c).astype(F32) for c in range(NCONST)] for k in range(TOP)]
    weight = [sum(consts[k][c] * gates[k] for k in range(TOP)) for c in range(NCONST)]
    columns = list(gates)
    columns += [
        copies[k] + sum(consts[k][c] * shares[c][0] for c in range(NCONST)) for k in range(TOP)
    ]
    columns += [consts[k][c] * shares[c][1] for k in range(TOP) for c in range(NCONST)]
    columns += [shares[c][i] for c in range(NCONST) for i in range(2)]
    columns += weight
    columns += [
        sum(copies[k] * gates[k] for k in range(TOP))
        + sum(shares[c][0] * weight[c] for c in range(NCONST))
    ]
    columns += [shares[c][1] * weight[c] for c in range(NCONST)]
    packed = jnp.zeros_like(raw)
    for index, column in enumerate(columns):
        packed = jnp.where(lane == index, column, packed)
    coefs[...] = packed
    if last:
        rows[:, features:] = value_rows(gates, gather, d_result[0])


GATE, MIXED, VECTOR, SHARE, WEIGHT, DIRECT, CONST = 0, 2, 4, 8, 12, 14, 15


def combine_kernel(coefs, middle, gains, scatter, outputs, vectors, result):
    coef = coefs[...]
    m = middle[...]
    total = m + coef[:, DIRECT : DIRECT + 1] * (m * inverse_rms(m) * gains[1:2])
    for k in range(TOP):
        total += coef[:, GATE + k : GATE + k + 1] * dot(scatter[k], outputs[:, : m.shape[1]])
    for c in range(NCONST):
        total += coef[:, CONST + c : CONST + c + 1] * vectors[c : c + 1]
    result[...] = total


def value_rows(gates, gather, d_result):
    return sum(
        dot(gather[k], (gates[k] * d_result[...]).astype(BF16)) for k in range(TOP)
    ).astype(BF16)


def two_parts(x):
    high = x.astype(BF16)
    return high, (x - high.astype(F32)).astype(BF16)


def gate_backward_kernel(
    coefs, middle, gains, scatter, outputs, vectors, routes, mixed_low, mixing_t, d_result, d_next,
    d_logits, d_mixed, grads,
):
    coef = coefs[...]
    m = middle[...]
    dh = d_result[...]
    lane = lax.broadcasted_iota(jnp.int32, coef.shape, 1)

    def column(index):
        return coef[:, index : index + 1]

    along = jnp.sum(m * inverse_rms(m) * gains[1:2] * dh, axis=-1, keepdims=True)
    with_vector = [
        jnp.sum(dh * vectors[c : c + 1], axis=-1, keepdims=True) for c in range(NCONST)
    ]
    d_gates = []
    for k in range(TOP):
        value = jnp.sum(dot(scatter[k], outputs[:, : dh.shape[1]]) * dh, axis=-1, keepdims=True)
        value += column(MIXED + k) * along
        value += sum(column(VECTOR + k * NCONST + c) * with_vector[c] for c in range(NCONST))
        d_gates.append(value)
    mean = sum(column(GATE + k) * d_gates[k] for k in range(TOP))
    terms = d_next[...]
    for k in range(TOP):
        chosen = column(GATE + k) * (d_gates[k] - mean)
        terms += jnp.where(lane == routes[:, k : k + 1], chosen, 0.0)
    d_logits[...] = terms
    vector_terms = jnp.zeros_like(terms)
    for c in range(NCONST):
        share = [column(SHARE + 2 * c + i) for i in range(2)]
        d_share = [column(WEIGHT + c) * along, column(WEIGHT + c) * with_vector[c]]
        mean = share[0] * d_share[0] + share[1] * d_share[1]
        for i in range(2):
            terms = jnp.where(
                lane == EXPERTS + 2 * c + i, share[i] * (d_share[i] - mean), terms
            )
        vector_terms = jnp.where(
            lane == EXPERTS + 2 * NCONST + c, column(CONST + c), vector_terms
        )
    high, lowest = two_parts(terms)
    d_mixed[...] = column(DIRECT) * dh + dot(high, mixing_t[...]) + dot(lowest, mixing_t[...])
    both = ((0,), (0,))
    total = dot(high, mixed_low[...], both) + dot(lowest, mixed_low[...], both)
    high, lowest = two_parts(vector_terms)
    dh_high, dh_low = two_parts(dh)
    total += dot(high, dh_high, both) + dot(lowest, dh_high, both) + dot(high, dh_low, both)
    grads[...] = total[: grads.shape[0]]


def expert_forward_kernel(inputs, w_gate_up, w_down, gate_up, activated, own, others):
    units = w_down.shape[0]
    wide = min(2 * LANES, units)
    kept = own.shape[0]

    @pl.loop(0, units // wide)
    def _(step):
        at = columns_of(step, wide)
        gate = dot(inputs[...], w_gate_up[:, at])
        up_at = pl.ds(pl.multiple_of(units + step * wide, wide), wide)
        up = dot(inputs[...], w_gate_up[:, up_at])
        gate_up[:, at] = gate
        gate_up[:, up_at] = up
        activated[:, at] = (gate / (1.0 + jnp.exp(-gate)) * up).astype(BF16)

    @pl.loop(0, w_down.shape[1] // (2 * LANES))
    def _(step):
        at = columns_of(step, 2 * LANES)
        out = dot(activated[...], w_down[:, at])
        own[:, at] = out[:kept]
        others[:, at] = out[kept:].astype(BF16)


def expert_backward_kernel(d_expert, w_gate_up, w_down, gate_up, d_gate_up, own, others):
    units = w_down.shape[0]
    wide = min(2 * LANES, units)
    kept = own.shape[0]

    @pl.loop(0, units // wide)
    def _(step):
        at = columns_of(step, wide)
        up_at = pl.ds(pl.multiple_of(units + step * wide, wide), wide)
        d_active = dot(d_expert[...], w_down[at, :], ((1,), (1,)))
        gate, up = gate_up[:, at], gate_up[:, up_at]
        sigmoid = 1.0 / (1.0 + jnp.exp(-gate))
        d_gate_up[:, at] = (
            d_active * up * sigmoid * (1.0 + gate * (1.0 - sigmoid))
        ).astype(BF16)
        d_gate_up[:, up_at] = (d_active * gate * sigmoid).astype(BF16)

    @pl.loop(0, w_gate_up.shape[0] // (2 * LANES))
    def _(step):
        at = columns_of(step, 2 * LANES)
        out = dot(d_gate_up[...], w_gate_up[at, :], ((1,), (1,)))
        own[:, at] = out[:kept]
        others[:, at] = out[kept:].astype(BF16)


def expert_both_kernel(
    rows, w_gate_up, w_down, d_gate_up, activated, own, others, gate_up
):
    features, units = w_gate_up.shape[0], w_down.shape[0]
    wide = min(2 * LANES, units)
    kept = own.shape[0]

    @pl.loop(0, units // wide)
    def _(step):
        at = columns_of(step, wide)
        up_at = pl.ds(pl.multiple_of(units + step * wide, wide), wide)
        gate_up[:, :wide] = dot(rows[:, :features], w_gate_up[:, at])
        gate_up[:, wide:] = dot(rows[:, :features], w_gate_up[:, up_at])
        d_active = dot(rows[:, features:], w_down[at, :], ((1,), (1,)))
        gate, up = gate_up[:, :wide], gate_up[:, wide:]
        sigmoid = 1.0 / (1.0 + jnp.exp(-gate))
        activated[:, at] = (gate * sigmoid * up).astype(BF16)
        d_gate_up[:, at] = (
            d_active * up * sigmoid * (1.0 + gate * (1.0 - sigmoid))
        ).astype(BF16)
        d_gate_up[:, up_at] = (d_active * gate * sigmoid).astype(BF16)

    @pl.loop(0, features // (2 * LANES))
    def _(step):
        at = columns_of(step, 2 * LANES)
        out = dot(activated[...], w_down[:, at])
        own[:, at] = out[:kept]
        others[:, at] = out[kept:].astype(BF16)
        out = dot(d_gate_up[...], w_gate_up[at, :], ((1,), (1,)))
        to = pl.ds(pl.multiple_of(features + step * 2 * LANES, 2 * LANES), 2 * LANES)
        own[:, to] = out[:kept]
        others[:, to] = out[kept:].astype(BF16)


def norm_backward(grad, source, gain):
    inverse = inverse_rms(source)
    scaled = grad * gain
    gain_grad = jnp.sum(grad * source * inverse, axis=0, keepdims=True)
    mean = jnp.mean(scaled * source, axis=-1, keepdims=True)
    return inverse * scaled - source * (inverse * inverse * inverse * mean), gain_grad


def attention_backward_kernel(more, *refs):
    refs = iter(refs)

    def take(number):
        return [next(refs) for _ in range(number)]

    d_result, d_mixed, d_rows, scatter, middle, hidden, gains, weights = take(8)
    cosine, sine, seg_col, seg_row, query, keys, values, log_total = take(8)
    coefs, gather = take(2) if more else (None, None)
    d_hidden, d_branch, d_projected, gain_grads = take(4)
    rows = take(1)[0] if more else None
    bias, d_attended, d_normed, held, arrived = take(5)
    copies = [
        pltpu.make_async_copy(weights.at[block], held.at[block], arrived.at[block])
        for block in range(4)
    ]
    for copy in copies[::-1]:
        copy.start()
    weights = held
    tokens, features = hidden.shape
    wide = 2 * LANES
    total = d_mixed[...] + dot(
        scatter[0] + scatter[1], d_rows[:, d_rows.shape[1] - features :]
    )
    d_middle, gain_grad = norm_backward(total, middle[...], gains[1:2])
    d_middle = d_middle + d_result[...]
    gain_grads[1:2] = gain_grad
    d_hidden[...] = d_middle
    d_branch[...] = d_middle.astype(BF16)
    bias[...] = attention_bias(seg_col, seg_row)
    copies[3].wait()

    @pl.loop(0, features // wide)
    def _(step):
        at = columns_of(step, wide)
        d_attended[:, at] = dot(d_branch[...], weights[3, at, :], ((1,), (1,))).astype(BF16)

    @pl.loop(0, features // LANES)
    def _(step):
        at = columns_of(step, LANES)
        q, k, v, da = query[:, at], keys[:, at], values[:, at], d_attended[:, at]
        lane = lax.broadcasted_iota(jnp.int32, log_total.shape, 1)
        zero = jnp.zeros((tokens, LANES), F32)
        dq, dk, dv = zero, zero, zero
        for half, mask in enumerate(head_masks(q.shape)):
            q_half, da_half = jnp.where(mask, q, 0), jnp.where(mask, da, 0)
            scores = dot(q_half, k, ((1,), (1,))) * SCALE + bias[...]
            shift = lane_pick(log_total[...], lane, step * (LANES // HEAD_DIM) + half)
            probs = jnp.exp(scores - shift)
            dv += dot(probs.astype(BF16), da_half, ((0,), (0,)))
            d_probs = dot(da_half, v, ((1,), (1,)))
            mean = jnp.sum(d_probs * probs, axis=-1, keepdims=True)
            d_scores = (probs * (d_probs - mean)).astype(BF16)
            dq += dot(d_scores, jnp.where(mask, k, 0))
            dk += dot(d_scores, q_half, ((0,), (0,)))
        d_projected[0, :, at] = turn(dq * SCALE, cosine[...], -sine[...]).astype(BF16)
        d_projected[1, :, at] = turn(dk * SCALE, cosine[...], -sine[...]).astype(BF16)
        d_projected[2, :, at] = dv.astype(BF16)

    for copy in copies[:3]:
        copy.wait()

    @pl.loop(0, features // wide)
    def _(step):
        at = columns_of(step, wide)
        d_normed[:, at] = sum(
            dot(d_projected[b], weights[b, at, :], ((1,), (1,))) for b in range(3)
        )

    d_input, gain_grad = norm_backward(d_normed[...], hidden[...].astype(F32), gains[0:1])
    gain_grads[0:1] = gain_grad
    d_hidden[...] += d_input
    if more:
        gates = [coefs[:, GATE + k : GATE + k + 1] for k in range(TOP)]
        rows[...] = value_rows(gates, gather, d_hidden)


def cost(micros):
    return pl.CostEstimate(flops=0, bytes_accessed=int(micros * 3.6e6), transcendentals=0)


def call(kernel, outs, args, scratch=(), apart=None, micros=5):
    specs = [
        pl.BlockSpec(memory_space=pl.ANY) if k == apart else pl.BlockSpec()
        for k in range(len(args))
    ]
    scratch = [pltpu.VMEM(shape, dtype) for shape, dtype in scratch]
    if apart is not None:
        scratch += [
            pltpu.VMEM(args[apart].shape, args[apart].dtype),
            pltpu.SemaphoreType.DMA((4,)),
        ]
    return pl.pallas_call(
        kernel,
        out_shape=[jax.ShapeDtypeStruct(shape, dtype) for shape, dtype in outs],
        in_specs=specs,
        scratch_shapes=scratch,
        compiler_params=pltpu.CompilerParams(vmem_limit_bytes=60 * 1024 * 1024),
        cost_estimate=cost(micros),
    )(*args)


def after(x, *others):
    return lax.optimization_barrier((x,) + others)[0]


class Layout:
    def __init__(self, mesh):
        self.reps, self.shards = mesh.shape["rep"], mesh.shape["shard"]
        self.lines = self.shards // EF
        assert self.shards % EF == 0 and EF % self.reps == 0

    def pairs(self, move):
        found = []
        for rep in range(self.reps):
            for shard in range(self.shards):
                r, z, j = move(rep, shard // EF, shard % EF)
                found.append((rep * self.shards + shard, r * self.shards + z * EF + j))
        return found

    def send(self, x, move):
        return lax.ppermute(x, AXES, self.pairs(move))

    def expert_move(self, mask, shift):
        def move(r, z, j):
            number = r * EF + j
            e, f = (number // self.reps) ^ mask, (number % self.reps + shift) % self.reps
            number = e * self.reps + f
            return number // EF, z, number % EF

        return move

    def place(self):
        rep, shard = lax.axis_index("rep"), lax.axis_index("shard")
        j = shard % EF
        return rep, j, (rep * EF + j) // self.reps

    def quad_exchange(self, blocks, j):
        got = lax.dynamic_update_slice_in_dim(
            jnp.zeros_like(blocks), lax.dynamic_slice_in_dim(blocks, j, 1, 0), j, 0
        )
        for mask in range(1, EF):
            other = j ^ mask
            block = lax.dynamic_slice_in_dim(blocks, other, 1, 0)
            block = self.send(block, lambda r, z, q: (r, z, q ^ mask))
            got = lax.dynamic_update_slice_in_dim(got, block, other, 0)
        return got

    def part_exchange(self, blocks, j):
        count = EF // self.reps
        mine = j // self.reps
        got = lax.dynamic_update_slice_in_dim(
            jnp.zeros_like(blocks), lax.dynamic_slice_in_dim(blocks, mine, 1, 0), mine, 0
        )
        for mask in range(1, count):
            other = mine ^ mask
            block = lax.dynamic_slice_in_dim(blocks, other, 1, 0)
            block = self.send(block, lambda r, z, q: (r, z, q ^ (mask * self.reps)))
            got = lax.dynamic_update_slice_in_dim(got, block, other, 0)
        return got

    def rep_gather(self, x, rep):
        got = lax.dynamic_update_slice_in_dim(
            jnp.zeros((self.reps,) + x.shape, x.dtype), x[None], rep, 0
        )
        for shift in range(1, self.reps):
            block = self.send(x, lambda r, z, q: ((r + shift) % self.reps, z, q))
            got = lax.dynamic_update_slice_in_dim(
                got, block[None], (rep + self.reps - shift) % self.reps, 0
            )
        return got

    def trade(self, blocks, chosen):
        groups = [
            [(n // EF) * self.shards + z * EF + n % EF for n in numbers]
            for z in range(self.lines)
            for numbers in chosen
        ]
        return lax.all_to_all(blocks, AXES, 0, 0, axis_index_groups=groups, tiled=True)

    def return_gate_up(self, blocks):
        return self.trade(
            jnp.concatenate([blocks] * self.reps), [list(range(self.reps * EF))]
        )

    def return_down(self, blocks):
        return self.trade(
            jnp.concatenate([blocks] * self.reps),
            [[e * self.reps + f for e in range(EF)] for f in range(self.reps)],
        )

    def line_groups(self):
        return [[z * EF + j for z in range(self.lines)] for j in range(EF)]

    def line_gather(self, x):
        return lax.all_gather(
            x, "shard", axis=0, tiled=True, axis_index_groups=self.line_groups()
        )

    def line_sum(self, x):
        return lax.psum_scatter(
            x, "shard", scatter_dimension=0, tiled=True, axis_index_groups=self.line_groups()
        )

    def dense_line(self, x):
        line = [x[None]]
        for shift in range(1, self.lines):
            line.append(self.send(x, lambda r, q, k: (r, (q + shift) % self.lines, k))[None])
        return jnp.concatenate(line)

    def dense_gather(self, line):
        reps, lines = self.reps, self.lines
        cut = lines // 2

        def over_rep(block, shift):
            return self.send(block, lambda r, q, k: ((r + shift) % reps, q, k))

        def over_high(block):
            return self.send(block, lambda r, q, k: (r, q, k ^ 2))

        sides = [over_rep(line, shift) for shift in range(1, reps)]
        flip = over_high(line)
        pieces = [(line, 0, 0, 0), (flip, 0, 0, 1)]
        for shift, block in enumerate(sides, 1):
            pieces.append((block, 0, shift, 0))
            pieces.append((over_high(block[:cut]), 0, shift, 1))
            pieces.append((over_rep(flip[cut:], shift), cut, shift, 1))
        pieces = [piece + (0,) for piece in pieces if piece[0].shape[0]]
        others = [
            (self.send(piece[0], lambda r, q, k: (r, q, k ^ 1)),) + piece[1:4] + (1,)
            for piece in pieces
        ]
        return pieces + others

    def assemble(self, pieces, where, count):
        reps, lines = self.reps, self.lines
        rows, features = pieces[0][0].shape[1:]
        slim = features // self.shards
        extra = rows - count * slim
        notes = [piece[1:] for piece in pieces]

        def kernel(where_ref, *refs):
            out = refs[len(pieces)]
            rep, z, high, core = [where_ref[k] for k in range(4)]
            for ref, (start, back, flip, other) in zip(refs, notes):
                r = lax.rem(rep + reps - back, reps)
                hi = high if flip == 0 else 1 - high
                lo = core if other == 0 else 1 - core
                for step in range(ref.shape[0]):
                    at = lax.rem(z + lines - start - step, lines)
                    for k in range(count):
                        out[r, k, at, hi, lo] = ref[step, k * slim : (k + 1) * slim]
                    if extra and back == 0:
                        refs[-1][at, hi, lo] = ref[step, count * slim :]

        shapes = [jax.ShapeDtypeStruct((reps, count, lines, 2, 2, slim, features), BF16)]
        if extra:
            shapes.append(jax.ShapeDtypeStruct((lines, 2, 2, extra, features), BF16))
        return pl.pallas_call(
            kernel,
            out_shape=shapes,
            in_specs=[pl.BlockSpec(memory_space=pltpu.SMEM)]
            + [pl.BlockSpec(memory_space=pltpu.VMEM)] * len(pieces),
            out_specs=[pl.BlockSpec(memory_space=pltpu.VMEM)] * len(shapes),
            compiler_params=pltpu.CompilerParams(vmem_limit_bytes=60 * 1024 * 1024),
            cost_estimate=cost(4),
        )(where, *[piece[0] for piece in pieces])

    def over_rep(self, block, shift):
        return self.send(block, lambda r, q, k: ((r + shift) % self.reps, q, k))

    def sum_core(self, terms, core):
        mine = lax.dynamic_slice_in_dim(terms, core, 1, 0)[0]
        other = lax.dynamic_slice_in_dim(terms, 1 - core, 1, 0)[0]
        other = self.send(other, lambda r, q, k: (r, q, k ^ 1))
        return (mine.astype(F32) + other.astype(F32)).astype(BF16)

    def rep_step(self, x, rep):
        total = lax.dynamic_slice_in_dim(x, rep, 1, 0)[0].astype(F32)
        for shift in range(1, self.reps):
            block = lax.dynamic_slice_in_dim(x, (rep + shift) % self.reps, 1, 0)[0]
            total = total + self.over_rep(block, shift).astype(F32)
        return total.astype(BF16)

    def high_step(self, x, high, axis):
        mine = lax.dynamic_slice_in_dim(x, high, 1, axis)
        other = lax.dynamic_slice_in_dim(x, 1 - high, 1, axis)
        other = self.send(other, lambda r, q, k: (r, q, k ^ 2))
        return jnp.squeeze(mine.astype(F32) + other.astype(F32), axis).astype(BF16)

    def sum_cross(self, both, rep, j):
        cut = self.lines // 2
        return self.high_step(both[:, :cut], j // 2, 2), self.rep_step(both[:, cut:], rep)

    def sum_cross_end(self, first, second, rep, j):
        return jnp.concatenate([self.rep_step(first, rep), self.high_step(second, j // 2, 1)])

    def sum_line(self, line):
        z = lax.axis_index("shard") // EF
        lines = self.lines
        total = lax.dynamic_slice_in_dim(line, z, 1, 0)[0].astype(F32)
        for shift in range(1, lines):
            block = lax.dynamic_slice_in_dim(line, (z + shift) % lines, 1, 0)[0]
            block = self.send(block, lambda r, q, k: (r, (q + shift) % lines, k))
            total = total + block.astype(F32)
        return total.astype(BF16)

    def dispatch(self, rows):
        blocks = rows.reshape(EF, CAP, -1)
        own = jnp.stack(
            [blocks[0]] + [self.send(blocks[m], self.expert_move(m, 0)) for m in range(1, EF)]
        )
        parts = [own] + [self.send(own, self.expert_move(0, g)) for g in range(1, self.reps)]
        return jnp.concatenate(parts).reshape(self.reps * EF * CAP, -1)

    def collect(self, own, others):
        total = own
        for g in range(1, self.reps):
            block = others[(g - 1) * EF * CAP : g * EF * CAP]
            total = total + self.send(block, self.expert_move(0, self.reps - g)).astype(F32)
        total = total.astype(BF16).reshape(EF, CAP, -1)
        return jnp.concatenate(
            [total[0]] + [self.send(total[m], self.expert_move(m, 0)) for m in range(1, EF)]
        )


def split_gate_up(layout, w_gate_up, layer, where):
    _, experts, rows, columns = w_gate_up.shape
    width = columns // (2 * layout.shards)
    parts = layout.reps
    per = layout.shards // parts

    def kernel(where_ref, x, o):
        for j in range(EF):
            e = where_ref[0] * (EF // layout.reps) + j // parts
            for b in range(2 * per):
                at = (b * parts + j % parts) * width
                o[j, :, b * width : (b + 1) * width] = x[0, e, :, at : at + width]

    return pl.pallas_call(
        kernel,
        grid=(1,),
        out_shape=jax.ShapeDtypeStruct((EF, rows, columns // parts), BF16),
        in_specs=[
            pl.BlockSpec(memory_space=pltpu.SMEM),
            pl.BlockSpec((1, experts, rows, columns), lambda _: (layer, 0, 0, 0)),
        ],
        out_specs=pl.BlockSpec((EF, rows, columns // parts), lambda _: (0, 0, 0)),
        compiler_params=pltpu.CompilerParams(vmem_limit_bytes=60 * 1024 * 1024),
        cost_estimate=cost(4),
    )(where, w_gate_up)


def expert_weights(layout, w_gate_up, w_down, layer, rep, j, where):
    count = EF // layout.reps
    mine = layout.quad_exchange(split_gate_up(layout, w_gate_up, layer, where), j)
    mine = mine.reshape(-1, mine.shape[-1])
    down = lax.dynamic_slice_in_dim(w_down[layer], rep * count, count, 0)
    down = layout.part_exchange(down, j)
    down = down.reshape(-1, down.shape[-1])
    return layout.line_gather(mine), layout.line_gather(down), down


def dense_gradients(layout, terms, small, count):
    tokens, features = terms[0].shape
    lines, slim = layout.lines, features // layout.shards
    wide = 2 * LANES
    extra = () if small is None else (small,)

    def kernel(normed, attended, d_projected, d_branch, *refs):
        out, turned = refs[-2:]
        turned[0] = normed[...].T
        turned[1] = attended[...].T
        for block in range(4):
            r, k = block // count, block % count

            @pl.loop(0, features // wide)
            def _(step):
                at = columns_of(step, wide)
                grad = d_branch[:, at] if block == 3 else d_projected[block, :, at]
                term = dot(turned[block // 3], grad).astype(BF16)
                for s in range(layout.shards):
                    out[s % 2, r, s // EF, s // 2 % 2, k * slim : (k + 1) * slim, at] = term[
                        s * slim : (s + 1) * slim
                    ]

        for s in range(layout.shards if extra else 0):
            for r in range(layout.reps):
                out[s % 2, r, s // EF, s // 2 % 2, count * slim :] = refs[0][s]

    shape = (2, layout.reps, lines, 2, count * slim + ROWS * len(extra), features)
    return call(kernel, [(shape, BF16)], (*terms, *extra), [((2, features, tokens), BF16)], micros=8)[0]


def store_layer(kernel, source, block, index, shape, layer, held):
    spec = pl.BlockSpec((1, 1) + shape[2:], lambda e: (layer, e) + (0,) * (len(shape) - 2))
    whole = [] if held is None else [held]
    return pl.pallas_call(
        (lambda x, o: kernel(x, o)) if held is None else (lambda x, h, o: kernel(x, o)),
        grid=(shape[1],),
        out_shape=jax.ShapeDtypeStruct(shape, F32),
        in_specs=[pl.BlockSpec(block, index)] + [pl.BlockSpec(memory_space=pl.ANY)] * len(whole),
        out_specs=spec,
        input_output_aliases={} if held is None else {1: 0},
        compiler_params=pltpu.CompilerParams(vmem_limit_bytes=60 * 1024 * 1024),
        cost_estimate=cost(4),
    )(source, *whole)


def store_gate_up(layout, source, shape, layer, held):
    width = shape[3] // (2 * layout.shards)
    per = layout.shards // layout.reps

    def kernel(x, o):
        for half in range(2):
            for b in range(per):
                for f in range(layout.reps):
                    start = ((half * per + b) * layout.reps + f) * width
                    at = (half * per + b) * width
                    o[0, 0, :, start : start + width] = x[0, f, :, at : at + width].astype(F32)

    block = (1,) + source.shape[1:]
    return store_layer(kernel, source, block, lambda e: (e, 0, 0, 0), shape, layer, held)


def store_down(source, shape, layer, held):
    def kernel(x, o):
        o[...] = x[...].astype(F32)

    block = (1, 1) + source.shape[2:]
    return store_layer(kernel, source, block, lambda e: (0, e, 0, 0), shape, layer, held)


def place_pairs(routes, priority, expert):
    flat = routes.reshape(-1)
    ahead = (flat[:, None] == flat[None, :]) & (priority[:, None] < priority[None, :])
    position = jnp.sum(ahead.astype(jnp.int32), axis=0)
    kept = (flat < EF) & (position < CAP)
    slot = jnp.where(kept, (flat ^ expert) * CAP + position, EF * CAP).reshape(-1, TOP).T
    places = jnp.arange(EF * CAP, dtype=jnp.int32)
    gather = (places[None, :, None] == slot[:, None, :]).astype(BF16)
    scatter = (places[None, None, :] == slot[:, :, None]).astype(BF16)
    return gather, scatter


def attention_forward(shared, dense, source, previous, routes, gather, d_result):
    gains, weights, mixing = dense
    tokens, features = source[1 if len(source) > 1 else 0].shape
    joined, last = len(source) > 1, d_result is not None
    low = ((tokens, features), BF16)
    full = ((tokens, features), F32)
    lanes = ((tokens, LANES), F32)
    found = call(
        functools.partial(attention_forward_kernel, joined, last),
        [full] * joined
        + [low, low, low, low, lanes, low, full, low, lanes, lanes]
        + [((gather.shape[1], features * (2 if last else 1)), BF16)],
        (*source, gains, weights, *shared, mixing, previous, routes, gather)
        + ((d_result,) if last else ()),
        [((tokens, tokens), F32)],
        len(source) + 1,
        12,
    )
    return found if joined else [source[0], *found]


def expert_both(rows, w_gate_up, w_down):
    count, double = rows.shape
    units = w_down.shape[0]
    return call(
        expert_both_kernel,
        [((count, 2 * units), BF16), ((count, units), BF16)]
        + [((EF * CAP, double), F32), ((count - EF * CAP, double), BF16)],
        (rows, w_gate_up, w_down),
        [((count, 2 * min(2 * LANES, units)), F32)],
        micros=12,
    )


def expert_forward(layout, inputs, w_gate_up, w_down):
    count, features = inputs.shape
    units = w_down.shape[0]
    return call(
        expert_forward_kernel,
        [((count, 2 * units), F32), ((count, units), BF16)]
        + [((EF * CAP, features), F32), ((count - EF * CAP, features), BF16)],
        (inputs, w_gate_up, w_down),
        micros=10,
    )


def expert_backward(layout, d_expert, w_gate_up, w_down, gate_up):
    count, features = d_expert.shape
    units = w_down.shape[0]
    return call(
        expert_backward_kernel,
        [((count, 2 * units), BF16)]
        + [((EF * CAP, features), F32), ((count - EF * CAP, features), BF16)],
        (d_expert, w_gate_up, w_down, gate_up),
        micros=10,
    )


def local(
    layout,
    hidden_in,
    gate_in,
    routes,
    priority,
    segments,
    norm_attn,
    w_qkv,
    w_out,
    norm_moe,
    w_router,
    w_const,
    const_vec,
    w_gate_up,
    w_down,
    grad_out,
):
    layers = w_qkv.shape[0]
    tokens, features = hidden_in.shape
    rep, j, expert = layout.place()
    slim = w_qkv.shape[1]
    small = [
        jnp.concatenate(
            [norm_attn[l][:, None], norm_moe[l][:, None], w_router[l], w_const[l], const_vec[l].T],
            axis=-1,
        ).reshape(1, -1)
        for l in range(layers)
    ]
    small = jnp.concatenate(small, axis=-1)
    extra = ROWS * features
    small = jnp.pad(small, ((0, 0), (0, extra - small.shape[1]))).reshape(ROWS, features)
    count = EF // layout.reps
    shard = lax.axis_index("shard")
    where = jnp.stack([rep, shard // EF, j // 2, j % 2]).astype(jnp.int32)

    group = rep.reshape(1).astype(jnp.int32)

    def share(l, *more):
        blocks = jnp.concatenate(
            [jnp.transpose(w_qkv[l].reshape(slim, 3, features), (1, 0, 2)), w_out[l][None]]
        )
        mine = lax.dynamic_slice_in_dim(blocks, rep * count, count, 0)
        return jnp.concatenate([mine.reshape(count * slim, features), *more])

    def dense_weights(x):
        full = layout.assemble(layout.dense_gather(x), where, count)
        return full[0].reshape(4, features, features), *full[1:]

    line = layout.dense_line(share(0, small))
    *found, last = expert_weights(layout, after(w_gate_up, line), w_down, 0, rep, j, group)
    moe = [found]
    full, small_full = dense_weights(after(line, last))
    small_full = small_full.reshape(layout.shards, -1)
    dense = [full]
    packs, vectors, mixing_t = [], [], []
    for l in range(layers):
        part = small_full[:, l * slim * SMALL : (l + 1) * slim * SMALL]
        part = part.reshape(features, SMALL)
        mixing = part[:, 2 : SMALL - NCONST]
        mixing = jnp.pad(mixing, ((0, 0), (0, LANES - mixing.shape[1])))
        packs.append([part[:, :2].T.astype(F32), None, mixing])
        mixing_t.append(mixing.T)
        vectors.append(part[:, SMALL - NCONST :].T.astype(F32))

    shared = (*rope_tables(tokens), segments.reshape(-1, 1), segments)
    pairs = [place_pairs(routes[l], priority[l, 0], expert) for l in range(layers)]

    source = (hidden_in,)
    previous = jnp.pad(gate_in, ((0, 0), (0, LANES - EXPERTS)))
    kept = []
    for l in range(layers):
        gather, scatter = pairs[l]
        packs[l][1] = dense[l]
        last = l + 1 == layers
        state = attention_forward(
            shared, packs[l], source, previous, routes[l], gather, grad_out if last else None
        )
        middle, logits, coefs, rows = state[7], state[9], state[10], state[11]
        inputs = layout.dispatch(rows)
        if last:
            d_gate_up, activated, own, others = expert_both(inputs, *moe[l])
            wide = dot(inputs[:, :features], d_gate_up, ((0,), (0,))).astype(BF16)
            down = dot(activated, inputs[:, features:], ((0,), (0,))).astype(BF16)
        else:
            dense.append(dense_weights(layout.dense_line(after(share(l + 1), rows)))[0])
            raw = after((w_gate_up, w_down), rows)
            moe.append(expert_weights(layout, *raw, l + 1, rep, j, group)[:2])
            gate_up, activated, own, others = expert_forward(layout, inputs, *moe[l])
        outputs = layout.collect(own, others)
        if last:
            outputs, wide, down = lax.optimization_barrier((outputs, wide, down))
        source = (coefs, middle, packs[l][0], scatter, outputs, vectors[l])
        previous = logits
        kept.append((state, inputs, gate_up, activated, outputs))
    (result,) = call(combine_kernel, [((tokens, features), F32)], source)

    grad_hidden = grad_out
    grad_gate = jnp.zeros_like(previous)
    join = lax.optimization_barrier

    def back_down(x):
        return layout.return_down(x.reshape(count, -1, features))

    def back_gate_up(x):
        return layout.return_gate_up(x.reshape(EF, -1, x.shape[-1]))

    def put_down(x, l, held):
        return store_down(x[None], (layers, EF) + w_down.shape[2:], l, held)

    def put_gate_up(x, l, held):
        x = x.reshape((EF, layout.reps) + x.shape[1:])
        return store_gate_up(layout, x, (layers, EF) + w_gate_up.shape[2:], l, held)

    boths, wides, downs = [None] * layers, [None] * layers, [None] * layers
    gate_up_out, down_out = None, None
    smalls = [None] * layers
    for l in reversed(range(layers)):
        gather, scatter = pairs[l]
        state, inputs, gate_up, activated, outputs = kept[l]
        hidden, normed, query, keys, values, log_total, attended, middle, low = state[:9]
        coefs = state[10]
        last = l + 1 == layers
        if not last:
            d_expert = layout.dispatch(rows)
        grad_gate, d_mixed, mix_grads = call(
            gate_backward_kernel,
            [((tokens, LANES), F32), ((tokens, features), F32), ((SMALL - 2, features), F32)],
            (coefs, middle, packs[l][0], scatter, outputs, vectors[l], routes[l], low)
            + (mixing_t[l], grad_hidden, grad_gate),
            micros=6,
        )
        if last:
            d_rows = outputs
            wides[l], downs[l] = layout.line_sum(wide), layout.line_sum(down)
        else:
            d_expert, d_mixed = join((d_expert, d_mixed))
            down = back_down(after(downs[l + 1], d_expert))
            d_gate_up, own, others = expert_backward(layout, d_expert, *moe[l], gate_up)
            own, down = join((own, down))
            down_out = put_down(down, l + 1, down_out)
            grad_gate_up = dot(inputs, d_gate_up, ((0,), (0,))).astype(BF16)
            d_rows = layout.collect(own, others)
            boths[l + 1] = layout.sum_core(
                dense_gradients(layout, *after(ready, own), count), j % 2
            )
            grad_down = dot(activated, d_expert, ((0,), (0,))).astype(BF16)
            d_rows, grad_gate_up, grad_down, boths[l + 1], down_out = join(
                (d_rows, grad_gate_up, grad_down, boths[l + 1], down_out)
            )
            wides[l], downs[l] = layout.line_sum(grad_gate_up), layout.line_sum(grad_down)
        more = () if l == 0 else (kept[l - 1][0][10], pairs[l - 1][0])
        grad_hidden, d_branch, d_projected, gain_grads, *rows = call(
            functools.partial(attention_backward_kernel, l > 0),
            [((tokens, features), F32), ((tokens, features), BF16)]
            + [((3, tokens, features), BF16), ((2, features), F32)]
            + [((gather.shape[1], features), BF16)] * (l > 0),
            (grad_hidden, d_mixed, d_rows, scatter, middle, hidden, packs[l][0], packs[l][1])
            + (*shared, query, keys, values, log_total, *more),
            [((tokens, tokens), F32), ((tokens, features), BF16), ((tokens, features), F32)],
            7,
            14,
        )
        rows = rows[0] if rows else None
        if not last:
            wide = back_gate_up(after(wides[l + 1], d_branch))
        small_grads = jnp.concatenate([gain_grads, mix_grads]).T.astype(BF16)
        smalls[l] = small_grads.reshape(layout.shards, slim * SMALL)
        ready = ((normed, attended, d_projected, d_branch), None)

    smalls = jnp.concatenate(smalls, axis=1)
    smalls = jnp.pad(smalls, ((0, 0), (0, ROWS * features - smalls.shape[1])))
    ready = (ready[0], smalls.reshape(layout.shards, ROWS, features))
    boths[0] = layout.sum_core(dense_gradients(layout, *ready, count), j % 2)
    both, wide = join((jnp.concatenate(boths, axis=3), wide))
    gate_up_out = put_gate_up(wide, 1, gate_up_out)
    cross, gate_up_out, down = join(
        (layout.sum_cross(both, rep, j), gate_up_out, back_down(after(downs[0], both)))
    )
    line = layout.sum_cross_end(*cross, rep, j)
    line, wides[0] = join((line, wides[0]))
    down_out = put_down(down, 0, down_out)
    line, wide, gate_up_out, down_out, result = join(
        (layout.sum_line(line), back_gate_up(wides[0]), gate_up_out, down_out, result)
    )
    gate_up_out = put_gate_up(wide, 0, gate_up_out)
    dense_all = layout.rep_gather(line, rep)
    small_all = dense_all[0, count * slim : count * slim + ROWS].reshape(-1)
    small_all = small_all[: layers * slim * SMALL].astype(F32).reshape(layers, slim, SMALL)
    starts = [0] + [l * count * slim + ROWS for l in range(1, layers)]
    dense_all = jnp.stack([dense_all[:, at : at + count * slim] for at in starts])
    dense_all = dense_all.astype(F32).reshape(layers, 4, slim, features)
    qkv_all = jnp.transpose(dense_all[:, :3], (0, 2, 1, 3)).reshape(layers, slim, 3 * features)
    return (
        result.astype(BF16),
        grad_hidden,
        grad_gate[:, :EXPERTS],
        small_all[:, :, 0],
        qkv_all,
        dense_all[:, 3],
        small_all[:, :, 1],
        small_all[:, :, 2 : 2 + EXPERTS],
        small_all[:, :, 2 + EXPERTS : SMALL - NCONST],
        jnp.transpose(small_all[:, :, SMALL - NCONST :], (0, 2, 1)),
        gate_up_out,
        down_out,
    )


def solution(mesh):
    return jax.shard_map(
        functools.partial(local, Layout(mesh)),
        mesh=mesh,
        in_specs=(
            P(("rep", "shard"), None),
            P(("rep", "shard"), None),
            P(None, ("rep", "shard"), None),
            P(None, ("rep", "shard"), None),
            P(("rep", "shard"), None),
            P(None, "shard"),
            P(None, "shard", None),
            P(None, "shard", None),
            P(None, "shard"),
            P(None, "shard", None),
            P(None, "shard", None),
            P(None, None, "shard"),
            P(None, None, "shard", None),
            P(None, None, "shard", None),
            P(("rep", "shard"), None),
        ),
        out_specs=(
            P(("rep", "shard"), None),
            P(("rep", "shard"), None),
            P(("rep", "shard"), None),
            P(None, "shard"),
            P(None, "shard", None),
            P(None, "shard", None),
            P(None, "shard"),
            P(None, "shard", None),
            P(None, "shard", None),
            P(None, None, "shard"),
            P(None, None, "shard", None),
            P(None, None, "shard", None),
        ),
        check_vma=False,
    )
```
